512 devices in a mesh: lon: 32 (over y, z_lo), lat: 16 (over x, z_hi, core).
Axes of the slice: x: 4, y: 8, z: 8 (z_hi: 2, z_lo: 4; z = z_hi * 4 + z_lo), core: 2. Of those that a mesh axis runs over, the one named last changes fastest.
Arguments:
- state: float32 [4, 40, 128, 4096], P(None, None, 'lat', 'lon'), may hold values from -6 to 6
- mixing: float32 [40, 128, 4096], P(None, 'lat', 'lon'), may hold values from 0.02 to 5
- wet_levels: int32 [128, 4096], P('lat', 'lon'), may hold values from 0 to 40, as said below
Outputs:
- new_state: float32 [4, 40, 128, 4096], P(None, None, 'lat', 'lon')
The draws below stay inside these ranges and needn't reach their ends.
Inputs may be any that keep to these rules, and one draw needn't show every extreme that they name: `wet_levels`: 0 marks a land column; whole tiles of 8 x 128 columns may be land, except in the top 8 rows of the grid, where every column has at least one wet level.
All inputs are finite; a program needn't handle non-finite values.
Results may differ from the reference program's by a relative error of at most 0.0003.
Values sent between devices are 32-bit elements; how exact they have to be, the bound alone decides.
No kernel may reach another device: no remote copies, remote signals or barrier semaphores. Data moves between devices by JAX's collectives and lax.ppermute only.
A program may use at most 128 MiB of HBM per device.

```python
import math
import jax
import jax.numpy as jnp
from jax import lax

LEV = 40
TY = 8
TX = 128
STEPS = 3
NY = 128
NX = 4096


def draw_wet_levels(key, part):
    key = jax.random.fold_in(key, 7)
    tile_key, coast_key, depth_key = jax.random.split(key, 3)
    tile_land = jax.random.randint(tile_key, (NY // TY, NX // TX), 0, 5) == 0
    coast_land = jax.random.randint(coast_key, (NY // 4, NX // 8), 0, 4) == 0
    depth_cells = jax.random.randint(depth_key, (NY, NX), 1, LEV + 1)
    land_cells = jnp.repeat(jnp.repeat(tile_land, TY, axis=0), TX, axis=1) | jnp.repeat(jnp.repeat(coast_land, 4, axis=0), 8, axis=1)
    row_index = jnp.arange(NY, dtype=jnp.int32)[:, None]
    land_cells = land_cells & (row_index < NY - TY)
    wet_count = jnp.where(land_cells, 0, depth_cells)
    wet_count = wet_count.at[0, 0].set(0).at[0, 1].set(LEV)
    return wet_count.astype(jnp.int32)


def block_scale(stream_key, extent, pieces, low, largest):
    def one(position, shards_of):
        steps = jax.random.uniform(jax.random.fold_in(jax.random.fold_in(stream_key, 6), position), (shards_of,), jnp.float32, low / len(pieces), largest / len(pieces))
        return jnp.repeat(jnp.exp(steps), extent[position] // shards_of).reshape((-1,) + (1,) * (len(extent) - position - 1))

    loudness = one(*pieces[0])
    for cut in pieces[1:]:
        loudness = loudness * one(*cut)
    return loudness


def scatter_about(rng, extent, spread, most, cuts=(), kind=jnp.bfloat16):
    gain = block_scale(rng, extent, cuts, -0.22, 0.18) if cuts else 1.0
    values = jax.random.normal(rng, extent, jnp.float32) * spread * gain
    return jnp.minimum(jnp.maximum(values, -most), most).astype(kind)


def setup_inputs(seed: int = 0) -> dict:
    seeds = jax.random.split(jax.random.key(seed), 4)
    return {
        "state": scatter_about(seeds[0], (4, LEV, NY, NX), 1.0, 6.0, ((2, 16), (3, 32)), jnp.float32),
        "mixing": jnp.clip(jnp.exp(math.log(5.0) - 5.521461 * jax.random.uniform(seeds[1], (LEV, NY, NX), jnp.float32) ** block_scale(seeds[1], (LEV, NY, NX), ((1, 16), (2, 32)), -0.2, 0.2)), 0.02, 5.0),
        "wet_levels": draw_wet_levels(jax.random.fold_in(seeds[3], 71), 0),
    }


ADVECT = 0.15
DIFFUSE = 0.12
VISCOSITY = 0.1
PRESSURE = 0.03
CORIOLIS = 0.3
EXPAND_HEAT = 0.6
EXPAND_SALT = 0.8
TAPER_SCALE = 1.0

def slab_cut(array, lower_end, upper_end, direction):
    return lax.slice_in_dim(array, lower_end, upper_end, axis=direction)

def minmod(first_diff, second_diff):
    smaller = jnp.where(jnp.abs(first_diff) < jnp.abs(second_diff), first_diff, second_diff)
    return jnp.where(first_diff * second_diff > 0.0, smaller, 0.0)

def vertical_grad(array):
    padded = jnp.pad(array, ((0, 0), (1, 1), (0, 0), (0, 0)))
    return 0.5 * (padded[:, 2:] - padded[:, :-2])

def advect_div(tracer, speed, wetness, direction, length):
    diffs = (slab_cut(tracer, 1, length + 4, direction) - slab_cut(tracer, 0, length + 3, direction)) * (slab_cut(wetness, 1, length + 4, direction) * slab_cut(wetness, 0, length + 3, direction))
    slopes = minmod(slab_cut(diffs, 1, length + 3, direction), slab_cut(diffs, 0, length + 2, direction))
    left_value = slab_cut(tracer, 1, length + 2, direction) + 0.5 * slab_cut(slopes, 0, length + 1, direction)
    right_value = slab_cut(tracer, 2, length + 3, direction) - 0.5 * slab_cut(slopes, 1, length + 2, direction)
    face_wet = slab_cut(wetness, 1, length + 2, direction) * slab_cut(wetness, 2, length + 3, direction)
    face_speed = 0.5 * (slab_cut(speed, 1, length + 2, direction) + slab_cut(speed, 2, length + 3, direction)) * face_wet
    fluxes = jnp.maximum(face_speed, 0.0) * left_value + jnp.minimum(face_speed, 0.0) * right_value
    return slab_cut(fluxes, 1, length + 1, direction) - slab_cut(fluxes, 0, length, direction)

def laplace_div(field, wetness, direction, length):
    face_wet = slab_cut(wetness, 0, length + 1, direction) * slab_cut(wetness, 1, length + 2, direction)
    fluxes = face_wet * (slab_cut(field, 1, length + 2, direction) - slab_cut(field, 0, length + 1, direction))
    return slab_cut(fluxes, 1, length + 1, direction) - slab_cut(fluxes, 0, length, direction)

def isopycnal_div(tracer, density, wetness, direction, length):
    grad_tracer = vertical_grad(tracer)
    grad_density = vertical_grad(density)
    face_wet = slab_cut(wetness, 0, length + 1, direction) * slab_cut(wetness, 1, length + 2, direction)
    tracer_step = slab_cut(tracer, 1, length + 2, direction) - slab_cut(tracer, 0, length + 1, direction)
    density_step = slab_cut(density, 1, length + 2, direction) - slab_cut(density, 0, length + 1, direction)
    face_rz = 0.5 * (slab_cut(grad_density, 0, length + 1, direction) + slab_cut(grad_density, 1, length + 2, direction))
    face_tz = 0.5 * (slab_cut(grad_tracer, 0, length + 1, direction) + slab_cut(grad_tracer, 1, length + 2, direction))
    slope = density_step * face_rz / (face_rz * face_rz + TAPER_SCALE)
    fluxes = face_wet * (tracer_step - slope * face_tz)
    return slab_cut(fluxes, 1, length + 1, direction) - slab_cut(fluxes, 0, length, direction)

def thomas(field, coupling):
    layers = field.shape[1]
    upper_terms = []
    solved = []
    for layer_index in range(layers):
        above_term = -coupling[:, layer_index]
        if layer_index == 0:
            pivot_value = 1.0 + coupling[:, 0]
            right_value = field[:, 0]
        else:
            below_term = -coupling[:, layer_index - 1]
            diagonal = 1.0 + coupling[:, layer_index] + coupling[:, layer_index - 1]
            pivot_value = diagonal - below_term * upper_terms[-1]
            right_value = field[:, layer_index] - below_term * solved[-1]
        upper_terms.append(above_term / pivot_value)
        solved.append(right_value / pivot_value)
    result = [solved[-1]]
    for layer_index in range(layers - 2, -1, -1):
        result.append(solved[layer_index] - upper_terms[layer_index] * result[-1])
    return jnp.stack(result[::-1], axis=1)

def density_of(fields):
    return EXPAND_SALT * fields[1:2] - EXPAND_HEAT * fields[0:1]

def advance(field, coupling, wetness, wet_east, wet_north, pad_fn, row_coord, total_rows):
    columns = field.shape[3]
    row_count = field.shape[2]
    east_west, north_south = pad_fn(field, 2, (1.0, 1.0, -1.0, -1.0))
    advected = advect_div(east_west[0:2], east_west[2:3], wet_east, 3, columns) + advect_div(north_south[0:2], north_south[3:4], wet_north, 2, row_count)
    tracers = (field[0:2] - ADVECT * advected) * wetness
    near_east = slab_cut(east_west, 1, columns + 3, 3)
    near_north = slab_cut(north_south, 1, row_count + 3, 2)
    wet_near_east = slab_cut(wet_east, 1, columns + 3, 3)
    wet_near_north = slab_cut(wet_north, 1, row_count + 3, 2)
    pressure_east = PRESSURE * jnp.cumsum(density_of(near_east), axis=1)
    pressure_north = PRESSURE * jnp.cumsum(density_of(near_north), axis=1)
    push_east = 0.5 * (slab_cut(pressure_east, 2, columns + 2, 3) - slab_cut(pressure_east, 0, columns, 3))
    push_north = 0.5 * (slab_cut(pressure_north, 2, row_count + 2, 2) - slab_cut(pressure_north, 0, row_count, 2))
    friction = laplace_div(near_east[2:4], wet_near_east, 3, columns) + laplace_div(near_north[2:4], wet_near_north, 2, row_count)
    rotation = CORIOLIS * jnp.sin(math.pi * (row_coord + 0.5) / total_rows - 0.9)
    eastward = (field[2:3] + rotation * field[3:4] - push_east + VISCOSITY * friction[0:1]) * wetness
    northward = (field[3:4] - rotation * field[2:3] - push_north + VISCOSITY * friction[1:2]) * wetness
    diff_east, diff_north = pad_fn(tracers, 1, (1.0, 1.0))
    lateral = isopycnal_div(diff_east, density_of(diff_east), wet_near_east, 3, columns) + isopycnal_div(diff_north, density_of(diff_north), wet_near_north, 2, row_count)
    tracers = (tracers + DIFFUSE * lateral) * wetness
    return thomas(jnp.concatenate([tracers, eastward, northward], axis=0), coupling)

def pad_global(field, halo_width, sign_list):
    total_rows = field.shape[2]
    east_west = jnp.concatenate([field[..., -halo_width:], field, field[..., :halo_width]], axis=3)
    sign_array = jnp.array(sign_list, dtype=jnp.float32).reshape(-1, 1, 1, 1)
    flipped = field[:, :, total_rows - 1 - halo_width:total_rows - 1, :][:, :, ::-1, ::-1]
    mirrored = jnp.roll(flipped, TX // 2, axis=3) * sign_array
    bottom = jnp.zeros(field.shape[:2] + (halo_width, field.shape[3]), jnp.float32)
    north_south = jnp.concatenate([bottom, field, mirrored], axis=2)
    return (east_west, north_south)

def reference(state, mixing, wet_levels):
    levels = jnp.arange(LEV, dtype=jnp.float32).reshape(1, LEV, 1, 1)
    depth = wet_levels.astype(jnp.float32)[None, None]
    wetness = (levels < depth).astype(jnp.float32)
    depth_east, depth_north = pad_global(depth, 2, (1.0,))
    wet_east = (levels < depth_east).astype(jnp.float32)
    wet_north = (levels < depth_north).astype(jnp.float32)
    below = jnp.concatenate([wetness[:, 1:], jnp.zeros_like(wetness[:, :1])], axis=1)
    coupling = mixing[None] * wetness * below
    row_coord = jnp.arange(NY, dtype=jnp.float32)[:, None]
    field = state * wetness
    for step_index in range(STEPS):
        field = advance(field, coupling, wetness, wet_east, wet_north, pad_global, row_coord, NY)
    return field
```

```python
import math

import jax
import jax.numpy as jnp
from jax import lax
from jax.sharding import PartitionSpec as P

STEPS = 3


ADVECT = 0.15
DIFFUSE = 0.12
VISCOSITY = 0.1
PRESSURE = 0.03
CORIOLIS = 0.3
EXPAND_HEAT = 0.6
EXPAND_SALT = 0.8
TAPER_SCALE = 1.0


def with_halo(cells, sides, width, closed):
    for axis, dim in sides:
        count = lax.axis_size(axis)
        ends = count if closed else count - 1
        head = lax.slice_in_dim(cells, 0, width, axis=dim)
        tail = lax.slice_in_dim(cells, cells.shape[dim] - width, cells.shape[dim], axis=dim)
        cells = jnp.concatenate(
            [
                lax.ppermute(tail, axis, [(i, (i + 1) % count) for i in range(ends)]),
                cells,
                lax.ppermute(head, axis, [((i + 1) % count, i) for i in range(ends)]),
            ],
            axis=dim,
        )
    return cells


def slab_cut(array, lower_end, upper_end, direction):
    return lax.slice_in_dim(array, lower_end, upper_end, axis=direction)


def minmod(first_diff, second_diff):
    smaller = jnp.where(jnp.abs(first_diff) < jnp.abs(second_diff), first_diff, second_diff)
    return jnp.where(first_diff * second_diff > 0.0, smaller, 0.0)


def vertical_grad(array):
    padded = jnp.pad(array, ((0, 0), (1, 1), (0, 0), (0, 0)))
    return 0.5 * (padded[:, 2:] - padded[:, :-2])


def advect_div(tracer, speed, wetness, direction, length):
    diffs = (
        slab_cut(tracer, 1, length + 4, direction) - slab_cut(tracer, 0, length + 3, direction)
    ) * (slab_cut(wetness, 1, length + 4, direction) * slab_cut(wetness, 0, length + 3, direction))
    slopes = minmod(
        slab_cut(diffs, 1, length + 3, direction), slab_cut(diffs, 0, length + 2, direction)
    )
    left_value = slab_cut(tracer, 1, length + 2, direction) + 0.5 * slab_cut(
        slopes, 0, length + 1, direction
    )
    right_value = slab_cut(tracer, 2, length + 3, direction) - 0.5 * slab_cut(
        slopes, 1, length + 2, direction
    )
    face_wet = slab_cut(wetness, 1, length + 2, direction) * slab_cut(
        wetness, 2, length + 3, direction
    )
    face_speed = (
        0.5
        * (slab_cut(speed, 1, length + 2, direction) + slab_cut(speed, 2, length + 3, direction))
        * face_wet
    )
    fluxes = jnp.maximum(face_speed, 0.0) * left_value + jnp.minimum(face_speed, 0.0) * right_value
    return slab_cut(fluxes, 1, length + 1, direction) - slab_cut(fluxes, 0, length, direction)


def laplace_div(field, wetness, direction, length):
    face_wet = slab_cut(wetness, 0, length + 1, direction) * slab_cut(
        wetness, 1, length + 2, direction
    )
    fluxes = face_wet * (
        slab_cut(field, 1, length + 2, direction) - slab_cut(field, 0, length + 1, direction)
    )
    return slab_cut(fluxes, 1, length + 1, direction) - slab_cut(fluxes, 0, length, direction)


def isopycnal_div(tracer, density, wetness, direction, length):
    grad_tracer = vertical_grad(tracer)
    grad_density = vertical_grad(density)
    face_wet = slab_cut(wetness, 0, length + 1, direction) * slab_cut(
        wetness, 1, length + 2, direction
    )
    tracer_step = slab_cut(tracer, 1, length + 2, direction) - slab_cut(
        tracer, 0, length + 1, direction
    )
    density_step = slab_cut(density, 1, length + 2, direction) - slab_cut(
        density, 0, length + 1, direction
    )
    face_rz = 0.5 * (
        slab_cut(grad_density, 0, length + 1, direction)
        + slab_cut(grad_density, 1, length + 2, direction)
    )
    face_tz = 0.5 * (
        slab_cut(grad_tracer, 0, length + 1, direction)
        + slab_cut(grad_tracer, 1, length + 2, direction)
    )
    slope = density_step * face_rz / (face_rz * face_rz + TAPER_SCALE)
    fluxes = face_wet * (tracer_step - slope * face_tz)
    return slab_cut(fluxes, 1, length + 1, direction) - slab_cut(fluxes, 0, length, direction)


def thomas(field, coupling):
    layers = field.shape[1]
    upper_terms = []
    solved = []
    for layer_index in range(layers):
        above_term = -coupling[:, layer_index]
        if layer_index == 0:
            pivot_value = 1.0 + coupling[:, 0]
            right_value = field[:, 0]
        else:
            below_term = -coupling[:, layer_index - 1]
            diagonal = 1.0 + coupling[:, layer_index] + coupling[:, layer_index - 1]
            pivot_value = diagonal - below_term * upper_terms[-1]
            right_value = field[:, layer_index] - below_term * solved[-1]
        upper_terms.append(above_term / pivot_value)
        solved.append(right_value / pivot_value)
    result = [solved[-1]]
    for layer_index in range(layers - 2, -1, -1):
        result.append(solved[layer_index] - upper_terms[layer_index] * result[-1])
    return jnp.stack(result[::-1], axis=1)


def density_of(fields):
    return EXPAND_SALT * fields[1:2] - EXPAND_HEAT * fields[0:1]


def advance(field, coupling, wetness, wet_east, wet_north, pad_fn, row_coord, total_rows):
    columns = field.shape[3]
    row_count = field.shape[2]
    east_west, north_south = pad_fn(field, 2, (1.0, 1.0, -1.0, -1.0))
    advected = advect_div(east_west[0:2], east_west[2:3], wet_east, 3, columns) + advect_div(
        north_south[0:2], north_south[3:4], wet_north, 2, row_count
    )
    tracers = (field[0:2] - ADVECT * advected) * wetness
    near_east = slab_cut(east_west, 1, columns + 3, 3)
    near_north = slab_cut(north_south, 1, row_count + 3, 2)
    wet_near_east = slab_cut(wet_east, 1, columns + 3, 3)
    wet_near_north = slab_cut(wet_north, 1, row_count + 3, 2)
    pressure_east = PRESSURE * jnp.cumsum(density_of(near_east), axis=1)
    pressure_north = PRESSURE * jnp.cumsum(density_of(near_north), axis=1)
    push_east = 0.5 * (
        slab_cut(pressure_east, 2, columns + 2, 3) - slab_cut(pressure_east, 0, columns, 3)
    )
    push_north = 0.5 * (
        slab_cut(pressure_north, 2, row_count + 2, 2) - slab_cut(pressure_north, 0, row_count, 2)
    )
    friction = laplace_div(near_east[2:4], wet_near_east, 3, columns) + laplace_div(
        near_north[2:4], wet_near_north, 2, row_count
    )
    rotation = CORIOLIS * jnp.sin(math.pi * (row_coord + 0.5) / total_rows - 0.9)
    eastward = (
        field[2:3] + rotation * field[3:4] - push_east + VISCOSITY * friction[0:1]
    ) * wetness
    northward = (
        field[3:4] - rotation * field[2:3] - push_north + VISCOSITY * friction[1:2]
    ) * wetness
    diff_east, diff_north = pad_fn(tracers, 1, (1.0, 1.0))
    lateral = isopycnal_div(
        diff_east, density_of(diff_east), wet_near_east, 3, columns
    ) + isopycnal_div(diff_north, density_of(diff_north), wet_near_north, 2, row_count)
    tracers = (tracers + DIFFUSE * lateral) * wetness
    return thomas(jnp.concatenate([tracers, eastward, northward], axis=0), coupling)


def pad_tile(field, halo_width, sign_list):
    row_count = field.shape[2]
    columns = field.shape[3]
    half_cols = columns // 2
    east_west = with_halo(field, (("lon", 3),), halo_width, True)
    north_south = with_halo(field, (("lat", 2),), halo_width, False)
    sign_array = jnp.array(sign_list, dtype=jnp.float32).reshape(-1, 1, 1, 1)
    outgoing = field[:, :, row_count - 1 - halo_width : row_count - 1, :][:, :, ::-1, :]
    turned = outgoing[..., ::-1]
    lons = lax.axis_size("lon")
    lats = lax.axis_size("lat")
    west_pairs = [(d * lats + lats - 1, ((lons - d) % lons) * lats + lats - 1) for d in range(lons)]
    east_pairs = [(d * lats + lats - 1, (lons - 1 - d) * lats + lats - 1) for d in range(lons)]
    mirrored = jnp.concatenate(
        [
            lax.ppermute(turned[..., half_cols:], ("lon", "lat"), west_pairs),
            lax.ppermute(turned[..., :half_cols], ("lon", "lat"), east_pairs),
        ],
        axis=3,
    )
    on_top = lax.axis_index("lat") == lax.axis_size("lat") - 1
    top_rows = jnp.where(
        on_top, mirrored * sign_array, north_south[:, :, row_count + halo_width :, :]
    )
    north_south = jnp.concatenate([north_south[:, :, : row_count + halo_width], top_rows], axis=2)
    return (east_west, north_south)


def local(state, mixing, wet_levels):
    layers = state.shape[1]
    row_count = state.shape[2]
    levels = jnp.arange(layers, dtype=jnp.float32).reshape(1, layers, 1, 1)
    depth = wet_levels.astype(jnp.float32)[None, None]
    wetness = (levels < depth).astype(jnp.float32)
    depth_east, depth_north = pad_tile(depth, 2, (1.0,))
    wet_east = (levels < depth_east).astype(jnp.float32)
    wet_north = (levels < depth_north).astype(jnp.float32)
    below = jnp.concatenate([wetness[:, 1:], jnp.zeros_like(wetness[:, :1])], axis=1)
    coupling = mixing[None] * wetness * below
    row_coord = (lax.axis_index("lat") * row_count + jnp.arange(row_count)).astype(jnp.float32)[
        :, None
    ]
    total_rows = row_count * lax.axis_size("lat")
    field = state * wetness
    for step_index in range(STEPS):
        field = advance(
            field, coupling, wetness, wet_east, wet_north, pad_tile, row_coord, total_rows
        )
    return field


def solution(mesh):
    return jax.shard_map(
        local,
        mesh=mesh,
        in_specs=(P(None, None, "lat", "lon"), P(None, "lat", "lon"), P("lat", "lon")),
        out_specs=P(None, None, "lat", "lon"),
        check_vma=False,
    )
```

```python
import functools
import math

import jax
import jax.numpy as jnp
from jax import lax
from jax.experimental import pallas as pl
from jax.experimental.pallas import tpu as pltpu
from jax.sharding import PartitionSpec as P

STEPS = 3
LEV = 40
ADVECT = 0.15
DIFFUSE = 0.12
VISCOSITY = 0.1
PRESSURE = 0.03
CORIOLIS = 0.3
EXPAND_HEAT = 0.6
EXPAND_SALT = 0.8

ITEMS = 5 * LEV + 1
TEMP, SALT, EAST, NORTH, COUP, WET = 0, LEV, 2 * LEV, 3 * LEV, 4 * LEV, 5 * LEV
HALF = (ITEMS + 1) // 2
MORE = 13
FAR = 88
STRIP = 9
PACKS = LEV // 2

FRAME_ROWS = list(range(-8, 8)) + [8, 9, 5, 6] + list(range(7, 17)) + [0, -9]

VM = pl.BlockSpec(memory_space=pltpu.VMEM)
SM = pl.BlockSpec(memory_space=pltpu.SMEM)


def call(body, outs, ins, flops, scratch=()):
    return pl.pallas_call(
        body,
        out_shape=tuple(jax.ShapeDtypeStruct(s, jnp.float32) for s in outs),
        in_specs=ins,
        out_specs=tuple(VM for _ in outs),
        scratch_shapes=list(scratch),
        compiler_params=pltpu.CompilerParams(vmem_limit_bytes=48 * 1024 * 1024),
        cost_estimate=pl.CostEstimate(flops=flops, bytes_accessed=4 * 1024 * 1024, transcendentals=0),
    )


def rows_of(shape=(8, 128)):
    return lax.broadcasted_iota(jnp.int32, shape, 0)


def lanes_of(shape=(8, 128)):
    return lax.broadcasted_iota(jnp.int32, shape, 1)


def loop(count, body, init=None, unroll=1):
    if init is None:
        lax.fori_loop(0, count, lambda i, c: (body(i), c)[1], 0, unroll=unroll)
        return None
    return lax.fori_loop(0, count, body, init, unroll=unroll)


def row_at(ref, tile, row):
    return jnp.broadcast_to(ref[tile, row : row + 1, :], (8, 128))


def turn(tile):
    turned = jnp.take_along_axis(tile, 127 - lanes_of(), axis=1)
    return jnp.take_along_axis(turned, 7 - rows_of(), axis=0)


def split_halves(full_ref, a_ref, b_ref, count):
    lanes = lanes_of()

    def one(k):
        near = pltpu.roll(full_ref[k], 64, axis=1)
        far = full_ref[k + count]
        a_ref[k] = jnp.where(lanes < 64, near, far)
        b_ref[k] = jnp.where(lanes < 64, far, near)

    loop(count, one, unroll=8)


def join_halves(full_ref, a_ref, b_ref, count):
    lanes = lanes_of()

    def one(k):
        a, b = a_ref[k], b_ref[k]
        full_ref[k] = jnp.where(lanes < 64, a, b)
        full_ref[k + count] = pltpu.roll(jnp.where(lanes < 64, b, a), 64, axis=1)

    loop(count, one, unroll=8)


def gather_body(flag_ref, state_ref, mixing_ref, wet_ref, x_ref, a_ref, b_ref, full_ref):
    wet = wet_ref[...].astype(jnp.float32)
    x_ref[WET] = wet

    def level(l):
        deep = wet > l.astype(jnp.float32)
        for k in range(4):
            x_ref[k * LEV + l] = jnp.where(deep, state_ref[k, l], 0.0)
        x_ref[COUP + l] = jnp.where(wet > (l + 1).astype(jnp.float32), mixing_ref[l], 0.0)

    loop(LEV, level, unroll=4)

    @pl.when(flag_ref[1] == 0)
    def _():
        def move(i):
            a_ref[i] = x_ref[i]

        def move_rest(i):
            b_ref[i] = x_ref[HALF + i]

        loop(HALF, move, unroll=8)
        loop(ITEMS - HALF, move_rest, unroll=8)
        b_ref[HALF - 1] = jnp.zeros((8, 128), jnp.float32)

    @pl.when(flag_ref[1] == 1)
    def _():
        def tracer(i):
            full_ref[i] = turn(x_ref[i])

        def current(i):
            full_ref[EAST + i] = -turn(x_ref[EAST + i])

        def couple(i):
            full_ref[COUP + i] = turn(x_ref[COUP + i])

        loop(2 * LEV, tracer, unroll=8)
        loop(2 * LEV, current, unroll=8)
        loop(LEV, couple, unroll=8)
        full_ref[WET] = turn(x_ref[WET])
        full_ref[2 * HALF - 1] = jnp.zeros((8, 128), jnp.float32)
        split_halves(full_ref, a_ref, b_ref, HALF)


def take_rows(ref, base, row):
    rows = rows_of()
    out = row_at(ref, base, row)
    for r in range(1, 8):
        out = jnp.where(rows == r, row_at(ref, base + r, row), out)
    return out


def outgoing_body(flag_ref, y_ref, c_ref, d_ref, full_ref):
    parity = flag_ref[0]
    fold = flag_ref[1]
    rows = rows_of()
    zero = jnp.zeros((8, 128), jnp.float32)

    def same(t):
        return t

    def mirror(t):
        return jnp.take_along_axis(t, 127 - lanes_of(), axis=1)

    def extra(out_ref, base, item, tiles, row, change):
        def eight(t):
            out_ref[base + t] = change(take_rows(y_ref, item + t * 8, row))

        loop(tiles, eight, unroll=5)

    def plain(row):
        extra(c_ref, 0, TEMP, 10, row, same)
        c_ref[10] = row_at(y_ref, WET, row)
        c_ref[11] = zero
        c_ref[12] = zero
        loop(MORE, lambda t: d_ref.__setitem__(t, zero))

    @pl.when((fold == 0) & (parity == 0))
    def _():
        plain(0)

    @pl.when((fold == 0) & (parity == 1))
    def _():
        plain(7)

    @pl.when(fold == 1)
    def _():
        extra(full_ref, 0, TEMP, 10, 6, mirror)
        extra(full_ref, 10, TEMP, 10, 7, mirror)
        extra(full_ref, 20, NORTH, 5, 7, lambda t: -mirror(t))
        wet = jnp.where(rows == 0, row_at(y_ref, WET, 6), row_at(y_ref, WET, 7))
        full_ref[25] = mirror(wet)
        split_halves(full_ref, c_ref, d_ref, MORE)


def frame_body(
    flag_ref, x_ref, y_ref, a_ref, b_ref, c_ref, d_ref, frame_ref, far_ref, east_ref, west_ref, full_ref, more_ref
):
    parity = flag_ref[0]
    fold = flag_ref[1]
    rows = rows_of()
    lanes = lanes_of()

    @pl.when(fold == 0)
    def _():
        def move(k):
            full_ref[k] = a_ref[k]
            full_ref[k + HALF] = b_ref[k]

        def move_more(k):
            more_ref[k] = c_ref[k]

        loop(HALF, move, unroll=8)
        loop(11, move_more, unroll=11)

    @pl.when(fold == 1)
    def _():
        join_halves(full_ref, a_ref, b_ref, HALF)
        join_halves(more_ref, c_ref, d_ref, MORE)

    def send_far(row):
        def eight(t):
            far_ref[pl.ds(pl.multiple_of(t * 8, 8), 8), :] = take_rows(full_ref, t * 8, row)

        loop(2 * LEV // 8, eight, unroll=5)
        far_ref[pl.ds(80, 8), :] = row_at(full_ref, WET, row)

    @pl.when(parity == 0)
    def _():
        send_far(7)

    @pl.when((parity == 1) & (fold == 0))
    def _():
        send_far(0)

    @pl.when(fold == 1)
    def _():
        send_far(1)

    def put(i, south, own, north):
        shifted = pltpu.roll(north, 5, axis=0)
        middle = jnp.where(rows < 2, north, jnp.where(rows < 5, pltpu.roll(own, 5, axis=0), shifted))
        frame_ref[i, 0:8] = south
        frame_ref[i, 8:16] = own
        frame_ref[i, 16:24] = middle
        frame_ref[i, 24:32] = jnp.where(rows < 5, shifted, 0.0)

    @pl.when(parity == 0)
    def _():
        def one(i):
            put(i, full_ref[i], x_ref[i], y_ref[i])

        loop(ITEMS, one, unroll=8)

    @pl.when((parity == 1) & (fold == 0))
    def _():
        def one(i):
            put(i, y_ref[i], x_ref[i], full_ref[i])

        loop(ITEMS, one, unroll=8)

    @pl.when(fold == 1)
    def _():
        def base(i):
            beyond = full_ref[i]
            own = x_ref[i]
            shifted = pltpu.roll(beyond, 4, axis=0)
            middle = jnp.where(
                rows < 2, pltpu.roll(beyond, 7, axis=0), jnp.where(rows < 4, pltpu.roll(own, 5, axis=0), shifted)
            )
            frame_ref[i, 0:8] = y_ref[i]
            frame_ref[i, 8:16] = own
            frame_ref[i, 16:24] = middle
            return jnp.where(rows < 4, shifted, 0.0)

        def with_near(first, tiles, more):
            def eight(t):
                for r in range(8):
                    i = first + t * 8 + r
                    frame_ref[i, 24:32] = jnp.where(rows == 4, row_at(more_ref, more + t, r), base(i))

            loop(tiles, eight)

        def eastward(i):
            frame_ref[EAST + i, 24:32] = base(EAST + i)

        def couple(i):
            frame_ref[COUP + i, 24:32] = jnp.where(rows < 3, base(COUP + i), 0.0)

        with_near(TEMP, 10, 10)
        loop(LEV, eastward, unroll=8)
        with_near(NORTH, 5, 20)
        loop(LEV, couple, unroll=8)
        frame_ref[WET, 24:32] = jnp.where(rows == 4, row_at(more_ref, 25, 1), base(WET))

    place = jnp.where(parity == 0, 7, 5)

    def far_rows(t):
        for r in range(8):
            i = t * 8 + r
            frame_ref[i, 24:32] = jnp.where(rows == place, row_at(more_ref, t, r), frame_ref[i, 24:32])

    loop(2 * LEV // 8, far_rows)
    wet_row = jnp.where(fold == 1, row_at(more_ref, 25, 0), row_at(more_ref, 10, 0))
    frame_ref[WET, 24:32] = jnp.where(rows == place, wet_row, frame_ref[WET, 24:32])

    wide = lanes_of((32, 128))

    def add_strip(out, tile, g, shift):
        here = (wide >= STRIP * g) & (wide < STRIP * (g + 1))
        return jnp.where(here, pltpu.roll(tile, (STRIP * g + shift) % 128, axis=1), out)

    def pack(k):
        to_east = to_west = jnp.zeros((32, 128), jnp.float32)
        for g in range(10):
            tile = frame_ref[(g % 5) * LEV + 2 * k + g // 5]
            to_east = add_strip(to_east, tile, g, STRIP)
            to_west = add_strip(to_west, tile, g, 0)
        east_ref[k] = to_east
        west_ref[k] = to_west

    loop(PACKS, pack)
    east_ref[0] = add_strip(east_ref[0], frame_ref[WET], 10, STRIP)
    west_ref[0] = add_strip(west_ref[0], frame_ref[WET], 10, 0)


def east_of(a):
    return pltpu.roll(a, 127, axis=1)


def west_of(a):
    return pltpu.roll(a, 1, axis=1)


def north_of(a):
    return pltpu.roll(a, a.shape[0] - 1, axis=0)


def south_of(a):
    return pltpu.roll(a, 1, axis=0)


def minmod(a, b):
    return jnp.maximum(jnp.minimum(a, b), 0.0) + jnp.minimum(jnp.maximum(a, b), 0.0)


def join_tracer(a):
    rows = rows_of()
    middle = a[16:24]
    middle = jnp.where(rows == 0, pltpu.roll(middle, 3, axis=0), middle)
    middle = jnp.where(rows == 3, pltpu.roll(a[8:16], 5, axis=0), middle)
    return jnp.concatenate([a[0:16], middle, a[24:32]], axis=0)


def join_field(a):
    rows = rows_of()
    middle = a[16:24]
    middle = jnp.where(rows < 2, pltpu.roll(middle, 3, axis=0), middle)
    middle = jnp.where((rows == 2) | (rows == 3), pltpu.roll(a[8:16], 5, axis=0), middle)
    return jnp.concatenate([a[0:16], middle, a[24:32]], axis=0)


def march(wet, turn_rate, f_ref, coup_ref, inv_ref, up_ref, adv_ref, sum_ref, dif_ref):
    wet_e = jnp.minimum(wet, east_of(wet))
    wet_n = jnp.minimum(wet, north_of(wet))
    zero = jnp.zeros((32, 128), jnp.float32)
    for k in range(4):
        sum_ref[k, 0] = zero
        sum_ref[k, LEV + 1] = zero

    def pivots(l, carry):
        above, inv_above = carry
        c = coup_ref[l]
        pivot = 1.0 + c + above * (1.0 - above * inv_above)
        inv = 1.0 / pivot
        inv_ref[l] = inv
        up_ref[l] = c * inv
        return c, inv

    loop(LEV, pivots, (zero, zero), unroll=4)

    def advect(q, face_e, face_n, speed_e, speed_n, from_w, from_s):
        de = jnp.where(face_e, east_of(q) - q, 0.0)
        dn = jnp.where(face_n, north_of(q) - q, 0.0)
        he = 0.5 * minmod(de, west_of(de))
        hn = 0.5 * minmod(dn, south_of(dn))
        fe = speed_e * jnp.where(from_w, q + he, east_of(q - he))
        fn = speed_n * jnp.where(from_s, q + hn, north_of(q - hn))
        return (fe - west_of(fe)) + (fn - south_of(fn))

    def friction(q, q_e, q_n, face_e, face_n):
        de = jnp.where(face_e, q_e - q, 0.0)
        dn = jnp.where(face_n, q_n - q, 0.0)
        return (de - west_of(de)) + (dn - south_of(dn))

    def explicit(l, pressure):
        lf = l.astype(jnp.float32)
        deep = wet > lf
        face_e = wet_e > lf
        face_n = wet_n > lf
        t, s, u, v = (f_ref[k, l] for k in range(4))
        u_e, v_n = east_of(u), north_of(v)
        speed_e = jnp.where(face_e, u + u_e, 0.0)
        speed_n = jnp.where(face_n, v + v_n, 0.0)
        from_w = speed_e > 0.0
        from_s = speed_n > 0.0
        for k, q in enumerate((t, s)):
            div = advect(q, face_e, face_n, speed_e, speed_n, from_w, from_s)
            a = join_tracer(jnp.where(deep, q - (0.5 * ADVECT) * div, 0.0))
            adv_ref[k, l] = a
            a_e, a_n = east_of(a), north_of(a)
            sum_ref[k, l + 1] = a + a_e
            dif_ref[k, l] = a_e - a
            sum_ref[2 + k, l + 1] = a + a_n
            dif_ref[2 + k, l] = a_n - a
        pressure = pressure + (EXPAND_SALT * s - EXPAND_HEAT * t)
        push_e = east_of(pressure) - west_of(pressure)
        push_n = north_of(pressure) - south_of(pressure)
        u1 = u + turn_rate * v - (0.5 * PRESSURE) * push_e + VISCOSITY * friction(u, u_e, north_of(u), face_e, face_n)
        v1 = v - turn_rate * u - (0.5 * PRESSURE) * push_n + VISCOSITY * friction(v, east_of(v), v_n, face_e, face_n)
        f_ref[2, l] = jnp.where(deep, u1, 0.0)
        f_ref[3, l] = jnp.where(deep, v1, 0.0)
        return pressure

    def lateral(l, carry):
        above, solved = carry
        lf = l.astype(jnp.float32)
        deep = wet > lf
        div = [None, None]
        for way, face, back in ((0, wet_e > lf, west_of), (2, wet_n > lf, south_of)):
            dt, ds = dif_ref[way, l], dif_ref[way + 1, l]
            gt = sum_ref[way, l + 2] - sum_ref[way, l]
            gs = sum_ref[way + 1, l + 2] - sum_ref[way + 1, l]
            gr = EXPAND_SALT * gs - EXPAND_HEAT * gt
            dr = EXPAND_SALT * ds - EXPAND_HEAT * dt
            slope = dr * gr / (gr * gr + 16.0)
            for k, (d, g) in enumerate(((dt, gt), (ds, gs))):
                flux = jnp.where(face, d - slope * g, 0.0)
                part = flux - back(flux)
                div[k] = part if div[k] is None else div[k] + part
        inv = inv_ref[l]
        done = []
        for k in range(4):
            rhs = jnp.where(deep, adv_ref[k, l] + DIFFUSE * div[k], 0.0) if k < 2 else f_ref[k, l]
            x = (rhs + above * solved[k]) * inv
            f_ref[k, l] = x
            done.append(x)
        return coup_ref[l], tuple(done)

    def back(i, solved):
        l = LEV - 1 - i
        up = up_ref[l]
        done = []
        for k in range(4):
            x = f_ref[k, l] + up * solved[k]
            f_ref[k, l] = join_field(x)
            done.append(x)
        return tuple(done)

    def step(_, carry):
        loop(LEV, explicit, zero, unroll=4)
        loop(LEV, lateral, (zero, (zero,) * 4), unroll=4)
        loop(LEV, back, (zero,) * 4, unroll=4)
        return carry

    lax.fori_loop(0, STEPS, step, 0)


WORK = [
    pltpu.VMEM((4, LEV, 32, 128), jnp.float32),
    pltpu.VMEM((LEV, 32, 128), jnp.float32),
    pltpu.VMEM((LEV, 32, 128), jnp.float32),
    pltpu.VMEM((LEV, 32, 128), jnp.float32),
    pltpu.VMEM((2, LEV, 32, 128), jnp.float32),
    pltpu.VMEM((4, LEV + 2, 32, 128), jnp.float32),
    pltpu.VMEM((4, LEV, 32, 128), jnp.float32),
]


def with_far(tile, i, far_ref, place):
    row = jnp.broadcast_to(far_ref[pl.ds(i, 1), :], (8, 128))
    return jnp.concatenate([tile[0:24], jnp.where(rows_of() == place, row, tile[24:32])], axis=0)


def main_body(flag_ref, frame_ref, far_ref, turn_ref, out_ref, f_ref, coup_ref, *work):
    place = jnp.where(flag_ref[0] == 0, 5, 7)

    def level(l):
        for k in range(2):
            f_ref[k, l] = with_far(frame_ref[k * LEV + l], k * LEV + l, far_ref, place)
        for k in range(2, 4):
            f_ref[k, l] = frame_ref[k * LEV + l]
        coup_ref[l] = frame_ref[COUP + l]

    loop(LEV, level, unroll=4)
    wet = with_far(frame_ref[WET], 80, far_ref, place)
    march(wet, turn_ref[...], f_ref, coup_ref, *work)

    def give(l):
        for k in range(4):
            out_ref[k, l] = f_ref[k, l, 8:16]

    loop(LEV, give, unroll=4)


def side_body(flag_ref, frame_ref, far_ref, turn_ref, east_ref, west_ref, main_ref, out_ref, f_ref, coup_ref, *work):
    place = jnp.where(flag_ref[0] == 0, 5, 7)
    wide = lanes_of((32, 128))

    def sides(tile, k, g):
        west = pltpu.roll(east_ref[k], (32 - STRIP - STRIP * g) % 128, axis=1)
        east = pltpu.roll(west_ref[k], (96 - STRIP * g) % 128, axis=1)
        out = jnp.where(wide < 64, pltpu.roll(tile, 32, axis=1), pltpu.roll(tile, 96, axis=1))
        out = jnp.where((wide >= 32 - STRIP) & (wide < 32), west, out)
        return jnp.where((wide >= 96) & (wide < 96 + STRIP), east, out)

    def unpack(k):
        for g in range(10):
            item, l = g % 5, 2 * k + g // 5
            tile = frame_ref[item * LEV + l]
            if item < 2:
                tile = with_far(tile, item * LEV + l, far_ref, place)
            tile = sides(tile, k, g)
            if item < 4:
                f_ref[item, l] = tile
            else:
                coup_ref[l] = tile

    loop(PACKS, unpack)
    wet = sides(with_far(frame_ref[WET], 80, far_ref, place), 0, 10)
    march(wet, turn_ref[...], f_ref, coup_ref, *work)
    lanes = lanes_of()

    def give(l):
        for k in range(4):
            side = f_ref[k, l, 8:16]
            out = main_ref[k, l]
            out = jnp.where(lanes < STRIP, pltpu.roll(side, 96, axis=1), out)
            out_ref[k, l] = jnp.where(lanes >= 128 - STRIP, pltpu.roll(side, 32, axis=1), out)

    loop(LEV, give, unroll=4)


def local(state, mixing, wet_levels):
    lons, lats = lax.axis_size("lon"), lax.axis_size("lat")
    lat = lax.axis_index("lat")
    flags = jnp.stack([lax.rem(lat, 2), (lat == lats - 1).astype(jnp.int32)]).astype(jnp.int32)
    grid_rows = lat * 8 + jnp.array(FRAME_ROWS, jnp.int32)
    grid_rows = jnp.where(grid_rows > lats * 8 - 1, 2 * (lats * 8 - 1) - grid_rows, grid_rows).astype(jnp.float32)
    rate = CORIOLIS * jnp.sin(math.pi * (grid_rows + 0.5) / (lats * 8) - 0.9)
    rate = jnp.broadcast_to(rate[:, None], (32, 128))

    def at(o, a):
        return o * lats + a

    pairs = [(at(o, a), at(o, a ^ 1)) for o in range(lons) for a in range(lats)]
    cross = [(at(o, a), at(o, a + 1 if a % 2 else a - 1)) for o in range(lons) for a in range(1, lats - 1)]
    fold_a = [(at(o, lats - 1), at((lons - o) % lons, lats - 1)) for o in range(lons)]
    fold_b = [(at(o, lats - 1), at(lons - 1 - o, lats - 1)) for o in range(lons)]
    both = ("lon", "lat")

    half = (HALF, 8, 128)
    more = (MORE, 8, 128)
    full = pltpu.VMEM((2 * HALF, 8, 128), jnp.float32)
    full_more = pltpu.VMEM((2 * MORE, 8, 128), jnp.float32)
    x, a, b = call(gather_body, [(ITEMS, 8, 128), half, half], [SM] + [VM] * 3, 10**6, [full])(
        flags, state, mixing, wet_levels
    )
    a = lax.ppermute(a, both, cross + fold_a)
    b = lax.ppermute(b, both, cross + fold_b)
    y = lax.ppermute(x, both, pairs)
    c, d = call(outgoing_body, [more, more], [SM, VM], 10**6, [full_more])(flags, y)
    c = lax.ppermute(c, both, cross + fold_a)
    d = lax.ppermute(d, both, fold_b)
    packed = (PACKS, 32, 128)
    frame, far, to_east, to_west = call(
        frame_body, [(ITEMS, 32, 128), (FAR, 128), packed, packed], [SM] + [VM] * 6, 10**6, [full, full_more]
    )(flags, x, y, a, b, c, d)
    far = lax.ppermute(far, both, pairs)
    from_west = lax.ppermute(to_east, "lon", [(i, (i + 1) % lons) for i in range(lons)])
    from_east = lax.ppermute(to_west, "lon", [((i + 1) % lons, i) for i in range(lons)])
    (middle,) = call(main_body, [state.shape], [SM] + [VM] * 3, 10**9, WORK)(flags, frame, far, rate)
    (out,) = call(side_body, [state.shape], [SM] + [VM] * 6, 10**9, WORK)(
        flags, frame, far, rate, from_west, from_east, middle
    )
    return out


def solution(mesh):
    return jax.shard_map(
        local,
        mesh=mesh,
        in_specs=(P(None, None, "lat", "lon"), P(None, "lat", "lon"), P("lat", "lon")),
        out_specs=P(None, None, "lat", "lon"),
        check_vma=False,
    )
```

```python
import math

import jax
import jax.numpy as jnp
from jax import lax
from jax.experimental import pallas as pl
from jax.experimental.pallas import tpu as pltpu
from jax.sharding import PartitionSpec as P

STEPS = 3
LEV = 40
GROUPS = LEV // 8
ADVECT = 0.15
DIFFUSE = 0.12
VISCOSITY = 0.1
PRESSURE = 0.03
CORIOLIS = 0.3
EXPAND_HEAT = 0.6
EXPAND_SALT = 0.8

TEMP, SALT, EAST, NORTH, COUP = range(5)

ROWS = 27
FRAME_ROWS = list(range(-9, 8)) + list(range(7, 17))
WET_AT = 5 * ROWS * LEV
FRAME = WET_AT + 32

OWN_WET = 40 * LEV
OWN = OWN_WET + 8
SLOT = {TEMP: 0, SALT: 8, NORTH: 16, EAST: 24, COUP: 31}
COUNT = {TEMP: 8, SALT: 8, NORTH: 8, EAST: 7, COUP: 6}
BULK_WET = 37 * LEV
HALF = (BULK_WET + 8) // 2
MORE = 144
MORE_WET = 7 * LEV
FAR = 2 * LEV + 8
STRIP = 9
WIDE = 14

STRIPS = (
    [(k, i) for k in (TEMP, SALT, NORTH) for i in range(1, 26)]
    + [(EAST, i) for i in range(2, 25)]
    + [(COUP, i) for i in range(3, 24)]
)
PACKS = -(-len(STRIPS) // WIDE)
STRIP_WET = PACKS * LEV

SPANS = (
    ((-7, 7), (7, 14), (-6, 7), (7, 13)),
    ((-4, 7), (7, 11), (-3, 7), (7, 10)),
    ((-1, 7), (8, 8), (0, 7), None),
)
PRESSURE_TILES = ((2, 10, 18), (5, 13, 14), (8, 11))
COLUMN_TILES = ((3, 11, 19), (6, 14), (9,))

VM = pl.BlockSpec(memory_space=pltpu.VMEM)
SM = pl.BlockSpec(memory_space=pltpu.SMEM)
LIMIT = 32 * 1024 * 1024
UNROLL = {"column": 4}


def call(body, outs, ins, flops, scratch=()):
    return pl.pallas_call(
        body,
        out_shape=tuple(jax.ShapeDtypeStruct(s, jnp.float32) for s in outs),
        in_specs=ins,
        out_specs=tuple(VM for _ in outs),
        scratch_shapes=[pltpu.VMEM(s, jnp.float32) for s in scratch],
        compiler_params=pltpu.CompilerParams(vmem_limit_bytes=LIMIT),
        cost_estimate=pl.CostEstimate(flops=flops, bytes_accessed=4 * 1024 * 1024, transcendentals=0),
    )


def rows_of(shape=(8, 128)):
    return lax.broadcasted_iota(jnp.int32, shape, 0)


def lanes_of(shape=(8, 128)):
    return lax.broadcasted_iota(jnp.int32, shape, 1)


def mirror(tile):
    return jnp.take_along_axis(tile, 127 - lanes_of(), axis=1)


def spread(ref, row):
    return jnp.broadcast_to(ref[row : row + 1, :], (8, 128))


def copy_block(out, to, source, at, change=lambda t: t):
    for g in range(GROUPS):
        out[to + 8 * g : to + 8 * g + 8, :] = change(source[at + 8 * g : at + 8 * g + 8, :])


def copy_blocks(out, to, source, at, count):
    if count:
        out[to : to + count * LEV, :] = source[at : at + count * LEV, :]


def split_halves(full_ref, a_ref, b_ref, rows):
    lanes = lanes_of()

    def one(k, c):
        at = pl.ds(pl.multiple_of(k * 8, 8), 8)
        near = pltpu.roll(full_ref[at, :], 64, axis=1)
        far = full_ref[pl.ds(pl.multiple_of(k * 8 + rows, 8), 8), :]
        a_ref[at, :] = jnp.where(lanes < 64, near, far)
        b_ref[at, :] = jnp.where(lanes < 64, far, near)
        return c

    lax.fori_loop(0, rows // 8, one, 0, unroll=8)


def join_halves(full_ref, a_ref, b_ref, rows):
    lanes = lanes_of()

    def one(k, c):
        at = pl.ds(pl.multiple_of(k * 8, 8), 8)
        a, b = a_ref[at, :], b_ref[at, :]
        full_ref[at, :] = jnp.where(lanes < 64, a, b)
        joined = pltpu.roll(jnp.where(lanes < 64, b, a), 64, axis=1)
        full_ref[pl.ds(pl.multiple_of(k * 8 + rows, 8), 8), :] = joined
        return c

    lax.fori_loop(0, rows // 8, one, 0, unroll=8)


def own_body(flag_ref, state_ref, mixing_ref, wet_ref, x_ref, a_ref, b_ref, full_ref):
    levels = rows_of().astype(jnp.float32)
    wet_ref_f = wet_ref[...].astype(jnp.float32)
    x_ref[OWN_WET:OWN, :] = wet_ref_f
    for r in range(8):
        wet = spread(x_ref, OWN_WET + r)
        for g in range(GROUPS):
            deep = wet > levels + float(8 * g)
            for k in range(4):
                tile = state_ref[pl.ds(k * 8 * LEV + g * 64 + r, 8, stride=8), :]
                at = (k * 8 + r) * LEV + 8 * g
                x_ref[at : at + 8, :] = jnp.where(deep, tile, 0.0)
            at = (COUP * 8 + r) * LEV + 8 * g
            tile = mixing_ref[pl.ds(g * 64 + r, 8, stride=8), :]
            x_ref[at : at + 8, :] = jnp.where(wet > levels + float(8 * g + 1), tile, 0.0)

    def ship(first_u, first_c):
        for k in SLOT:
            first = {EAST: first_u, COUP: first_c}.get(k, 0)
            copy_blocks(full_ref, SLOT[k] * LEV, x_ref, (k * 8 + first) * LEV, COUNT[k])
        full_ref[BULK_WET : BULK_WET + 8, :] = x_ref[OWN_WET:OWN, :]
        a_ref[...] = full_ref[0:HALF, :]
        b_ref[...] = full_ref[HALF : 2 * HALF, :]

    even = flag_ref[0] == 0
    fold = flag_ref[1] == 1

    @pl.when(even)
    def _():
        ship(0, 0)

    @pl.when(jnp.logical_not(even | fold))
    def _():
        ship(1, 2)

    @pl.when(fold)
    def _():
        for k in SLOT:
            sign = (lambda t: -mirror(t)) if k in (EAST, NORTH) else mirror
            for j in range(COUNT[k]):
                copy_block(full_ref, (SLOT[k] + j) * LEV, x_ref, (k * 8 + 7 - j) * LEV, sign)
        wet = jnp.zeros((8, 128), jnp.float32)
        for j in range(8):
            wet = jnp.where(rows_of() == j, spread(x_ref, OWN_WET + 7 - j), wet)
        full_ref[BULK_WET : BULK_WET + 8, :] = mirror(wet)
        split_halves(full_ref, a_ref, b_ref, HALF)


def outgoing_body(flag_ref, x_ref, y_ref, c_ref, d_ref, full_ref):
    even = flag_ref[0] == 0
    fold = flag_ref[1] == 1

    def plain(row):
        for k in (TEMP, SALT):
            copy_blocks(c_ref, k * LEV, y_ref, (k * 8 + row) * LEV, 1)
        c_ref[2 * LEV : 2 * LEV + 8, :] = spread(y_ref, OWN_WET + row)
        c_ref[2 * LEV + 8 : MORE, :] = jnp.zeros((MORE - 2 * LEV - 8, 128), jnp.float32)
        d_ref[...] = jnp.zeros((MORE, 128), jnp.float32)

    @pl.when(even)
    def _():
        plain(0)

    @pl.when(jnp.logical_not(even | fold))
    def _():
        plain(7)

    @pl.when(fold)
    def _():
        minus = lambda t: -mirror(t)
        for n, (source, k, row, change) in enumerate(
            (
                (y_ref, TEMP, 7, mirror),
                (y_ref, SALT, 7, mirror),
                (y_ref, NORTH, 7, minus),
                (y_ref, TEMP, 6, mirror),
                (y_ref, SALT, 6, mirror),
                (x_ref, EAST, 0, minus),
                (x_ref, COUP, 1, mirror),
            )
        ):
            copy_block(full_ref, n * LEV, source, (k * 8 + row) * LEV, change)
        wet = jnp.where(rows_of() == 0, spread(y_ref, OWN_WET + 7), spread(y_ref, OWN_WET + 6))
        full_ref[MORE_WET : MORE_WET + 8, :] = mirror(wet)
        split_halves(full_ref, c_ref, d_ref, MORE)


def frame_body(flag_ref, x_ref, y_ref, a_ref, b_ref, c_ref, d_ref, frame_ref, far_ref, east_ref, west_ref, full_ref, more_ref):
    even = flag_ref[0] == 0
    fold = flag_ref[1] == 1
    plain_odd = jnp.logical_not(even | fold)

    def at(k, place):
        return (k * ROWS + place) * LEV

    def bulk(k, place, slot, count):
        copy_blocks(frame_ref, at(k, place), full_ref, (SLOT[k] + slot) * LEV, count)

    def wet_rows(place, source, first, count):
        frame_ref[WET_AT + place : WET_AT + place + count, :] = source[first : first + count, :]

    def send_far(slot, wet_row):
        for k in (TEMP, SALT):
            copy_blocks(far_ref, k * LEV, full_ref, (SLOT[k] + slot) * LEV, 1)
        far_ref[2 * LEV : FAR, :] = spread(full_ref, BULK_WET + wet_row)

    frame_ref[WET_AT : WET_AT + 32, :] = jnp.zeros((32, 128), jnp.float32)

    @pl.when(jnp.logical_not(fold))
    def _():
        full_ref[0:HALF, :] = a_ref[...]
        full_ref[HALF : 2 * HALF, :] = b_ref[...]
        for k in range(5):
            copy_blocks(frame_ref, at(k, 17), x_ref, (k * 8 + 7) * LEV, 1)
        wet_rows(17, x_ref, OWN_WET + 7, 1)

    for k in range(5):
        copy_blocks(frame_ref, at(k, 9), x_ref, k * 8 * LEV, 8)
    wet_rows(9, x_ref, OWN_WET, 8)

    @pl.when(even)
    def _():
        for k in range(5):
            bulk(k, 9 - COUNT[k], 0, COUNT[k])
            copy_blocks(frame_ref, at(k, 18), y_ref, k * 8 * LEV, 8)
        wet_rows(1, full_ref, BULK_WET, 8)
        wet_rows(18, y_ref, OWN_WET, 8)
        for k in (TEMP, SALT):
            copy_blocks(frame_ref, at(k, 0), c_ref, k * LEV, 1)
            copy_blocks(frame_ref, at(k, 26), c_ref, k * LEV, 1)
        wet_rows(0, c_ref, 2 * LEV, 1)
        send_far(7, 7)

    @pl.when(jnp.logical_not(even))
    def _():
        for k in range(5):
            copy_blocks(frame_ref, at(k, 1), y_ref, k * 8 * LEV, 8)
        wet_rows(1, y_ref, OWN_WET, 8)

    @pl.when(plain_odd)
    def _():
        for k in range(5):
            bulk(k, 18, 0, COUNT[k])
        wet_rows(18, full_ref, BULK_WET, 8)
        for k in (TEMP, SALT):
            copy_blocks(frame_ref, at(k, 0), c_ref, k * LEV, 1)
            copy_blocks(frame_ref, at(k, 26), c_ref, k * LEV, 1)
        wet_rows(26, c_ref, 2 * LEV, 1)
        send_far(0, 0)

    @pl.when(fold)
    def _():
        join_halves(full_ref, a_ref, b_ref, HALF)
        join_halves(more_ref, c_ref, d_ref, MORE)
        for k in range(5):
            bulk(k, 17, 0, COUNT[k])
        wet_rows(17, full_ref, BULK_WET, 8)
        for n, (k, place) in enumerate(
            ((TEMP, 25), (SALT, 25), (NORTH, 25), (TEMP, 26), (SALT, 26), (EAST, 24), (COUP, 23))
        ):
            copy_blocks(frame_ref, at(k, place), more_ref, n * LEV, 1)
        wet_rows(25, more_ref, MORE_WET, 2)
        for k in (TEMP, SALT):
            copy_blocks(frame_ref, at(k, 0), more_ref, 3 * LEV + k * LEV, 1)
        send_far(1, 1)

    lanes = lanes_of()

    def add_strip(out, tile, n, shift):
        here = (lanes >= STRIP * n) & (lanes < STRIP * (n + 1))
        return jnp.where(here, pltpu.roll(tile, (STRIP * n + shift) % 128, axis=1), out)

    zero = jnp.zeros((8, 128), jnp.float32)

    def pack(g, c):
        first = pl.multiple_of(g * 8, 8)
        for p in range(PACKS):
            to_east = to_west = zero
            for n, (k, place) in enumerate(STRIPS[p * WIDE : (p + 1) * WIDE]):
                tile = frame_ref[pl.ds(first + at(k, place), 8), :]
                to_east = add_strip(to_east, tile, n, STRIP)
                to_west = add_strip(to_west, tile, n, 0)
            east_ref[pl.ds(first + p * LEV, 8), :] = to_east
            west_ref[pl.ds(first + p * LEV, 8), :] = to_west
        return c

    lax.fori_loop(0, GROUPS, pack, 0)
    for t in range(0, 32, 8):
        tile = frame_ref[WET_AT + t : WET_AT + t + 8, :]
        east_ref[STRIP_WET + t : STRIP_WET + t + 8, :] = add_strip(zero, tile, 0, STRIP)
        west_ref[STRIP_WET + t : STRIP_WET + t + 8, :] = add_strip(zero, tile, 0, 0)


def east_of(a):
    return pltpu.roll(a, 127, axis=1)


def west_of(a):
    return pltpu.roll(a, 1, axis=1)


def minmod(a, b):
    return jnp.maximum(jnp.minimum(a, b), 0.0) + jnp.minimum(jnp.maximum(a, b), 0.0)


def place_of(row, north):
    if north:
        return row + 10 if row >= 7 else row + 9
    return row + 9 if row <= 7 else row + 10


WINDOW = 5


def in_turn(jobs):
    waiting, active = list(jobs), []
    while waiting or active:
        if waiting and len(active) < WINDOW:
            active.append(waiting.pop(0))
        for job in list(active):
            if next(job, "end") == "end":
                active.remove(job)


ADV = LEV + 16


def march(first_step, coup, wet_ref, rate_ref, emit, f_ref, rhs_ref, adv_ref, p_ref, coef_ref, wet_e_ref):
    levels = rows_of().astype(jnp.float32)
    zero = jnp.zeros((8, 128), jnp.float32)
    wet_e_ref[...] = jnp.minimum(wet_ref[...], pltpu.roll(wet_ref[...], 127, axis=1))
    for k in range(2):
        for place in range(ROWS):
            at = (k * ROWS + place) * ADV
            adv_ref[at : at + 8, :] = zero
            adv_ref[at + 8 + LEV : at + ADV, :] = zero

    def eight(ref, k, place, level):
        return ref[pl.ds((k * ROWS + place) * LEV + level, 8, stride=LEV), :]

    def put_eight(ref, k, place, level, value):
        ref[pl.ds((k * ROWS + place) * LEV + level, 8, stride=LEV), :] = value

    def pivots(l, carry):
        done = []
        for tile, (above, up_above) in zip(COLUMN_TILES[0], carry):
            c = coup(tile, l)
            inv = 1.0 / (1.0 + c + above * (1.0 - up_above))
            up = c * inv
            put_eight(coef_ref, 0, tile, l, inv)
            put_eight(coef_ref, 1, tile, l, above * inv)
            put_eight(coef_ref, 2, tile, l, up)
            done.append((c, up))
        return tuple(done)

    lax.fori_loop(0, LEV, pivots, ((zero, zero),) * 3, unroll=4)

    def explicit(step, g):
        south_a, north_a, south_f, north_f = SPANS[step]
        first = g * 8 if isinstance(g, int) else pl.multiple_of(g * 8, 8)
        depth = levels + (float(8 * g) if isinstance(g, int) else (g * 8).astype(jnp.float32))
        cache = {}

        def once(key, make):
            if key not in cache:
                cache[key] = make()
            return cache[key]

        def field(k, place):
            def load():
                if step == 0:
                    return first_step(k, place, first)
                return f_ref[pl.ds(first + (k * ROWS + place) * LEV, 8), :]

            return once((k, place), load)

        def pressure(place):
            return once(("p", place), lambda: p_ref[pl.ds(first + place * LEV, 8), :])

        def deep(place):
            return once(("m", place), lambda: spread(wet_ref, place) > depth)

        def face_e(place):
            return once(("e", place), lambda: spread(wet_e_ref, place) > depth)

        def to_east(k, place):
            return once(("r", k, place), lambda: east_of(field(k, place)))

        jobs = []

        def piece(north, span_a, span_f):

            def here(row):
                return place_of(row, north)

            def face_n(row):
                return once(("n", north, row), lambda: deep(here(row)) & deep(here(row + 1)))

            def diff_n(k, row):
                def make():
                    return jnp.where(face_n(row), field(k, here(row + 1)) - field(k, here(row)), 0.0)

                return once(("d", north, k, row), make)

            def half_n(k, row):
                return once(("h", north, k, row), lambda: 0.5 * minmod(diff_n(k, row - 1), diff_n(k, row)))

            def speed_n(row):
                def make():
                    u = jnp.where(face_n(row), field(NORTH, here(row)) + field(NORTH, here(row + 1)), 0.0)
                    return u, u > 0.0

                return once(("s", north, row), make)

            def flux_n(k, row):
                def make():
                    speed, upward = speed_n(row)
                    below = field(k, here(row)) + half_n(k, row)
                    above = field(k, here(row + 1)) - half_n(k, row + 1)
                    return speed * jnp.where(upward, below, above)

                return once(("f", north, k, row), make)

            def work(row):
                place = here(row)
                mask_e = face_e(place)
                tracers = (TEMP, SALT)
                new_fields = span_f is not None and span_f[0] <= row <= span_f[1]
                for k in (TEMP, SALT, EAST):
                    to_east(k, place)
                if new_fields:
                    to_east(NORTH, place)
                    p_e, p_w = east_of(pressure(place)), west_of(pressure(place))
                yield
                diffs = [jnp.where(mask_e, to_east(k, place) - field(k, place), 0.0) for k in range(4 if new_fields else 2)]
                diffs_w = [west_of(d) for d in diffs]
                yield
                halves = [0.5 * minmod(diffs_w[k], diffs[k]) for k in tracers]
                beyond = [east_of(field(k, place) - halves[k]) for k in tracers]
                yield
                speed_e = jnp.where(mask_e, field(EAST, place) + to_east(EAST, place), 0.0)
                fluxes = [
                    speed_e * jnp.where(speed_e > 0.0, field(k, place) + halves[k], beyond[k]) for k in tracers
                ]
                fluxes_w = [west_of(f) for f in fluxes]
                yield
                for k in tracers:
                    div = (fluxes[k] - fluxes_w[k]) + (flux_n(k, row) - flux_n(k, row - 1))
                    out = jnp.where(deep(place), field(k, place) - (0.5 * ADVECT) * div, 0.0)
                    adv_ref[pl.ds(first + (k * ROWS + place) * ADV + 8, 8), :] = out
                if new_fields:
                    u, v = field(EAST, place), field(NORTH, place)
                    rate = spread(rate_ref, place)
                    push_n = pressure(here(row + 1)) - pressure(here(row - 1))
                    for k, other, push in ((EAST, rate * v, p_e - p_w), (NORTH, -(rate * u), push_n)):
                        lap = (diffs[k] - diffs_w[k]) + (diff_n(k, row) - diff_n(k, row - 1))
                        out = field(k, place) + other - (0.5 * PRESSURE) * push + VISCOSITY * lap
                        rhs_ref[pl.ds(first + (k * ROWS + place) * LEV, 8), :] = jnp.where(deep(place), out, 0.0)

            return [work(row) for row in range(span_a[0], span_a[1] + 1)]

        jobs += piece(False, south_a, south_f)
        jobs += piece(True, north_a, north_f)

        in_turn(jobs)

    def lateral(step, g):
        _, _, south_f, north_f = SPANS[step]
        first = g * 8 if isinstance(g, int) else pl.multiple_of(g * 8, 8)
        depth = levels + (float(8 * g) if isinstance(g, int) else (g * 8).astype(jnp.float32))
        cache = {}

        def once(key, make):
            if key not in cache:
                cache[key] = make()
            return cache[key]

        def tracer(k, place, shift=0):
            at = first + (k * ROWS + place) * ADV + 8 + shift
            return once((k, place, shift), lambda: adv_ref[pl.ds(at, 8), :])

        def grad(k, place):
            return once(("g", k, place), lambda: tracer(k, place, 1) - tracer(k, place, -1))

        def deep(place):
            return once(("m", place), lambda: spread(wet_ref, place) > depth)

        def fluxes(mask, dt, ds, gt, gs):
            gr = EXPAND_SALT * gs - EXPAND_HEAT * gt
            dr = EXPAND_SALT * ds - EXPAND_HEAT * dt
            slope = dr * gr / (gr * gr + 16.0)
            return jnp.where(mask, dt - slope * gt, 0.0), jnp.where(mask, ds - slope * gs, 0.0)

        def piece(north, span_f):
            def here(row):
                return place_of(row, north)

            def flux_n(row):
                def make():
                    a, b = here(row), here(row + 1)
                    return fluxes(
                        deep(a) & deep(b),
                        tracer(TEMP, b) - tracer(TEMP, a),
                        tracer(SALT, b) - tracer(SALT, a),
                        grad(TEMP, a) + grad(TEMP, b),
                        grad(SALT, a) + grad(SALT, b),
                    )

                return once(("f", north, row), make)

            def work(row):
                place = here(row)
                cells = [(tracer(k, place), grad(k, place)) for k in (TEMP, SALT)]
                beyond = [(east_of(q), east_of(g)) for q, g in cells]
                yield
                flux_n(row)
                yield
                (t, gt), (s, gs) = cells
                (t_e, gt_e), (s_e, gs_e) = beyond
                east = fluxes(spread(wet_e_ref, place) > depth, t_e - t, s_e - s, gt + gt_e, gs + gs_e)
                west = [west_of(f) for f in east]
                yield
                for k in (TEMP, SALT):
                    div = (east[k] - west[k]) + (flux_n(row)[k] - flux_n(row - 1)[k])
                    out = jnp.where(deep(place), cells[k][0] + DIFFUSE * div, 0.0)
                    rhs_ref[pl.ds(first + (k * ROWS + place) * LEV, 8), :] = out

            return [work(row) for row in range(span_f[0], span_f[1] + 1)]

        in_turn(piece(False, south_f) + (piece(True, north_f) if north_f else []))

    for step in range(STEPS):

        def weigh(l, carry):
            done = []
            for tile, p in zip(PRESSURE_TILES[step], carry):
                if step == 0:
                    t, s = (first_step(k, tile, l, LEV) for k in (TEMP, SALT))
                else:
                    t, s = eight(f_ref, TEMP, tile, l), eight(f_ref, SALT, tile, l)
                p = p + (EXPAND_SALT * s - EXPAND_HEAT * t)
                put_eight(p_ref, 0, tile, l, p)
                done.append(p)
            return tuple(done)

        lax.fori_loop(0, LEV, weigh, (zero,) * len(PRESSURE_TILES[step]), unroll=UNROLL["column"])

        def explicit_group(g, c):
            explicit(step, g)
            return c

        def lateral_group(g, c):
            lateral(step, g)
            return c

        lax.fori_loop(0, GROUPS, explicit_group, 0)
        lax.fori_loop(0, GROUPS, lateral_group, 0)
        tiles = COLUMN_TILES[step]

        def down(l, carry):
            done = []
            for tile, above in zip(tiles, carry):
                inv, low = eight(coef_ref, 0, tile, l), eight(coef_ref, 1, tile, l)
                solved = []
                for k in range(4):
                    x = eight(rhs_ref, k, tile, l) * inv + low * above[k]
                    put_eight(rhs_ref, k, tile, l, x)
                    solved.append(x)
                done.append(tuple(solved))
            return tuple(done)

        def up(i, carry):
            l = LEV - 1 - i
            done = []
            for tile, below in zip(tiles, carry):
                factor = eight(coef_ref, 2, tile, l)
                solved = []
                for k in range(4):
                    x = eight(rhs_ref, k, tile, l) + factor * below[k]
                    if step < STEPS - 1:
                        put_eight(f_ref, k, tile, l, x)
                    else:
                        emit(k, l, x)
                    solved.append(x)
                done.append(tuple(solved))
            return tuple(done)

        start = ((zero,) * 4,) * len(tiles)
        lax.fori_loop(0, LEV, down, start, unroll=UNROLL["column"])
        lax.fori_loop(0, LEV, up, start, unroll=UNROLL["column"])


WORK = [
    (4 * ROWS * LEV, 128),
    (4 * ROWS * LEV, 128),
    (2 * ROWS * ADV, 128),
    (ROWS * LEV, 128),
    (3 * ROWS * LEV, 128),
    (32, 128),
]


def far_place(even, place):
    return even if place == 26 else jnp.logical_not(even)


def load_wet(even, frame_ref, far_ref, wet_ref):
    wet_ref[...] = frame_ref[WET_AT : WET_AT + 32, :]
    for place in (0, 26):
        old = frame_ref[WET_AT + place : WET_AT + place + 1, :]
        wet_ref[place : place + 1, :] = jnp.where(far_place(even, place), far_ref[2 * LEV : 2 * LEV + 1, :], old)


def main_body(flag_ref, frame_ref, far_ref, rate_ref, out_ref, wet_ref, *work):
    even = flag_ref[0] == 0
    load_wet(even, frame_ref, far_ref, wet_ref)

    def first_step(k, place, row, stride=None):
        at = (k * ROWS + place) * LEV + row
        if stride is not None:
            return frame_ref[pl.ds(at, 8, stride=stride), :]
        tile = frame_ref[pl.ds(at, 8), :]
        if place in (0, 26):
            tile = jnp.where(far_place(even, place), far_ref[pl.ds(row + k * LEV, 8), :], tile)
        return tile

    def coup(place, l):
        return frame_ref[pl.ds((COUP * ROWS + place) * LEV + l, 8, stride=LEV), :]

    def emit(k, l, x):
        out_ref[k, l] = x

    march(first_step, coup, wet_ref, rate_ref, emit, *work)


def side_body(flag_ref, frame_ref, far_ref, rate_ref, east_ref, west_ref, main_ref, out_ref, wet_ref, side_ref, *work):
    even = flag_ref[0] == 0
    load_wet(even, frame_ref, far_ref, wet_ref)
    lanes = lanes_of()

    def edges(tile):
        return jnp.where(lanes < 64, pltpu.roll(tile, 32, axis=1), pltpu.roll(tile, 96, axis=1))

    def with_strips(tile, west, east, n):
        out = edges(tile)
        west = pltpu.roll(west, (32 - STRIP - STRIP * n) % 128, axis=1)
        east = pltpu.roll(east, (96 - STRIP * n) % 128, axis=1)
        out = jnp.where((lanes >= 32 - STRIP) & (lanes < 32), west, out)
        return jnp.where((lanes >= 96) & (lanes < 96 + STRIP), east, out)

    for t in range(0, 32, 8):
        at = STRIP_WET + t
        wet_ref[t : t + 8, :] = with_strips(wet_ref[t : t + 8, :], east_ref[at : at + 8, :], west_ref[at : at + 8, :], 0)

    def unpack(g, c):
        first = pl.multiple_of(g * 8, 8)
        for n, (k, place) in enumerate(STRIPS):
            at = pl.ds(first + (k * ROWS + place) * LEV, 8)
            p = pl.ds(first + n // WIDE * LEV, 8)
            side_ref[at, :] = with_strips(frame_ref[at, :], east_ref[p, :], west_ref[p, :], n % WIDE)
        for k in (TEMP, SALT):
            for place in (0, 26):
                at = pl.ds(first + (k * ROWS + place) * LEV, 8)
                far = far_ref[pl.ds(first + k * LEV, 8), :]
                side_ref[at, :] = edges(jnp.where(far_place(even, place), far, frame_ref[at, :]))
        return c

    lax.fori_loop(0, GROUPS, unpack, 0)

    def first_step(k, place, row, stride=None):
        at = (k * ROWS + place) * LEV + row
        if stride is not None:
            return side_ref[pl.ds(at, 8, stride=stride), :]
        return side_ref[pl.ds(at, 8), :]

    def coup(place, l):
        return side_ref[pl.ds((COUP * ROWS + place) * LEV + l, 8, stride=LEV), :]

    def emit(k, l, x):
        out = jnp.where(lanes < STRIP, pltpu.roll(x, 96, axis=1), main_ref[k, l])
        out_ref[k, l] = jnp.where(lanes >= 128 - STRIP, pltpu.roll(x, 32, axis=1), out)

    march(first_step, coup, wet_ref, rate_ref, emit, *work)


def local(state, mixing, wet_levels):
    lons, lats = lax.axis_size("lon"), lax.axis_size("lat")
    lat = lax.axis_index("lat")
    flags = jnp.stack([lax.rem(lat, 2), (lat == lats - 1).astype(jnp.int32)]).astype(jnp.int32)
    grid_rows = lat * 8 + jnp.array(FRAME_ROWS + [0] * (32 - ROWS), jnp.int32)
    grid_rows = jnp.where(grid_rows > lats * 8 - 1, 2 * (lats * 8 - 1) - grid_rows, grid_rows).astype(jnp.float32)
    rate = CORIOLIS * jnp.sin(math.pi * (grid_rows + 0.5) / (lats * 8) - 0.9)
    rate = jnp.broadcast_to(rate[:, None], (32, 128))

    def at(o, a):
        return o * lats + a

    pairs = [(at(o, a), at(o, a ^ 1)) for o in range(lons) for a in range(lats)]
    cross = [(at(o, a), at(o, a + 1 if a % 2 else a - 1)) for o in range(lons) for a in range(1, lats - 1)]
    fold_a = [(at(o, lats - 1), at((lons - o) % lons, lats - 1)) for o in range(lons)]
    fold_b = [(at(o, lats - 1), at(lons - 1 - o, lats - 1)) for o in range(lons)]
    both = ("lon", "lat")

    half = (HALF, 128)
    more = (MORE, 128)
    x, a, b = call(own_body, [(OWN, 128), half, half], [SM] + [VM] * 3, 10**6, [(2 * HALF, 128)])(
        flags, state.reshape(4 * LEV * 8, 128), mixing.reshape(LEV * 8, 128), wet_levels
    )
    a = lax.ppermute(a, both, cross + fold_a)
    b = lax.ppermute(b, both, cross + fold_b)
    y = lax.ppermute(x, both, pairs)
    c, d = call(outgoing_body, [more, more], [SM, VM, VM], 10**6, [(2 * MORE, 128)])(flags, x, y)
    c = lax.ppermute(c, both, cross + fold_a)
    d = lax.ppermute(d, both, fold_b)
    packed = (STRIP_WET + 32, 128)
    frame, far, to_east, to_west = call(
        frame_body,
        [(FRAME, 128), (FAR, 128), packed, packed],
        [SM] + [VM] * 6,
        10**6,
        [(2 * HALF, 128), (2 * MORE, 128)],
    )(flags, x, y, a, b, c, d)
    far = lax.ppermute(far, both, pairs)
    from_west = lax.ppermute(to_east, "lon", [(i, (i + 1) % lons) for i in range(lons)])
    from_east = lax.ppermute(to_west, "lon", [((i + 1) % lons, i) for i in range(lons)])
    wet = (32, 128)
    (middle,) = call(main_body, [state.shape], [SM] + [VM] * 3, 10**9, [wet] + WORK)(flags, frame, far, rate)
    (out,) = call(side_body, [state.shape], [SM] + [VM] * 6, 10**9, [wet, (WET_AT, 128)] + WORK)(
        flags, frame, far, rate, from_west, from_east, middle
    )
    return out


def solution(mesh):
    return jax.shard_map(
        local,
        mesh=mesh,
        in_specs=(P(None, None, "lat", "lon"), P(None, "lat", "lon"), P("lat", "lon")),
        out_specs=P(None, None, "lat", "lon"),
        check_vma=False,
    )
```

```python
import math

import jax
import jax.numpy as jnp
from jax import lax
from jax.experimental import pallas as pl
from jax.experimental.pallas import tpu as pltpu
from jax.sharding import PartitionSpec as P

STEPS = 3
LEV = 40
GROUPS = LEV // 8
ADVECT = 0.15
DIFFUSE = 0.12
VISCOSITY = 0.1
PRESSURE = 0.03
CORIOLIS = 0.3
EXPAND_HEAT = 0.6
EXPAND_SALT = 0.8

TEMP, SALT, EAST, NORTH, COUP = range(5)

ROWS = 27
PLACE_NEAR = {16: 0, 15: 1, 14: 2, 13: 6} | {r: 14 + r for r in range(13)}
PLACE_FAR = {-9: 3, -8: 4, -7: 5} | {-r: 13 - r for r in range(7)}
PLACE_ROW = {p: r for r, p in (PLACE_NEAR | PLACE_FAR).items()} | {14: 0, 13: 0}
WET_AT = 5 * ROWS * LEV
FRAME = WET_AT + 32

OWN_WET = 40 * LEV
OWN = OWN_WET + 8
SLOT = {TEMP: 0, SALT: 8, NORTH: 16, EAST: 24, COUP: 31}
COUNT = {TEMP: 8, SALT: 8, NORTH: 8, EAST: 7, COUP: 6}
BULK_WET = 37 * LEV
HALF = (BULK_WET + 8) // 2
MORE = 144
MORE_WET = 7 * LEV
FAR = 2 * LEV + 8
STRIP = 9
WIDE = 14


class Strips:
    def __init__(self, items):
        self.items = items
        self.packs = -(-len(items) // WIDE)
        self.wet = self.packs * LEV
        self.shape = (self.wet + 32, 128)


EARLY = Strips([(k, PLACE_NEAR[r]) for k in range(4) for r in range(16)] + [(COUP, PLACE_NEAR[r]) for r in range(14)])
LATE = Strips(
    [(k, PLACE_FAR[-r]) for k in (TEMP, SALT, NORTH) for r in range(9)]
    + [(EAST, PLACE_FAR[-r]) for r in range(8)]
    + [(COUP, PLACE_FAR[-r]) for r in range(7)]
)

PARTS = {
    "early": (
        (range(2, 14), (), range(3, 13), (), (6, 16, 19), (17, 19)),
        (range(5, 11), (), range(6, 10), (), (19,), (19,)),
    ),
    "late": (
        ((0, 1, 14), range(0, -8, -1), (0, 1, 2, 13), range(0, -7, -1), (2, 10, 19), (6, 14)),
        ((0, 1, 2, 3, 4, 11), range(0, -5, -1), (0, 1, 2, 3, 4, 5, 10), range(0, -4, -1), (9, 17, 19), (10, 18)),
        (range(0, 9), (-1,), range(0, 8), (), (12, 15), (14,)),
    ),
}
PIVOT_TILES = {"early": (17, 19), "late": (6, 14, 19)}
HANDED = ((range(3, 13), (2, 3, 12, 13)), (range(6, 10), (5, 6, 9, 10)))

VM = pl.BlockSpec(memory_space=pltpu.VMEM)
SM = pl.BlockSpec(memory_space=pltpu.SMEM)
LIMIT = 32 * 1024 * 1024
UNROLL = {"column": 4}


def call(body, outs, ins, flops, scratch=()):
    return pl.pallas_call(
        body,
        out_shape=tuple(jax.ShapeDtypeStruct(s, jnp.float32) for s in outs),
        in_specs=ins,
        out_specs=tuple(VM for _ in outs),
        scratch_shapes=[pltpu.VMEM(s, jnp.float32) for s in scratch],
        compiler_params=pltpu.CompilerParams(vmem_limit_bytes=LIMIT),
        cost_estimate=pl.CostEstimate(flops=flops, bytes_accessed=4 * 1024 * 1024, transcendentals=0),
    )


def rows_of(shape=(8, 128)):
    return lax.broadcasted_iota(jnp.int32, shape, 0)


def lanes_of(shape=(8, 128)):
    return lax.broadcasted_iota(jnp.int32, shape, 1)


def mirror(tile):
    return jnp.take_along_axis(tile, 127 - lanes_of(), axis=1)


def spread(ref, row):
    return jnp.broadcast_to(ref[row : row + 1, :], (8, 128))


def copy_block(out, to, source, at, change=lambda t: t):
    for g in range(GROUPS):
        out[to + 8 * g : to + 8 * g + 8, :] = change(source[at + 8 * g : at + 8 * g + 8, :])


def copy_blocks(out, to, source, at, count):
    if count:
        out[to : to + count * LEV, :] = source[at : at + count * LEV, :]


def split_halves(full_ref, a_ref, b_ref, rows):
    lanes = lanes_of()

    def one(k, c):
        at = pl.ds(pl.multiple_of(k * 8, 8), 8)
        near = pltpu.roll(full_ref[at, :], 64, axis=1)
        far = full_ref[pl.ds(pl.multiple_of(k * 8 + rows, 8), 8), :]
        a_ref[at, :] = jnp.where(lanes < 64, near, far)
        b_ref[at, :] = jnp.where(lanes < 64, far, near)
        return c

    lax.fori_loop(0, rows // 8, one, 0, unroll=8)


def join_halves(full_ref, a_ref, b_ref, rows):
    lanes = lanes_of()

    def one(k, c):
        at = pl.ds(pl.multiple_of(k * 8, 8), 8)
        a, b = a_ref[at, :], b_ref[at, :]
        full_ref[at, :] = jnp.where(lanes < 64, a, b)
        joined = pltpu.roll(jnp.where(lanes < 64, b, a), 64, axis=1)
        full_ref[pl.ds(pl.multiple_of(k * 8 + rows, 8), 8), :] = joined
        return c

    lax.fori_loop(0, rows // 8, one, 0, unroll=8)


def own_body(flag_ref, state_ref, mixing_ref, wet_ref, x_ref, a_ref, b_ref, full_ref):
    levels = rows_of().astype(jnp.float32)
    odd = flag_ref[0] == 1
    fold = flag_ref[1] == 1
    order = jnp.where(odd, 7 - rows_of(), rows_of())
    x_ref[OWN_WET:OWN, :] = jnp.take_along_axis(wet_ref[...].astype(jnp.float32), order, axis=0)

    def load(turned):
        for r in range(8):
            wet = spread(x_ref, OWN_WET + r)
            source = 7 - r if turned else r
            for g in range(GROUPS):
                deep = wet > levels + float(8 * g)
                for k in range(4):
                    tile = state_ref[pl.ds(k * 8 * LEV + g * 64 + source, 8, stride=8), :]
                    at = (k * 8 + r) * LEV + 8 * g
                    x_ref[at : at + 8, :] = jnp.where(deep, -tile if turned and k == NORTH else tile, 0.0)
                at = (COUP * 8 + r) * LEV + 8 * g
                tile = mixing_ref[pl.ds(g * 64 + source, 8, stride=8), :]
                x_ref[at : at + 8, :] = jnp.where(wet > levels + float(8 * g + 1), tile, 0.0)

    pl.when(odd)(lambda: load(True))
    pl.when(jnp.logical_not(odd))(lambda: load(False))

    @pl.when(jnp.logical_not(fold))
    def _():
        for k in SLOT:
            if k == NORTH:
                for j in range(COUNT[k]):
                    copy_block(full_ref, (SLOT[k] + j) * LEV, x_ref, (k * 8 + j) * LEV, lambda t: -t)
            else:
                copy_blocks(full_ref, SLOT[k] * LEV, x_ref, k * 8 * LEV, COUNT[k])
        full_ref[BULK_WET : BULK_WET + 8, :] = x_ref[OWN_WET:OWN, :]
        a_ref[...] = full_ref[0:HALF, :]
        b_ref[...] = full_ref[HALF : 2 * HALF, :]

    @pl.when(fold)
    def _():
        for k in SLOT:
            sign = (lambda t: -mirror(t)) if k in (EAST, NORTH) else mirror
            for j in range(COUNT[k]):
                copy_block(full_ref, (SLOT[k] + j) * LEV, x_ref, (k * 8 + j) * LEV, sign)
        full_ref[BULK_WET : BULK_WET + 8, :] = mirror(x_ref[OWN_WET:OWN, :])
        split_halves(full_ref, a_ref, b_ref, HALF)


def block_at(k, place):
    return (k * ROWS + place) * LEV


def wet_row(ref, place, source, row):
    ref[WET_AT + place : WET_AT + place + 1, :] = source[row : row + 1, :]


def pack_strips(strips, frame_ref, east_ref, west_ref):
    lanes = lanes_of()
    zero = jnp.zeros((8, 128), jnp.float32)

    def add_strip(out, tile, n, shift):
        here = (lanes >= STRIP * n) & (lanes < STRIP * (n + 1))
        return jnp.where(here, pltpu.roll(tile, (STRIP * n + shift) % 128, axis=1), out)

    def pack(g, c):
        first = pl.multiple_of(g * 8, 8)
        for p in range(strips.packs):
            to_east = to_west = zero
            for n, (k, place) in enumerate(strips.items[p * WIDE : (p + 1) * WIDE]):
                tile = frame_ref[pl.ds(first + block_at(k, place), 8), :]
                to_east = add_strip(to_east, tile, n, STRIP)
                to_west = add_strip(to_west, tile, n, 0)
            east_ref[pl.ds(first + p * LEV, 8), :] = to_east
            west_ref[pl.ds(first + p * LEV, 8), :] = to_west
        return c

    lax.fori_loop(0, GROUPS, pack, 0)
    for t in range(0, 32, 8):
        tile = frame_ref[WET_AT + t : WET_AT + t + 8, :]
        east_ref[strips.wet + t : strips.wet + t + 8, :] = add_strip(zero, tile, 0, STRIP)
        west_ref[strips.wet + t : strips.wet + t + 8, :] = add_strip(zero, tile, 0, 0)


def early_frame_body(flag_ref, x_ref, y_ref, b_in, b_ref, c_ref, frame_ref, east_ref, west_ref, full_ref):
    fold = flag_ref[1] == 1
    b_ref[0:HALF, :] = b_in[...]

    @pl.when(jnp.logical_not(fold))
    def _():
        for k in (TEMP, SALT):
            copy_blocks(b_ref, HALF + k * LEV, y_ref, (k * 8 + 7) * LEV, 1)
        b_ref[HALF + 2 * LEV : HALF + 2 * LEV + 8, :] = spread(y_ref, OWN_WET + 7)
        b_ref[HALF + 2 * LEV + 8 : HALF + MORE, :] = jnp.zeros((MORE - 2 * LEV - 8, 128), jnp.float32)
        c_ref[...] = jnp.zeros((MORE, 128), jnp.float32)

    @pl.when(fold)
    def _():
        for n, (source, k, row, change) in enumerate(
            (
                (y_ref, TEMP, 7, mirror),
                (y_ref, SALT, 7, mirror),
                (y_ref, NORTH, 7, mirror),
                (y_ref, TEMP, 6, mirror),
                (y_ref, SALT, 6, mirror),
                (x_ref, EAST, 7, lambda t: -mirror(t)),
                (x_ref, COUP, 6, mirror),
            )
        ):
            copy_block(full_ref, n * LEV, source, (k * 8 + row) * LEV, change)
        wet = jnp.where(rows_of() == 0, spread(y_ref, OWN_WET + 7), spread(y_ref, OWN_WET + 6))
        full_ref[MORE_WET : MORE_WET + 8, :] = mirror(wet)
        split_halves(full_ref, c_ref, b_ref.at[HALF : HALF + MORE], MORE)

    frame_ref[...] = jnp.zeros((FRAME, 128), jnp.float32)
    for k in range(5):
        copy_blocks(frame_ref, block_at(k, PLACE_NEAR[0]), x_ref, k * 8 * LEV, 8)
        for r in range(8, 16):
            change = (lambda t: -t) if k == NORTH else (lambda t: t)
            copy_block(frame_ref, block_at(k, PLACE_NEAR[r]), y_ref, (k * 8 + 15 - r) * LEV, change)
    for r in range(8):
        wet_row(frame_ref, PLACE_NEAR[r], x_ref, OWN_WET + r)
        wet_row(frame_ref, PLACE_NEAR[r + 8], y_ref, OWN_WET + 7 - r)
    pack_strips(EARLY, frame_ref, east_ref, west_ref)


def frame_body(
    flag_ref, early_ref, a_ref, b_ref, c_ref, main_early, side_early, frame_ref, far_ref, east_ref, west_ref, full_ref, more_ref
):
    fold = flag_ref[1] == 1

    def bulk(k, row, slot, count):
        for j in range(count):
            copy_blocks(frame_ref, block_at(k, PLACE_FAR[row - j]), full_ref, (SLOT[k] + slot + j) * LEV, 1)

    def send_far(slot):
        for k in (TEMP, SALT):
            copy_blocks(far_ref, k * LEV, full_ref, (SLOT[k] + slot) * LEV, 1)
        far_ref[2 * LEV : FAR, :] = spread(full_ref, BULK_WET + slot)

    frame_ref[...] = early_ref[...]

    @pl.when(jnp.logical_not(fold))
    def _():
        full_ref[0:HALF, :] = a_ref[...]
        full_ref[HALF : 2 * HALF, :] = b_ref[0:HALF, :]
        for k in range(5):
            copy_blocks(frame_ref, block_at(k, PLACE_FAR[0]), early_ref, block_at(k, PLACE_NEAR[0]), 1)
            bulk(k, -1, 0, COUNT[k])
        wet_row(frame_ref, PLACE_FAR[0], early_ref, WET_AT + PLACE_NEAR[0])
        for r in range(8):
            wet_row(frame_ref, PLACE_FAR[-1 - r], full_ref, BULK_WET + r)
        for k in (TEMP, SALT):
            copy_blocks(frame_ref, block_at(k, PLACE_FAR[-9]), b_ref, HALF + k * LEV, 1)
        wet_row(frame_ref, PLACE_FAR[-9], b_ref, HALF + 2 * LEV)
        send_far(0)

    @pl.when(fold)
    def _():
        join_halves(full_ref, a_ref, b_ref, HALF)
        join_halves(more_ref, c_ref, b_ref.at[HALF : HALF + MORE], MORE)
        for k in range(5):
            bulk(k, 0, 0, COUNT[k])
        for r in range(8):
            wet_row(frame_ref, PLACE_FAR[-r], full_ref, BULK_WET + r)
        for n, (k, row) in enumerate(
            ((TEMP, -8), (SALT, -8), (NORTH, -8), (TEMP, -9), (SALT, -9), (EAST, -7), (COUP, -6))
        ):
            copy_blocks(frame_ref, block_at(k, PLACE_FAR[row]), more_ref, n * LEV, 1)
        wet_row(frame_ref, PLACE_FAR[-8], more_ref, MORE_WET)
        wet_row(frame_ref, PLACE_FAR[-9], more_ref, MORE_WET + 1)
        send_far(1)

    pack_strips(LATE, frame_ref, east_ref, west_ref)


def east_of(a):
    return pltpu.roll(a, 127, axis=1)


def west_of(a):
    return pltpu.roll(a, 1, axis=1)


def minmod(a, b):
    return jnp.maximum(jnp.minimum(a, b), 0.0) + jnp.minimum(jnp.maximum(a, b), 0.0)


def place_of(row, far):
    if far:
        return PLACE_FAR[row] if row <= 0 else PLACE_NEAR[row]
    return PLACE_NEAR[row] if row >= 0 else PLACE_FAR[row]


WINDOW = 5


def in_turn(jobs):
    waiting, active = list(jobs), []
    while waiting or active:
        if waiting and len(active) < WINDOW:
            active.append(waiting.pop(0))
        for job in list(active):
            if next(job, "end") == "end":
                active.remove(job)


ADV = LEV + 16


def march(
    part, frame_ref, wet_ref, rate_ref, after, emit, f_ref, rhs_ref, adv_ref, adv_e_ref, p_ref, coef_ref, wet_e_ref
):
    levels = rows_of().astype(jnp.float32)
    zero = jnp.zeros((8, 128), jnp.float32)
    spans = PARTS[part]
    last = len(spans) - 1
    wet_e_ref[...] = jnp.minimum(wet_ref[...], pltpu.roll(wet_ref[...], 127, axis=1))
    for k in range(2):
        for place in range(ROWS):
            at = (k * ROWS + place) * ADV
            for ref in (adv_ref, adv_e_ref):
                ref[at : at + 8, :] = zero
                ref[at + 8 + LEV : at + ADV, :] = zero

    def eight(ref, k, place, level):
        return ref[pl.ds((k * ROWS + place) * LEV + level, 8, stride=LEV), :]

    def put_eight(ref, k, place, level, value):
        ref[pl.ds((k * ROWS + place) * LEV + level, 8, stride=LEV), :] = value

    def pivots(l, carry):
        done = []
        for tile, (above, up_above) in zip(PIVOT_TILES[part], carry):
            c = eight(frame_ref, COUP, tile, l)
            inv = 1.0 / (1.0 + c + above * (1.0 - up_above))
            up = c * inv
            put_eight(coef_ref, 0, tile, l, inv)
            put_eight(coef_ref, 1, tile, l, above * inv)
            put_eight(coef_ref, 2, tile, l, up)
            done.append((c, up))
        return tuple(done)

    lax.fori_loop(0, LEV, pivots, ((zero, zero),) * len(PIVOT_TILES[part]), unroll=4)

    def explicit(step, g):
        near_a, far_a, near_f, far_f = spans[step][:4]
        first = g * 8 if isinstance(g, int) else pl.multiple_of(g * 8, 8)
        depth = levels + (float(8 * g) if isinstance(g, int) else (g * 8).astype(jnp.float32))
        cache = {}

        def once(key, make):
            if key not in cache:
                cache[key] = make()
            return cache[key]

        def field(k, place):
            ref = frame_ref if step == 0 else f_ref
            return once((k, place), lambda: ref[pl.ds(first + block_at(k, place), 8), :])

        def pressure(place):
            return once(("p", place), lambda: p_ref[pl.ds(first + place * LEV, 8), :])

        def deep(place):
            return once(("m", place), lambda: spread(wet_ref, place) > depth)

        def face_e(place):
            return once(("e", place), lambda: spread(wet_e_ref, place) > depth)

        def to_east(k, place):
            return once(("r", k, place), lambda: east_of(field(k, place)))

        def piece(far, span_a, span_f):

            def here(row):
                return place_of(row, far)

            def face_n(row):
                return once(("n", far, row), lambda: deep(here(row)) & deep(here(row + 1)))

            def diff_n(k, row):
                def make():
                    return jnp.where(face_n(row), field(k, here(row + 1)) - field(k, here(row)), 0.0)

                return once(("d", far, k, row), make)

            def half_n(k, row):
                return once(("h", far, k, row), lambda: 0.5 * minmod(diff_n(k, row - 1), diff_n(k, row)))

            def speed_n(row):
                def make():
                    u = jnp.where(face_n(row), field(NORTH, here(row)) + field(NORTH, here(row + 1)), 0.0)
                    return u, u > 0.0

                return once(("s", far, row), make)

            def flux_n(k, row):
                def make():
                    speed, upward = speed_n(row)
                    below = field(k, here(row)) + half_n(k, row)
                    above = field(k, here(row + 1)) - half_n(k, row + 1)
                    return speed * jnp.where(upward, below, above)

                return once(("f", far, k, row), make)

            def work(row):
                place = here(row)
                mask_e = face_e(place)
                tracers = (TEMP, SALT)
                new_fields = row in span_f
                for k in (TEMP, SALT, EAST):
                    to_east(k, place)
                if new_fields:
                    to_east(NORTH, place)
                    p_e = east_of(pressure(place))
                yield
                diffs = [jnp.where(mask_e, to_east(k, place) - field(k, place), 0.0) for k in range(4 if new_fields else 2)]
                terms = list(diffs)
                if new_fields:
                    terms[EAST] = VISCOSITY * diffs[EAST] - (0.5 * PRESSURE) * pressure(place)
                diffs_w = [west_of(d) for d in terms]
                yield
                halves = [0.5 * minmod(diffs_w[k], diffs[k]) for k in tracers]
                beyond = [east_of(field(k, place) - halves[k]) for k in tracers]
                yield
                speed_e = jnp.where(mask_e, field(EAST, place) + to_east(EAST, place), 0.0)
                fluxes = [
                    speed_e * jnp.where(speed_e > 0.0, field(k, place) + halves[k], beyond[k]) for k in tracers
                ]
                fluxes_w = [west_of(f) for f in fluxes]
                yield
                for k in tracers if row in span_a else ():
                    div = (fluxes[k] - fluxes_w[k]) + (flux_n(k, row) - flux_n(k, row - 1))
                    out = jnp.where(deep(place), field(k, place) - (0.5 * ADVECT) * div, 0.0)
                    adv_ref[pl.ds(first + (k * ROWS + place) * ADV + 8, 8), :] = out
                    if new_fields:
                        adv_e_ref[pl.ds(first + (k * ROWS + place) * ADV + 8, 8), :] = east_of(out)
                if new_fields:
                    u, v = field(EAST, place), field(NORTH, place)
                    rate = spread(rate_ref, place)
                    push_n = pressure(here(row + 1)) - pressure(here(row - 1))
                    lap_n = [diff_n(k, row) - diff_n(k, row - 1) for k in (EAST, NORTH)]
                    u1 = u + rate * v - (0.5 * PRESSURE) * p_e + VISCOSITY * (diffs[EAST] + lap_n[0]) - diffs_w[EAST]
                    lap = (diffs[NORTH] - diffs_w[NORTH]) + lap_n[1]
                    v1 = v - rate * u - (0.5 * PRESSURE) * push_n + VISCOSITY * lap
                    for k, out in ((EAST, u1), (NORTH, v1)):
                        rhs_ref[pl.ds(first + (k * ROWS + place) * LEV, 8), :] = jnp.where(deep(place), out, 0.0)

            return [work(row) for row in sorted({*span_a, *span_f})]

        in_turn(piece(False, near_a, near_f) + piece(True, far_a, far_f))

    def lateral(step, g):
        near_f, far_f = spans[step][2:4]
        first = g * 8 if isinstance(g, int) else pl.multiple_of(g * 8, 8)
        depth = levels + (float(8 * g) if isinstance(g, int) else (g * 8).astype(jnp.float32))
        cache = {}

        def once(key, make):
            if key not in cache:
                cache[key] = make()
            return cache[key]

        def tracer(k, place, shift=0):
            at = first + (k * ROWS + place) * ADV + 8 + shift
            return once((k, place, shift), lambda: adv_ref[pl.ds(at, 8), :])

        def grad(k, place):
            return once(("g", k, place), lambda: tracer(k, place, 1) - tracer(k, place, -1))

        def deep(place):
            return once(("m", place), lambda: spread(wet_ref, place) > depth)

        def fluxes(mask, dt, ds, gt, gs):
            gr = EXPAND_SALT * gs - EXPAND_HEAT * gt
            dr = EXPAND_SALT * ds - EXPAND_HEAT * dt
            slope = dr * gr / (gr * gr + 16.0)
            return jnp.where(mask, dt - slope * gt, 0.0), jnp.where(mask, ds - slope * gs, 0.0)

        def piece(far, span_f):
            def here(row):
                return place_of(row, far)

            def flux_n(row):
                def make():
                    a, b = here(row), here(row + 1)
                    return fluxes(
                        deep(a) & deep(b),
                        tracer(TEMP, b) - tracer(TEMP, a),
                        tracer(SALT, b) - tracer(SALT, a),
                        grad(TEMP, a) + grad(TEMP, b),
                        grad(SALT, a) + grad(SALT, b),
                    )

                return once(("f", far, row), make)

            def work(row):
                place = here(row)
                cells = [(tracer(k, place), grad(k, place)) for k in (TEMP, SALT)]
                beyond = []
                for k in (TEMP, SALT):
                    at = first + (k * ROWS + place) * ADV + 8
                    q, below, above = (adv_e_ref[pl.ds(at + shift, 8), :] for shift in (0, 1, -1))
                    beyond.append((q, below - above))
                yield
                flux_n(row)
                yield
                (t, gt), (s, gs) = cells
                (t_e, gt_e), (s_e, gs_e) = beyond
                east = fluxes(spread(wet_e_ref, place) > depth, t_e - t, s_e - s, gt + gt_e, gs + gs_e)
                west = [west_of(f) for f in east]
                yield
                for k in (TEMP, SALT):
                    div = (east[k] - west[k]) + (flux_n(row)[k] - flux_n(row - 1)[k])
                    out = jnp.where(deep(place), cells[k][0] + DIFFUSE * div, 0.0)
                    rhs_ref[pl.ds(first + (k * ROWS + place) * LEV, 8), :] = out

            return [work(row) for row in sorted(span_f)]

        in_turn(piece(False, near_f) + piece(True, far_f))

    for step in range(len(spans)):
        source = frame_ref if step == 0 else f_ref
        weights, tiles = spans[step][4:]

        def weigh(l, carry):
            done = []
            for tile, p in zip(weights, carry):
                p = p + (EXPAND_SALT * eight(source, SALT, tile, l) - EXPAND_HEAT * eight(source, TEMP, tile, l))
                put_eight(p_ref, 0, tile, l, p)
                done.append(p)
            return tuple(done)

        lax.fori_loop(0, LEV, weigh, (zero,) * len(weights), unroll=UNROLL["column"])

        def explicit_group(g, c):
            explicit(step, g)
            return c

        def lateral_group(g, c):
            lateral(step, g)
            return c

        lax.fori_loop(0, GROUPS, explicit_group, 0)
        after(step, "adv")
        lax.fori_loop(0, GROUPS, lateral_group, 0)

        def down(l, carry):
            loads = [(eight(coef_ref, 0, t, l), eight(coef_ref, 1, t, l), [eight(rhs_ref, k, t, l) for k in range(4)]) for t in tiles]
            done = []
            for (inv, low, rhs), above in zip(loads, carry):
                done.append(tuple(rhs[k] * inv + low * above[k] for k in range(4)))
            for tile, solved in zip(tiles, done):
                for k in range(4):
                    put_eight(rhs_ref, k, tile, l, solved[k])
            return tuple(done)

        def up(i, carry):
            l = LEV - 1 - i
            done = []
            for tile, below in zip(tiles, carry):
                factor = eight(coef_ref, 2, tile, l)
                solved = []
                for k in range(4):
                    x = eight(rhs_ref, k, tile, l) + factor * below[k]
                    if emit is None or step < last:
                        put_eight(f_ref, k, tile, l, x)
                    else:
                        emit(k, l, x)
                    solved.append(x)
                done.append(tuple(solved))
            return tuple(done)

        start = ((zero,) * 4,) * len(tiles)
        lax.fori_loop(0, LEV, down, start, unroll=UNROLL["column"])
        lax.fori_loop(0, LEV, up, start, unroll=UNROLL["column"])
        after(step, "new")


WORK = [
    (4 * ROWS * LEV, 128),
    (4 * ROWS * LEV, 128),
    (2 * ROWS * ADV, 128),
    (2 * ROWS * ADV, 128),
    (ROWS * LEV, 128),
    (3 * ROWS * LEV, 128),
    (32, 128),
]
HANDED_SHAPES = [
    shape for rows, adv_rows in HANDED for shape in ((2 * len(adv_rows) * ADV, 128), (4 * len(rows) * LEV, 128))
]


def early(frame_ref, wet_ref, rate_ref, outs, work):
    f_ref, _, adv_ref = work[:3]

    def after(step, what):
        rows, adv_rows = HANDED[step]
        adv_out, new_out = outs[2 * step : 2 * step + 2]
        if what == "adv":
            for k in range(2):
                for n, r in enumerate(adv_rows):
                    at, to = (k * ROWS + PLACE_NEAR[r]) * ADV, (k * len(adv_rows) + n) * ADV
                    adv_out[to : to + ADV, :] = adv_ref[at : at + ADV, :]
        else:
            for k in range(4):
                copy_blocks(new_out, k * len(rows) * LEV, f_ref, block_at(k, PLACE_NEAR[rows[0]]), len(rows))

    march("early", frame_ref, wet_ref, rate_ref, after, None, *work)


def late(frame_ref, wet_ref, rate_ref, emit, ins, work):
    f_ref, _, adv_ref, adv_e_ref = work[:4]

    def after(step, what):
        if step >= len(HANDED):
            return
        rows, adv_rows = HANDED[step]
        adv_in, new_in = ins[2 * step : 2 * step + 2]
        if what == "adv":
            for k in range(2):
                for n, r in enumerate(adv_rows):
                    at, source = (k * ROWS + PLACE_NEAR[r]) * ADV, (k * len(adv_rows) + n) * ADV
                    adv_ref[at : at + ADV, :] = adv_in[source : source + ADV, :]
                    if r in PARTS["late"][step][2]:
                        for g in range(GROUPS):
                            to, part = at + 8 + 8 * g, source + 8 + 8 * g
                            adv_e_ref[to : to + 8, :] = east_of(adv_in[part : part + 8, :])
        else:
            for k in range(4):
                copy_blocks(f_ref, block_at(k, PLACE_NEAR[rows[0]]), new_in, k * len(rows) * LEV, len(rows))

    march("late", frame_ref, wet_ref, rate_ref, after, emit, *work)


def early_main_body(flag_ref, frame_ref, rate_ref, *rest):
    outs, (wet_ref, *work) = rest[:4], rest[4:]
    wet_ref[...] = frame_ref[WET_AT : WET_AT + 32, :]
    early(frame_ref, wet_ref, rate_ref, outs, work)


def edges(tile):
    return jnp.where(lanes_of() < 64, pltpu.roll(tile, 32, axis=1), pltpu.roll(tile, 96, axis=1))


def with_strips(tile, west, east, n):
    lanes = lanes_of()
    out = edges(tile)
    west = pltpu.roll(west, (32 - STRIP - STRIP * n) % 128, axis=1)
    east = pltpu.roll(east, (96 - STRIP * n) % 128, axis=1)
    out = jnp.where((lanes >= 32 - STRIP) & (lanes < 32), west, out)
    return jnp.where((lanes >= 96) & (lanes < 96 + STRIP), east, out)


def unpack_strips(strips, frame_ref, east_ref, west_ref, side_ref):
    def unpack(g, c):
        first = pl.multiple_of(g * 8, 8)
        for n, (k, place) in enumerate(strips.items):
            at = pl.ds(first + block_at(k, place), 8)
            p = pl.ds(first + n // WIDE * LEV, 8)
            side_ref[at, :] = with_strips(frame_ref[at, :], east_ref[p, :], west_ref[p, :], n % WIDE)
        return c

    lax.fori_loop(0, GROUPS, unpack, 0)


def unpack_wet(strips, tile_ref, east_ref, west_ref, out_ref, base, places):
    rows = rows_of()
    for t in range(0, 32, 8):
        at = strips.wet + t
        here = [p - t for p in places if t <= p < t + 8]
        if here:
            tile = with_strips(tile_ref[WET_AT + t : WET_AT + t + 8, :], east_ref[at : at + 8, :], west_ref[at : at + 8, :], 0)
            mask = rows == here[0]
            for p in here[1:]:
                mask = mask | (rows == p)
            out_ref[base + t : base + t + 8, :] = jnp.where(mask, tile, out_ref[base + t : base + t + 8, :])


def early_side_body(flag_ref, frame_ref, rate_ref, east_ref, west_ref, side_ref, *rest):
    outs, work = rest[:4], rest[4:]
    wet_ref, *work = work
    side_ref[...] = jnp.zeros((FRAME, 128), jnp.float32)
    unpack_strips(EARLY, frame_ref, east_ref, west_ref, side_ref)
    unpack_wet(EARLY, frame_ref, east_ref, west_ref, side_ref, WET_AT, [PLACE_NEAR[r] for r in range(16)])
    wet_ref[...] = side_ref[WET_AT : WET_AT + 32, :]
    early(side_ref, wet_ref, rate_ref, outs, work)


def late_main_body(flag_ref, frame_in, far_ref, rate_ref, *rest):
    ins, (out_ref, frame_ref, wet_ref, *work) = rest[:4], rest[4:]
    frame_ref[...] = frame_in[...]
    for k in (TEMP, SALT):
        copy_blocks(frame_ref, block_at(k, PLACE_NEAR[16]), far_ref, k * LEV, 1)
    wet_row(frame_ref, PLACE_NEAR[16], far_ref, 2 * LEV)
    wet_ref[...] = frame_ref[WET_AT : WET_AT + 32, :]

    def emit(k, l, x):
        out_ref[k, l] = x

    late(frame_ref, wet_ref, rate_ref, emit, ins, work)


def late_side_body(flag_ref, frame_in, far_ref, rate_ref, side_in, east_ref, west_ref, main_ref, *rest):
    ins, (out_ref, frame_ref, wet_ref, *work) = rest[:4], rest[4:]
    frame_ref[...] = side_in[...]
    unpack_strips(LATE, frame_in, east_ref, west_ref, frame_ref)
    unpack_wet(LATE, frame_in, east_ref, west_ref, frame_ref, WET_AT, [PLACE_FAR[-r] for r in range(9)])
    for k in (TEMP, SALT):
        copy_block(frame_ref, block_at(k, PLACE_NEAR[16]), far_ref, k * LEV, edges)
        copy_block(frame_ref, block_at(k, PLACE_FAR[-9]), frame_in, block_at(k, PLACE_FAR[-9]), edges)
    wet_ref[...] = frame_ref[WET_AT : WET_AT + 32, :]
    for place, row in (
        (PLACE_NEAR[16], spread(far_ref, 2 * LEV)),
        (PLACE_FAR[-9], spread(frame_in, WET_AT + PLACE_FAR[-9])),
    ):
        wet_ref[place : place + 1, :] = edges(row)[0:1, :]
    lanes = lanes_of()
    odd = flag_ref[0] == 1
    order = jnp.where(odd, 7 - rows_of(), rows_of())
    sign = jnp.where(odd, -1.0, 1.0)

    def emit(k, l, x):
        out = jnp.where(lanes < STRIP, pltpu.roll(x, 96, axis=1), main_ref[k, l])
        out = jnp.where(lanes >= 128 - STRIP, pltpu.roll(x, 32, axis=1), out)
        out = jnp.take_along_axis(out, order, axis=0)
        out_ref[k, l] = out * sign if k == NORTH else out

    late(frame_ref, wet_ref, rate_ref, emit, ins, work)


def local(state, mixing, wet_levels):
    lons, lats = lax.axis_size("lon"), lax.axis_size("lat")
    lat = lax.axis_index("lat")
    odd = lax.rem(lat, 2)
    flags = jnp.stack([odd, (lat == lats - 1).astype(jnp.int32)]).astype(jnp.int32)
    rows = jnp.array([PLACE_ROW.get(p, 0) for p in range(32)], jnp.int32)
    grid_rows = lat * 8 + jnp.where(odd == 1, 7 - rows, rows)
    grid_rows = jnp.where(grid_rows > lats * 8 - 1, 2 * (lats * 8 - 1) - grid_rows, grid_rows).astype(jnp.float32)
    rate = CORIOLIS * jnp.sin(math.pi * (grid_rows + 0.5) / (lats * 8) - 0.9)
    rate = jnp.broadcast_to(jnp.where(odd == 1, -rate, rate)[:, None], (32, 128))

    def at(o, a):
        return o * lats + a

    pairs = [(at(o, a), at(o, a ^ 1)) for o in range(lons) for a in range(lats)]
    cross = [(at(o, a), at(o, a + 1 if a % 2 else a - 1)) for o in range(lons) for a in range(1, lats - 1)]
    fold_a = [(at(o, lats - 1), at((lons - o) % lons, lats - 1)) for o in range(lons)]
    fold_b = [(at(o, lats - 1), at(lons - 1 - o, lats - 1)) for o in range(lons)]
    both = ("lon", "lat")

    half = (HALF, 128)
    x, a, b = call(own_body, [(OWN, 128), half, half], [SM] + [VM] * 3, 10**6, [(2 * HALF, 128)])(
        flags, state.reshape(4 * LEV * 8, 128), mixing.reshape(LEV * 8, 128), wet_levels
    )
    a = lax.ppermute(a, both, cross + fold_a)
    y = lax.ppermute(x, both, pairs)
    to_east_pairs = [(i, (i + 1) % lons) for i in range(lons)]
    to_west_pairs = [((i + 1) % lons, i) for i in range(lons)]
    b, c, early_frame, to_east, to_west = call(
        early_frame_body,
        [(HALF + MORE, 128), (MORE, 128), (FRAME, 128), EARLY.shape, EARLY.shape],
        [SM, VM, VM, VM],
        10**6,
        [(2 * MORE, 128)],
    )(flags, x, y, b)
    from_west = lax.ppermute(to_east, "lon", to_east_pairs)
    from_east = lax.ppermute(to_west, "lon", to_west_pairs)
    b = lax.ppermute(b, both, cross + fold_b)
    c = lax.ppermute(c, both, fold_a)
    wet = (32, 128)
    main_early = call(early_main_body, HANDED_SHAPES, [SM, VM, VM], 10**9, [wet] + WORK)(flags, early_frame, rate)
    side_frame, *side_early = call(
        early_side_body, [(FRAME, 128)] + HANDED_SHAPES, [SM] + [VM] * 4, 10**11, [wet] + WORK
    )(flags, early_frame, rate, from_west, from_east)
    frame, far, to_east, to_west = call(
        frame_body,
        [(FRAME, 128), (FAR, 128), LATE.shape, LATE.shape],
        [SM] + [VM] * 4 + [pl.BlockSpec(memory_space=pl.ANY)] * 2,
        10**6,
        [(2 * HALF, 128), (2 * MORE, 128)],
    )(flags, early_frame, a, b, c, main_early[0], side_early[0])
    far = lax.ppermute(far, both, pairs)
    from_west = lax.ppermute(to_east, "lon", to_east_pairs)
    from_east = lax.ppermute(to_west, "lon", to_west_pairs)
    work = [(FRAME, 128), wet] + WORK
    (middle,) = call(late_main_body, [state.shape], [SM] + [VM] * 7, 10**9, work)(flags, frame, far, rate, *main_early)
    (out,) = call(late_side_body, [state.shape], [SM] + [VM] * 11, 10**9, work)(
        flags, frame, far, rate, side_frame, from_west, from_east, middle, *side_early
    )
    return out


def solution(mesh):
    return jax.shard_map(
        local,
        mesh=mesh,
        in_specs=(P(None, None, "lat", "lon"), P(None, "lat", "lon"), P("lat", "lon")),
        out_specs=P(None, None, "lat", "lon"),
        check_vma=False,
    )
```

```python
import math

import jax
import jax.numpy as jnp
from jax import lax
from jax.experimental import pallas as pl
from jax.experimental.pallas import tpu as pltpu
from jax.sharding import PartitionSpec as P

STEPS = 3
LEV = 40
GROUPS = LEV // 8
ADVECT = 0.15
DIFFUSE = 0.12
VISCOSITY = 0.1
PRESSURE = 0.03
CORIOLIS = 0.3
EXPAND_HEAT = 0.6
EXPAND_SALT = 0.8

TEMP, SALT, EAST, NORTH, COUP = range(5)

ROWS = 27
PLACE_NEAR = {16: 0, 15: 1, 14: 2, 13: 6} | {r: 14 + r for r in range(13)}
PLACE_FAR = {-9: 3, -8: 4, -7: 5} | {-r: 13 - r for r in range(7)}
PLACE_ROW = {p: r for r, p in (PLACE_NEAR | PLACE_FAR).items()} | {14: 0, 13: 0}
WET_AT = 5 * ROWS * LEV
FRAME = WET_AT + 32

OWN_WET = 40 * LEV
OWN = OWN_WET + 8
SLOT = {TEMP: 0, SALT: 8, NORTH: 16, EAST: 24, COUP: 31}
COUNT = {TEMP: 8, SALT: 8, NORTH: 8, EAST: 7, COUP: 6}
BULK_WET = 37 * LEV
HALF = (BULK_WET + 8) // 2
MORE = 144
MORE_WET = 7 * LEV
FAR = 2 * LEV + 8
STRIP = 9
WIDE = 14


class Strips:
    def __init__(self, items):
        self.items = items
        self.packs = -(-len(items) // WIDE)
        self.wet = self.packs * LEV
        self.shape = (self.wet + 32, 128)


EARLY = Strips([(k, PLACE_NEAR[r]) for k in range(4) for r in range(16)] + [(COUP, PLACE_NEAR[r]) for r in range(14)])
LATE = Strips(
    [(k, PLACE_FAR[-r]) for k in (TEMP, SALT, NORTH) for r in range(9)]
    + [(EAST, PLACE_FAR[-r]) for r in range(8)]
    + [(COUP, PLACE_FAR[-r]) for r in range(7)]
)

PARTS = {
    "early": (
        (range(2, 14), (), range(3, 13), (), (6, 16, 19), (17, 19)),
        (range(5, 11), (), range(6, 10), (), (19,), (19,)),
    ),
    "late": (
        ((0, 1, 14), range(0, -8, -1), (0, 1, 2, 13), range(0, -7, -1), (2, 10, 19), (6, 14)),
        ((0, 1, 2, 3, 4, 11), range(0, -5, -1), (0, 1, 2, 3, 4, 5, 10), range(0, -4, -1), (9, 17, 19), (10, 18)),
        (range(0, 9), (-1,), range(0, 8), (), (12, 15), (14,)),
    ),
}
PIVOT_TILES = {"early": (17, 19), "late": (6, 14, 19)}
HANDED = ((range(3, 13), (2, 3, 12, 13)), (range(6, 10), (5, 6, 9, 10)))

VM = pl.BlockSpec(memory_space=pltpu.VMEM)
SM = pl.BlockSpec(memory_space=pltpu.SMEM)
LIMIT = 32 * 1024 * 1024
UNROLL = {"column": 8}


def call(body, outs, ins, flops, scratch=()):
    return pl.pallas_call(
        body,
        out_shape=tuple(jax.ShapeDtypeStruct(s, jnp.float32) for s in outs),
        in_specs=ins,
        out_specs=tuple(VM for _ in outs),
        scratch_shapes=[pltpu.VMEM(s, jnp.float32) if isinstance(s, tuple) else s for s in scratch],
        compiler_params=pltpu.CompilerParams(vmem_limit_bytes=LIMIT),
        cost_estimate=pl.CostEstimate(flops=flops, bytes_accessed=4 * 1024 * 1024, transcendentals=0),
    )


def rows_of(shape=(8, 128)):
    return lax.broadcasted_iota(jnp.int32, shape, 0)


def lanes_of(shape=(8, 128)):
    return lax.broadcasted_iota(jnp.int32, shape, 1)


def mirror(tile):
    return jnp.take_along_axis(tile, 127 - lanes_of(), axis=1)


def spread(ref, row):
    return jnp.broadcast_to(ref[row : row + 1, :], (8, 128))


def copy_block(out, to, source, at, change=lambda t: t):
    for g in range(GROUPS):
        out[to + 8 * g : to + 8 * g + 8, :] = change(source[at + 8 * g : at + 8 * g + 8, :])


def copy_blocks(out, to, source, at, count):
    if count:
        out[to : to + count * LEV, :] = source[at : at + count * LEV, :]


def split_halves(full_ref, a_ref, b_ref, rows):
    lanes = lanes_of()

    def one(k, c):
        at = pl.ds(pl.multiple_of(k * 8, 8), 8)
        near = pltpu.roll(full_ref[at, :], 64, axis=1)
        far = full_ref[pl.ds(pl.multiple_of(k * 8 + rows, 8), 8), :]
        a_ref[at, :] = jnp.where(lanes < 64, near, far)
        b_ref[at, :] = jnp.where(lanes < 64, far, near)
        return c

    lax.fori_loop(0, rows // 8, one, 0, unroll=8)


def join_halves(full_ref, a_ref, b_ref, rows):
    lanes = lanes_of()

    def one(k, c):
        at = pl.ds(pl.multiple_of(k * 8, 8), 8)
        a, b = a_ref[at, :], b_ref[at, :]
        full_ref[at, :] = jnp.where(lanes < 64, a, b)
        joined = pltpu.roll(jnp.where(lanes < 64, b, a), 64, axis=1)
        full_ref[pl.ds(pl.multiple_of(k * 8 + rows, 8), 8), :] = joined
        return c

    lax.fori_loop(0, rows // 8, one, 0, unroll=8)


def own_body(
    flag_ref, state_in, mixing_in, wet_in, x_ref, a_ref, b_ref, full_ref, state_ref, mixing_ref, wet_ref, arrived
):
    pairs = ((wet_in, wet_ref), (mixing_in, mixing_ref), (state_in, state_ref))
    copies = [pltpu.make_async_copy(source, out, arrived.at[n]) for n, (source, out) in enumerate(pairs)]
    for copy in copies:
        copy.start()
    for copy in copies:
        copy.wait()
    levels = rows_of().astype(jnp.float32)
    odd = flag_ref[0] == 1
    fold = flag_ref[1] == 1
    order = jnp.where(odd, 7 - rows_of(), rows_of())
    x_ref[OWN_WET:OWN, :] = jnp.take_along_axis(wet_ref[...].astype(jnp.float32), order, axis=0)

    def load(turned):
        for r in range(8):
            wet = spread(x_ref, OWN_WET + r)
            source = 7 - r if turned else r
            for g in range(GROUPS):
                deep = wet > levels + float(8 * g)
                for k in range(4):
                    tile = state_ref[pl.ds(k * 8 * LEV + g * 64 + source, 8, stride=8), :]
                    at = (k * 8 + r) * LEV + 8 * g
                    x_ref[at : at + 8, :] = jnp.where(deep, -tile if turned and k == NORTH else tile, 0.0)
                at = (COUP * 8 + r) * LEV + 8 * g
                tile = mixing_ref[pl.ds(g * 64 + source, 8, stride=8), :]
                x_ref[at : at + 8, :] = jnp.where(wet > levels + float(8 * g + 1), tile, 0.0)

    pl.when(odd)(lambda: load(True))
    pl.when(jnp.logical_not(odd))(lambda: load(False))

    @pl.when(jnp.logical_not(fold))
    def _():
        for k in SLOT:
            if k == NORTH:
                for j in range(COUNT[k]):
                    copy_block(full_ref, (SLOT[k] + j) * LEV, x_ref, (k * 8 + j) * LEV, lambda t: -t)
            else:
                copy_blocks(full_ref, SLOT[k] * LEV, x_ref, k * 8 * LEV, COUNT[k])
        full_ref[BULK_WET : BULK_WET + 8, :] = x_ref[OWN_WET:OWN, :]
        a_ref[...] = full_ref[0:HALF, :]
        b_ref[...] = full_ref[HALF : 2 * HALF, :]

    @pl.when(fold)
    def _():
        for k in SLOT:
            sign = (lambda t: -mirror(t)) if k in (EAST, NORTH) else mirror
            for j in range(COUNT[k]):
                copy_block(full_ref, (SLOT[k] + j) * LEV, x_ref, (k * 8 + j) * LEV, sign)
        full_ref[BULK_WET : BULK_WET + 8, :] = mirror(x_ref[OWN_WET:OWN, :])
        split_halves(full_ref, a_ref, b_ref, HALF)


def block_at(k, place):
    return (k * ROWS + place) * LEV


def wet_row(ref, place, source, row):
    ref[WET_AT + place : WET_AT + place + 1, :] = source[row : row + 1, :]


def pack_strips(strips, frame_ref, east_ref, west_ref):
    lanes = lanes_of()
    zero = jnp.zeros((8, 128), jnp.float32)

    def add_strip(out, tile, n, shift):
        here = (lanes >= STRIP * n) & (lanes < STRIP * (n + 1))
        return jnp.where(here, pltpu.roll(tile, (STRIP * n + shift) % 128, axis=1), out)

    def pack(g, c):
        first = pl.multiple_of(g * 8, 8)
        for p in range(strips.packs):
            to_east = to_west = zero
            for n, (k, place) in enumerate(strips.items[p * WIDE : (p + 1) * WIDE]):
                tile = frame_ref[pl.ds(first + block_at(k, place), 8), :]
                to_east = add_strip(to_east, tile, n, STRIP)
                to_west = add_strip(to_west, tile, n, 0)
            east_ref[pl.ds(first + p * LEV, 8), :] = to_east
            west_ref[pl.ds(first + p * LEV, 8), :] = to_west
        return c

    lax.fori_loop(0, GROUPS, pack, 0)
    for t in range(0, 32, 8):
        tile = frame_ref[WET_AT + t : WET_AT + t + 8, :]
        east_ref[strips.wet + t : strips.wet + t + 8, :] = add_strip(zero, tile, 0, STRIP)
        west_ref[strips.wet + t : strips.wet + t + 8, :] = add_strip(zero, tile, 0, 0)


def early_frame_body(flag_ref, x_ref, y_ref, b_in, b_ref, c_ref, frame_ref, east_ref, west_ref, full_ref):
    fold = flag_ref[1] == 1
    b_ref[0:HALF, :] = b_in[...]

    @pl.when(jnp.logical_not(fold))
    def _():
        for k in (TEMP, SALT):
            copy_blocks(b_ref, HALF + k * LEV, y_ref, (k * 8 + 7) * LEV, 1)
        b_ref[HALF + 2 * LEV : HALF + 2 * LEV + 8, :] = spread(y_ref, OWN_WET + 7)
        b_ref[HALF + 2 * LEV + 8 : HALF + MORE, :] = jnp.zeros((MORE - 2 * LEV - 8, 128), jnp.float32)
        c_ref[...] = jnp.zeros((MORE, 128), jnp.float32)

    @pl.when(fold)
    def _():
        for n, (source, k, row, change) in enumerate(
            (
                (y_ref, TEMP, 7, mirror),
                (y_ref, SALT, 7, mirror),
                (y_ref, NORTH, 7, mirror),
                (y_ref, TEMP, 6, mirror),
                (y_ref, SALT, 6, mirror),
                (x_ref, EAST, 7, lambda t: -mirror(t)),
                (x_ref, COUP, 6, mirror),
            )
        ):
            copy_block(full_ref, n * LEV, source, (k * 8 + row) * LEV, change)
        wet = jnp.where(rows_of() == 0, spread(y_ref, OWN_WET + 7), spread(y_ref, OWN_WET + 6))
        full_ref[MORE_WET : MORE_WET + 8, :] = mirror(wet)
        split_halves(full_ref, c_ref, b_ref.at[HALF : HALF + MORE], MORE)

    for k in range(5):
        copy_blocks(frame_ref, block_at(k, PLACE_NEAR[0]), x_ref, k * 8 * LEV, 8)
        for r in range(8, 16):
            change = (lambda t: -t) if k == NORTH else (lambda t: t)
            copy_block(frame_ref, block_at(k, PLACE_NEAR[r]), y_ref, (k * 8 + 15 - r) * LEV, change)
    for r in range(8):
        wet_row(frame_ref, PLACE_NEAR[r], x_ref, OWN_WET + r)
        wet_row(frame_ref, PLACE_NEAR[r + 8], y_ref, OWN_WET + 7 - r)
    pack_strips(EARLY, frame_ref, east_ref, west_ref)


def frame_body(
    flag_ref, early_ref, a_ref, b_ref, c_ref, main_early, side_early, frame_ref, far_ref, east_ref, west_ref, full_ref, more_ref
):
    fold = flag_ref[1] == 1

    def bulk(k, row, slot, count):
        for j in range(count):
            copy_blocks(frame_ref, block_at(k, PLACE_FAR[row - j]), full_ref, (SLOT[k] + slot + j) * LEV, 1)

    def send_far(slot):
        for k in (TEMP, SALT):
            copy_blocks(far_ref, k * LEV, full_ref, (SLOT[k] + slot) * LEV, 1)
        far_ref[2 * LEV : FAR, :] = spread(full_ref, BULK_WET + slot)

    frame_ref[...] = early_ref[...]

    @pl.when(jnp.logical_not(fold))
    def _():
        full_ref[0:HALF, :] = a_ref[...]
        full_ref[HALF : 2 * HALF, :] = b_ref[0:HALF, :]
        for k in range(5):
            copy_blocks(frame_ref, block_at(k, PLACE_FAR[0]), early_ref, block_at(k, PLACE_NEAR[0]), 1)
            bulk(k, -1, 0, COUNT[k])
        wet_row(frame_ref, PLACE_FAR[0], early_ref, WET_AT + PLACE_NEAR[0])
        for r in range(8):
            wet_row(frame_ref, PLACE_FAR[-1 - r], full_ref, BULK_WET + r)
        for k in (TEMP, SALT):
            copy_blocks(frame_ref, block_at(k, PLACE_FAR[-9]), b_ref, HALF + k * LEV, 1)
        wet_row(frame_ref, PLACE_FAR[-9], b_ref, HALF + 2 * LEV)
        send_far(0)

    @pl.when(fold)
    def _():
        join_halves(full_ref, a_ref, b_ref, HALF)
        join_halves(more_ref, c_ref, b_ref.at[HALF : HALF + MORE], MORE)
        for k in range(5):
            bulk(k, 0, 0, COUNT[k])
        for r in range(8):
            wet_row(frame_ref, PLACE_FAR[-r], full_ref, BULK_WET + r)
        for n, (k, row) in enumerate(
            ((TEMP, -8), (SALT, -8), (NORTH, -8), (TEMP, -9), (SALT, -9), (EAST, -7), (COUP, -6))
        ):
            copy_blocks(frame_ref, block_at(k, PLACE_FAR[row]), more_ref, n * LEV, 1)
        wet_row(frame_ref, PLACE_FAR[-8], more_ref, MORE_WET)
        wet_row(frame_ref, PLACE_FAR[-9], more_ref, MORE_WET + 1)
        send_far(1)

    pack_strips(LATE, frame_ref, east_ref, west_ref)


def east_of(a):
    return pltpu.roll(a, 127, axis=1)


def west_of(a):
    return pltpu.roll(a, 1, axis=1)


def minmod(a, b):
    return jnp.maximum(jnp.minimum(a, b), 0.0) + jnp.minimum(jnp.maximum(a, b), 0.0)


def place_of(row, far):
    if far:
        return PLACE_FAR[row] if row <= 0 else PLACE_NEAR[row]
    return PLACE_NEAR[row] if row >= 0 else PLACE_FAR[row]


WINDOW = 5


def in_turn(jobs):
    waiting, active = list(jobs), []
    while waiting or active:
        if waiting and len(active) < WINDOW:
            active.append(waiting.pop(0))
        for job in list(active):
            if next(job, "end") == "end":
                active.remove(job)


ADV = LEV + 16


def march(
    part, frame_ref, wet_ref, rate_ref, after, emit, f_ref, rhs_ref, adv_ref, adv_e_ref, p_ref, coef_ref, wet_e_ref, far_ref=None
):
    levels = rows_of().astype(jnp.float32)
    zero = jnp.zeros((8, 128), jnp.float32)
    spans = PARTS[part]
    last = len(spans) - 1
    wet_e_ref[...] = jnp.minimum(wet_ref[...], pltpu.roll(wet_ref[...], 127, axis=1))
    for k in range(2):
        for place in range(ROWS):
            at = (k * ROWS + place) * ADV
            for ref in (adv_ref, adv_e_ref):
                ref[at : at + 8, :] = zero
                ref[at + 8 + LEV : at + ADV, :] = zero

    def eight(ref, k, place, level):
        return ref[pl.ds((k * ROWS + place) * LEV + level, 8, stride=LEV), :]

    def put_eight(ref, k, place, level, value):
        ref[pl.ds((k * ROWS + place) * LEV + level, 8, stride=LEV), :] = value

    def pivots(l, carry):
        done = []
        for tile, (above, up_above) in zip(PIVOT_TILES[part], carry):
            c = eight(frame_ref, COUP, tile, l)
            inv = 1.0 / (1.0 + c + above * (1.0 - up_above))
            up = c * inv
            put_eight(coef_ref, 0, tile, l, inv)
            put_eight(coef_ref, 1, tile, l, above * inv)
            put_eight(coef_ref, 2, tile, l, up)
            done.append((c, up))
        return tuple(done)

    lax.fori_loop(0, LEV, pivots, ((zero, zero),) * len(PIVOT_TILES[part]), unroll=4)

    def explicit(step, g):
        near_a, far_a, near_f, far_f = spans[step][:4]
        first = g * 8 if isinstance(g, int) else pl.multiple_of(g * 8, 8)
        depth = levels + (float(8 * g) if isinstance(g, int) else (g * 8).astype(jnp.float32))
        cache = {}

        def once(key, make):
            if key not in cache:
                cache[key] = make()
            return cache[key]

        def field(k, place):
            if step == 0 and far_ref is not None and place == PLACE_NEAR[16] and k in (TEMP, SALT):
                return once((k, place), lambda: far_ref[pl.ds(first + k * LEV, 8), :])
            ref = frame_ref if step == 0 else f_ref
            return once((k, place), lambda: ref[pl.ds(first + block_at(k, place), 8), :])

        def pressure(place):
            return once(("p", place), lambda: p_ref[pl.ds(first + place * LEV, 8), :])

        def deep(place):
            return once(("m", place), lambda: spread(wet_ref, place) > depth)

        def face_e(place):
            return once(("e", place), lambda: spread(wet_e_ref, place) > depth)

        def to_east(k, place):
            return once(("r", k, place), lambda: east_of(field(k, place)))

        def piece(far, span_a, span_f):

            def here(row):
                return place_of(row, far)

            def face_n(row):
                return once(("n", far, row), lambda: deep(here(row)) & deep(here(row + 1)))

            def diff_n(k, row):
                def make():
                    return jnp.where(face_n(row), field(k, here(row + 1)) - field(k, here(row)), 0.0)

                return once(("d", far, k, row), make)

            def half_n(k, row):
                return once(("h", far, k, row), lambda: 0.5 * minmod(diff_n(k, row - 1), diff_n(k, row)))

            def speed_n(row):
                def make():
                    u = jnp.where(face_n(row), field(NORTH, here(row)) + field(NORTH, here(row + 1)), 0.0)
                    return u, u > 0.0

                return once(("s", far, row), make)

            def flux_n(k, row):
                def make():
                    speed, upward = speed_n(row)
                    below = field(k, here(row)) + half_n(k, row)
                    above = field(k, here(row + 1)) - half_n(k, row + 1)
                    return speed * jnp.where(upward, below, above)

                return once(("f", far, k, row), make)

            def work(row):
                place = here(row)
                mask_e = face_e(place)
                tracers = (TEMP, SALT)
                new_fields = row in span_f
                for k in (TEMP, SALT, EAST):
                    to_east(k, place)
                if new_fields:
                    to_east(NORTH, place)
                    p_e = east_of(pressure(place))
                yield
                diffs = [jnp.where(mask_e, to_east(k, place) - field(k, place), 0.0) for k in range(4 if new_fields else 2)]
                terms = list(diffs)
                if new_fields:
                    terms[EAST] = VISCOSITY * diffs[EAST] - (0.5 * PRESSURE) * pressure(place)
                diffs_w = [west_of(d) for d in terms]
                yield
                halves = [0.5 * minmod(diffs_w[k], diffs[k]) for k in tracers]
                beyond = [east_of(field(k, place) - halves[k]) for k in tracers]
                yield
                speed_e = jnp.where(mask_e, field(EAST, place) + to_east(EAST, place), 0.0)
                fluxes = [
                    speed_e * jnp.where(speed_e > 0.0, field(k, place) + halves[k], beyond[k]) for k in tracers
                ]
                fluxes_w = [west_of(f) for f in fluxes]
                yield
                for k in tracers if row in span_a else ():
                    div = (fluxes[k] - fluxes_w[k]) + (flux_n(k, row) - flux_n(k, row - 1))
                    out = jnp.where(deep(place), field(k, place) - (0.5 * ADVECT) * div, 0.0)
                    adv_ref[pl.ds(first + (k * ROWS + place) * ADV + 8, 8), :] = out
                    if new_fields:
                        adv_e_ref[pl.ds(first + (k * ROWS + place) * ADV + 8, 8), :] = east_of(out)
                if new_fields:
                    u, v = field(EAST, place), field(NORTH, place)
                    rate = spread(rate_ref, place)
                    push_n = pressure(here(row + 1)) - pressure(here(row - 1))
                    lap_n = [diff_n(k, row) - diff_n(k, row - 1) for k in (EAST, NORTH)]
                    u1 = u + rate * v - (0.5 * PRESSURE) * p_e + VISCOSITY * (diffs[EAST] + lap_n[0]) - diffs_w[EAST]
                    lap = (diffs[NORTH] - diffs_w[NORTH]) + lap_n[1]
                    v1 = v - rate * u - (0.5 * PRESSURE) * push_n + VISCOSITY * lap
                    for k, out in ((EAST, u1), (NORTH, v1)):
                        rhs_ref[pl.ds(first + (k * ROWS + place) * LEV, 8), :] = jnp.where(deep(place), out, 0.0)

            return [work(row) for row in sorted({*span_a, *span_f})]

        in_turn(piece(False, near_a, near_f) + piece(True, far_a, far_f))

    def lateral(step, g):
        near_f, far_f = spans[step][2:4]
        first = g * 8 if isinstance(g, int) else pl.multiple_of(g * 8, 8)
        depth = levels + (float(8 * g) if isinstance(g, int) else (g * 8).astype(jnp.float32))
        cache = {}

        def once(key, make):
            if key not in cache:
                cache[key] = make()
            return cache[key]

        def tracer(k, place, shift=0):
            at = first + (k * ROWS + place) * ADV + 8 + shift
            return once((k, place, shift), lambda: adv_ref[pl.ds(at, 8), :])

        def grad(k, place):
            return once(("g", k, place), lambda: tracer(k, place, 1) - tracer(k, place, -1))

        def deep(place):
            return once(("m", place), lambda: spread(wet_ref, place) > depth)

        def fluxes(mask, dt, ds, gt, gs):
            gr = EXPAND_SALT * gs - EXPAND_HEAT * gt
            dr = EXPAND_SALT * ds - EXPAND_HEAT * dt
            slope = dr * gr / (gr * gr + 16.0)
            return jnp.where(mask, dt - slope * gt, 0.0), jnp.where(mask, ds - slope * gs, 0.0)

        def piece(far, span_f):
            def here(row):
                return place_of(row, far)

            def flux_n(row):
                def make():
                    a, b = here(row), here(row + 1)
                    return fluxes(
                        deep(a) & deep(b),
                        tracer(TEMP, b) - tracer(TEMP, a),
                        tracer(SALT, b) - tracer(SALT, a),
                        grad(TEMP, a) + grad(TEMP, b),
                        grad(SALT, a) + grad(SALT, b),
                    )

                return once(("f", far, row), make)

            def work(row):
                place = here(row)
                cells = [(tracer(k, place), grad(k, place)) for k in (TEMP, SALT)]
                beyond = []
                for k in (TEMP, SALT):
                    at = first + (k * ROWS + place) * ADV + 8
                    q, below, above = (adv_e_ref[pl.ds(at + shift, 8), :] for shift in (0, 1, -1))
                    beyond.append((q, below - above))
                yield
                flux_n(row)
                yield
                (t, gt), (s, gs) = cells
                (t_e, gt_e), (s_e, gs_e) = beyond
                east = fluxes(spread(wet_e_ref, place) > depth, t_e - t, s_e - s, gt + gt_e, gs + gs_e)
                west = [west_of(f) for f in east]
                yield
                for k in (TEMP, SALT):
                    div = (east[k] - west[k]) + (flux_n(row)[k] - flux_n(row - 1)[k])
                    out = jnp.where(deep(place), cells[k][0] + DIFFUSE * div, 0.0)
                    rhs_ref[pl.ds(first + (k * ROWS + place) * LEV, 8), :] = out

            return [work(row) for row in sorted(span_f)]

        in_turn(piece(False, near_f) + piece(True, far_f))

    for step in range(len(spans)):
        source = frame_ref if step == 0 else f_ref
        weights, tiles = spans[step][4:]

        def weigh(l, carry):
            done = []
            for tile, p in zip(weights, carry):
                p = p + (EXPAND_SALT * eight(source, SALT, tile, l) - EXPAND_HEAT * eight(source, TEMP, tile, l))
                put_eight(p_ref, 0, tile, l, p)
                done.append(p)
            return tuple(done)

        lax.fori_loop(0, LEV, weigh, (zero,) * len(weights), unroll=UNROLL["column"])

        def explicit_group(g, c):
            explicit(step, g)
            return c

        def lateral_group(g, c):
            lateral(step, g)
            return c

        lax.fori_loop(0, GROUPS, explicit_group, 0)
        after(step, "adv")
        lax.fori_loop(0, GROUPS, lateral_group, 0)

        def down(l, carry):
            loads = [(eight(coef_ref, 0, t, l), eight(coef_ref, 1, t, l), [eight(rhs_ref, k, t, l) for k in range(4)]) for t in tiles]
            done = []
            for (inv, low, rhs), above in zip(loads, carry):
                done.append(tuple(rhs[k] * inv + low * above[k] for k in range(4)))
            for tile, solved in zip(tiles, done):
                for k in range(4):
                    put_eight(rhs_ref, k, tile, l, solved[k])
            return tuple(done)

        def up(i, carry):
            l = LEV - 1 - i
            done = []
            for tile, below in zip(tiles, carry):
                factor = eight(coef_ref, 2, tile, l)
                solved = []
                for k in range(4):
                    x = eight(rhs_ref, k, tile, l) + factor * below[k]
                    if emit is None or step < last:
                        put_eight(f_ref, k, tile, l, x)
                    else:
                        emit(k, l, x)
                    solved.append(x)
                done.append(tuple(solved))
            return tuple(done)

        start = ((zero,) * 4,) * len(tiles)
        lax.fori_loop(0, LEV, down, start, unroll=UNROLL["column"])
        lax.fori_loop(0, LEV, up, start, unroll=UNROLL["column"])
        after(step, "new")


WORK = [
    (4 * ROWS * LEV, 128),
    (4 * ROWS * LEV, 128),
    (2 * ROWS * ADV, 128),
    (2 * ROWS * ADV, 128),
    (ROWS * LEV, 128),
    (3 * ROWS * LEV, 128),
    (32, 128),
]
HANDED_SHAPES = [
    shape for rows, adv_rows in HANDED for shape in ((2 * len(adv_rows) * ADV, 128), (4 * len(rows) * LEV, 128))
]


def early(frame_ref, wet_ref, rate_ref, outs, work):
    f_ref, _, adv_ref = work[:3]

    def after(step, what):
        rows, adv_rows = HANDED[step]
        adv_out, new_out = outs[2 * step : 2 * step + 2]
        if what == "adv":
            for k in range(2):
                for n, r in enumerate(adv_rows):
                    at, to = (k * ROWS + PLACE_NEAR[r]) * ADV, (k * len(adv_rows) + n) * ADV
                    adv_out[to : to + ADV, :] = adv_ref[at : at + ADV, :]
        else:
            for k in range(4):
                copy_blocks(new_out, k * len(rows) * LEV, f_ref, block_at(k, PLACE_NEAR[rows[0]]), len(rows))

    march("early", frame_ref, wet_ref, rate_ref, after, None, *work)


def late(frame_ref, wet_ref, rate_ref, emit, ins, work, far_ref=None):
    f_ref, _, adv_ref, adv_e_ref = work[:4]

    def after(step, what):
        if step >= len(HANDED):
            return
        rows, adv_rows = HANDED[step]
        adv_in, new_in = ins[2 * step : 2 * step + 2]
        if what == "adv":
            for k in range(2):
                for n, r in enumerate(adv_rows):
                    at, source = (k * ROWS + PLACE_NEAR[r]) * ADV, (k * len(adv_rows) + n) * ADV
                    adv_ref[at : at + ADV, :] = adv_in[source : source + ADV, :]
                    if r in PARTS["late"][step][2]:
                        for g in range(GROUPS):
                            to, part = at + 8 + 8 * g, source + 8 + 8 * g
                            adv_e_ref[to : to + 8, :] = east_of(adv_in[part : part + 8, :])
        else:
            for k in range(4):
                copy_blocks(f_ref, block_at(k, PLACE_NEAR[rows[0]]), new_in, k * len(rows) * LEV, len(rows))

    march("late", frame_ref, wet_ref, rate_ref, after, emit, *work, far_ref=far_ref)


def early_main_body(flag_ref, frame_ref, rate_ref, *rest):
    outs, (wet_ref, *work) = rest[:4], rest[4:]
    wet_ref[...] = frame_ref[WET_AT : WET_AT + 32, :]
    early(frame_ref, wet_ref, rate_ref, outs, work)


def edges(tile):
    return jnp.where(lanes_of() < 64, pltpu.roll(tile, 32, axis=1), pltpu.roll(tile, 96, axis=1))


def with_strips(tile, west, east, n):
    lanes = lanes_of()
    out = edges(tile)
    west = pltpu.roll(west, (32 - STRIP - STRIP * n) % 128, axis=1)
    east = pltpu.roll(east, (96 - STRIP * n) % 128, axis=1)
    out = jnp.where((lanes >= 32 - STRIP) & (lanes < 32), west, out)
    return jnp.where((lanes >= 96) & (lanes < 96 + STRIP), east, out)


def unpack_strips(strips, frame_ref, east_ref, west_ref, side_ref):
    def unpack(g, c):
        first = pl.multiple_of(g * 8, 8)
        for n, (k, place) in enumerate(strips.items):
            at = pl.ds(first + block_at(k, place), 8)
            p = pl.ds(first + n // WIDE * LEV, 8)
            side_ref[at, :] = with_strips(frame_ref[at, :], east_ref[p, :], west_ref[p, :], n % WIDE)
        return c

    lax.fori_loop(0, GROUPS, unpack, 0)


def unpack_wet(strips, tile_ref, east_ref, west_ref, out_ref, base, places):
    rows = rows_of()
    for t in range(0, 32, 8):
        at = strips.wet + t
        here = [p - t for p in places if t <= p < t + 8]
        if here:
            tile = with_strips(tile_ref[WET_AT + t : WET_AT + t + 8, :], east_ref[at : at + 8, :], west_ref[at : at + 8, :], 0)
            mask = rows == here[0]
            for p in here[1:]:
                mask = mask | (rows == p)
            out_ref[base + t : base + t + 8, :] = jnp.where(mask, tile, out_ref[base + t : base + t + 8, :])


def early_side_body(flag_ref, frame_ref, rate_ref, east_ref, west_ref, side_ref, *rest):
    outs, work = rest[:4], rest[4:]
    wet_ref, *work = work
    side_ref[...] = jnp.zeros((FRAME, 128), jnp.float32)
    unpack_strips(EARLY, frame_ref, east_ref, west_ref, side_ref)
    unpack_wet(EARLY, frame_ref, east_ref, west_ref, side_ref, WET_AT, [PLACE_NEAR[r] for r in range(16)])
    wet_ref[...] = side_ref[WET_AT : WET_AT + 32, :]
    early(side_ref, wet_ref, rate_ref, outs, work)


def late_main_body(flag_ref, frame_ref, far_ref, rate_ref, *rest):
    ins, (out_ref, wet_ref, *work) = rest[:4], rest[4:]
    wet_ref[...] = frame_ref[WET_AT : WET_AT + 32, :]
    wet_ref[PLACE_NEAR[16] : PLACE_NEAR[16] + 1, :] = far_ref[2 * LEV : 2 * LEV + 1, :]

    def emit(k, l, x):
        out_ref[k, l] = x

    late(frame_ref, wet_ref, rate_ref, emit, ins, work, far_ref)


def late_side_body(flag_ref, frame_in, far_ref, rate_ref, side_in, east_ref, west_ref, main_ref, *rest):
    ins, (out_ref, frame_ref, wet_ref, *work) = rest[:4], rest[4:]
    frame_ref[...] = side_in[...]
    unpack_strips(LATE, frame_in, east_ref, west_ref, frame_ref)
    unpack_wet(LATE, frame_in, east_ref, west_ref, frame_ref, WET_AT, [PLACE_FAR[-r] for r in range(9)])
    for k in (TEMP, SALT):
        copy_block(frame_ref, block_at(k, PLACE_NEAR[16]), far_ref, k * LEV, edges)
        copy_block(frame_ref, block_at(k, PLACE_FAR[-9]), frame_in, block_at(k, PLACE_FAR[-9]), edges)
    wet_ref[...] = frame_ref[WET_AT : WET_AT + 32, :]
    for place, row in (
        (PLACE_NEAR[16], spread(far_ref, 2 * LEV)),
        (PLACE_FAR[-9], spread(frame_in, WET_AT + PLACE_FAR[-9])),
    ):
        wet_ref[place : place + 1, :] = edges(row)[0:1, :]
    lanes = lanes_of()
    odd = flag_ref[0] == 1
    order = jnp.where(odd, 7 - rows_of(), rows_of())
    sign = jnp.where(odd, -1.0, 1.0)

    def emit(k, l, x):
        out = jnp.where(lanes < STRIP, pltpu.roll(x, 96, axis=1), main_ref[k, l])
        out = jnp.where(lanes >= 128 - STRIP, pltpu.roll(x, 32, axis=1), out)
        out = jnp.take_along_axis(out, order, axis=0)
        out_ref[k, l] = out * sign if k == NORTH else out

    late(frame_ref, wet_ref, rate_ref, emit, ins, work)


def local(state, mixing, wet_levels):
    lons, lats = lax.axis_size("lon"), lax.axis_size("lat")
    lat = lax.axis_index("lat")
    odd = lax.rem(lat, 2)
    flags = jnp.stack([odd, (lat == lats - 1).astype(jnp.int32)]).astype(jnp.int32)
    rows = jnp.array([PLACE_ROW.get(p, 0) for p in range(32)], jnp.int32)
    grid_rows = lat * 8 + jnp.where(odd == 1, 7 - rows, rows)
    grid_rows = jnp.where(grid_rows > lats * 8 - 1, 2 * (lats * 8 - 1) - grid_rows, grid_rows).astype(jnp.float32)
    rate = CORIOLIS * jnp.sin(math.pi * (grid_rows + 0.5) / (lats * 8) - 0.9)
    rate = jnp.broadcast_to(jnp.where(odd == 1, -rate, rate)[:, None], (32, 128))

    def at(o, a):
        return o * lats + a

    pairs = [(at(o, a), at(o, a ^ 1)) for o in range(lons) for a in range(lats)]
    cross = [(at(o, a), at(o, a + 1 if a % 2 else a - 1)) for o in range(lons) for a in range(1, lats - 1)]
    fold_a = [(at(o, lats - 1), at((lons - o) % lons, lats - 1)) for o in range(lons)]
    fold_b = [(at(o, lats - 1), at(lons - 1 - o, lats - 1)) for o in range(lons)]
    both = ("lon", "lat")

    half = (HALF, 128)
    x, a, b = call(
        own_body,
        [(OWN, 128), half, half],
        [SM] + [pl.BlockSpec(memory_space=pltpu.HBM)] * 3,
        10**6,
        [
            (2 * HALF, 128),
            (4 * LEV * 8, 128),
            (LEV * 8, 128),
            pltpu.VMEM(wet_levels.shape, wet_levels.dtype),
            pltpu.SemaphoreType.DMA((3,)),
        ],
    )(
        flags, state.reshape(4 * LEV * 8, 128), mixing.reshape(LEV * 8, 128), wet_levels
    )
    a = lax.ppermute(a, both, cross + fold_a)
    y = lax.ppermute(x, both, pairs)
    to_east_pairs = [(i, (i + 1) % lons) for i in range(lons)]
    to_west_pairs = [((i + 1) % lons, i) for i in range(lons)]
    b, c, early_frame, to_east, to_west = call(
        early_frame_body,
        [(HALF + MORE, 128), (MORE, 128), (FRAME, 128), EARLY.shape, EARLY.shape],
        [SM, VM, VM, VM],
        10**6,
        [(2 * MORE, 128)],
    )(flags, x, y, b)
    from_west = lax.ppermute(to_east, "lon", to_east_pairs)
    from_east = lax.ppermute(to_west, "lon", to_west_pairs)
    b = lax.ppermute(b, both, cross + fold_b)
    c = lax.ppermute(c, both, fold_a)
    wet = (32, 128)
    main_early = call(early_main_body, HANDED_SHAPES, [SM, VM, VM], 10**9, [wet] + WORK)(flags, early_frame, rate)
    side_frame, *side_early = call(
        early_side_body, [(FRAME, 128)] + HANDED_SHAPES, [SM] + [VM] * 4, 10**11, [wet] + WORK
    )(flags, early_frame, rate, from_west, from_east)
    frame, far, to_east, to_west = call(
        frame_body,
        [(FRAME, 128), (FAR, 128), LATE.shape, LATE.shape],
        [SM] + [VM] * 4 + [pl.BlockSpec(memory_space=pl.ANY)] * 2,
        10**6,
        [(2 * HALF, 128), (2 * MORE, 128)],
    )(flags, early_frame, a, b, c, main_early[0], side_early[0])
    far = lax.ppermute(far, both, pairs)
    from_west = lax.ppermute(to_east, "lon", to_east_pairs)
    from_east = lax.ppermute(to_west, "lon", to_west_pairs)
    work = [(FRAME, 128), wet] + WORK
    (middle,) = call(late_main_body, [state.shape], [SM] + [VM] * 7, 10**9, [wet] + WORK)(flags, frame, far, rate, *main_early)
    (out,) = call(late_side_body, [state.shape], [SM] + [VM] * 11, 10**9, work)(
        flags, frame, far, rate, side_frame, from_west, from_east, middle, *side_early
    )
    return out


def solution(mesh):
    return jax.shard_map(
        local,
        mesh=mesh,
        in_specs=(P(None, None, "lat", "lon"), P(None, "lat", "lon"), P("lat", "lon")),
        out_specs=P(None, None, "lat", "lon"),
        check_vma=False,
    )
```

```python
import math

import jax
import jax.numpy as jnp
from jax import lax
from jax.experimental import pallas as pl
from jax.experimental.pallas import tpu as pltpu
from jax.sharding import PartitionSpec as P

STEPS = 3
LEV = 40
GROUPS = LEV // 8
ADVECT = 0.15
DIFFUSE = 0.12
VISCOSITY = 0.1
PRESSURE = 0.03
CORIOLIS = 0.3
EXPAND_HEAT = 0.6
EXPAND_SALT = 0.8

TEMP, SALT, EAST, NORTH, COUP = range(5)

ROWS = 27
PLACE_NEAR = {16: 0, 15: 1, 14: 2, 13: 6} | {r: 14 + r for r in range(13)}
PLACE_FAR = {-9: 3, -8: 4, -7: 5} | {-r: 13 - r for r in range(7)}
PLACE_ROW = {p: r for r, p in (PLACE_NEAR | PLACE_FAR).items()} | {14: 0, 13: 0}
WET_AT = 5 * ROWS * LEV
FRAME = WET_AT + 32

OWN_WET = 40 * LEV
OWN = OWN_WET + 8
SLOT = {TEMP: 0, SALT: 8, NORTH: 16, EAST: 24, COUP: 31}
COUNT = {TEMP: 8, SALT: 8, NORTH: 8, EAST: 7, COUP: 6}
BULK_WET = 37 * LEV
HALF = (BULK_WET + 8) // 2
MORE = 144
MORE_WET = 7 * LEV
FAR = 2 * LEV + 8
STRIP = 9
WIDE = 14


class Strips:
    def __init__(self, items):
        self.items = items
        self.packs = -(-len(items) // WIDE)
        self.wet = self.packs * LEV
        self.shape = (self.wet + 32, 128)


EARLY = Strips([(k, PLACE_NEAR[r]) for k in range(4) for r in range(16)] + [(COUP, PLACE_NEAR[r]) for r in range(14)])
LATE = Strips(
    [(k, PLACE_FAR[-r]) for k in (TEMP, SALT, NORTH) for r in range(9)]
    + [(EAST, PLACE_FAR[-r]) for r in range(8)]
    + [(COUP, PLACE_FAR[-r]) for r in range(7)]
)

PARTS = {
    "early": (
        (range(2, 14), (), range(3, 13), (), (6, 16, 19), (17, 19)),
        (range(5, 11), (), range(6, 10), (), (19,), (19,)),
    ),
    "late": (
        ((0, 1, 14), range(0, -8, -1), (0, 1, 2, 13), range(0, -7, -1), (2, 10, 19), (6, 14)),
        ((0, 1, 2, 3, 4, 11), range(0, -5, -1), (0, 1, 2, 3, 4, 5, 10), range(0, -4, -1), (9, 17, 19), (10, 18)),
        (range(0, 9), (-1,), range(0, 8), (), (12, 15), (14,)),
    ),
}
PIVOT_TILES = {"early": (17, 19), "late": (6, 14, 19)}
HANDED = ((range(3, 13), (2, 3, 12, 13)), (range(6, 10), (5, 6, 9, 10)))

VM = pl.BlockSpec(memory_space=pltpu.VMEM)
SM = pl.BlockSpec(memory_space=pltpu.SMEM)
LIMIT = 32 * 1024 * 1024
UNROLL = {"column": 8}
TOGETHER = {"explicit": 0, "lateral": 0}


def call(body, outs, ins, flops, scratch=()):
    return pl.pallas_call(
        body,
        out_shape=tuple(jax.ShapeDtypeStruct(s, jnp.float32) for s in outs),
        in_specs=ins,
        out_specs=tuple(VM for _ in outs),
        scratch_shapes=[pltpu.VMEM(s, jnp.float32) for s in scratch],
        compiler_params=pltpu.CompilerParams(vmem_limit_bytes=LIMIT),
        cost_estimate=pl.CostEstimate(flops=flops, bytes_accessed=4 * 1024 * 1024, transcendentals=0),
    )


def rows_of(shape=(8, 128)):
    return lax.broadcasted_iota(jnp.int32, shape, 0)


def lanes_of(shape=(8, 128)):
    return lax.broadcasted_iota(jnp.int32, shape, 1)


def mirror(tile):
    return jnp.take_along_axis(tile, 127 - lanes_of(), axis=1)


def spread(ref, row):
    return jnp.broadcast_to(ref[row : row + 1, :], (8, 128))


def copy_block(out, to, source, at, change=lambda t: t):
    for g in range(GROUPS):
        out[to + 8 * g : to + 8 * g + 8, :] = change(source[at + 8 * g : at + 8 * g + 8, :])


def copy_blocks(out, to, source, at, count):
    if count:
        out[to : to + count * LEV, :] = source[at : at + count * LEV, :]


def split_halves(full_ref, a_ref, b_ref, rows):
    lanes = lanes_of()

    def one(k, c):
        at = pl.ds(pl.multiple_of(k * 8, 8), 8)
        near = pltpu.roll(full_ref[at, :], 64, axis=1)
        far = full_ref[pl.ds(pl.multiple_of(k * 8 + rows, 8), 8), :]
        a_ref[at, :] = jnp.where(lanes < 64, near, far)
        b_ref[at, :] = jnp.where(lanes < 64, far, near)
        return c

    lax.fori_loop(0, rows // 8, one, 0, unroll=8)


def join_halves(full_ref, a_ref, b_ref, rows):
    lanes = lanes_of()

    def one(k, c):
        at = pl.ds(pl.multiple_of(k * 8, 8), 8)
        a, b = a_ref[at, :], b_ref[at, :]
        full_ref[at, :] = jnp.where(lanes < 64, a, b)
        joined = pltpu.roll(jnp.where(lanes < 64, b, a), 64, axis=1)
        full_ref[pl.ds(pl.multiple_of(k * 8 + rows, 8), 8), :] = joined
        return c

    lax.fori_loop(0, rows // 8, one, 0, unroll=8)


def own_body(flag_ref, state_ref, mixing_ref, wet_ref, x_ref, a_ref, b_ref, full_ref):
    levels = rows_of().astype(jnp.float32)
    odd = flag_ref[0] == 1
    fold = flag_ref[1] == 1
    order = jnp.where(odd, 7 - rows_of(), rows_of())
    x_ref[OWN_WET:OWN, :] = jnp.take_along_axis(wet_ref[...].astype(jnp.float32), order, axis=0)

    def load(turned):
        for r in range(8):
            wet = spread(x_ref, OWN_WET + r)
            source = 7 - r if turned else r
            for g in range(GROUPS):
                deep = wet > levels + float(8 * g)
                for k in range(4):
                    tile = state_ref[pl.ds(k * 8 * LEV + g * 64 + source, 8, stride=8), :]
                    at = (k * 8 + r) * LEV + 8 * g
                    x_ref[at : at + 8, :] = jnp.where(deep, -tile if turned and k == NORTH else tile, 0.0)
                at = (COUP * 8 + r) * LEV + 8 * g
                tile = mixing_ref[pl.ds(g * 64 + source, 8, stride=8), :]
                x_ref[at : at + 8, :] = jnp.where(wet > levels + float(8 * g + 1), tile, 0.0)

    pl.when(odd)(lambda: load(True))
    pl.when(jnp.logical_not(odd))(lambda: load(False))

    @pl.when(jnp.logical_not(fold))
    def _():
        for k in SLOT:
            if k == NORTH:
                for j in range(COUNT[k]):
                    copy_block(full_ref, (SLOT[k] + j) * LEV, x_ref, (k * 8 + j) * LEV, lambda t: -t)
            else:
                copy_blocks(full_ref, SLOT[k] * LEV, x_ref, k * 8 * LEV, COUNT[k])
        full_ref[BULK_WET : BULK_WET + 8, :] = x_ref[OWN_WET:OWN, :]
        a_ref[...] = full_ref[0:HALF, :]
        b_ref[...] = full_ref[HALF : 2 * HALF, :]

    @pl.when(fold)
    def _():
        for k in SLOT:
            sign = (lambda t: -mirror(t)) if k in (EAST, NORTH) else mirror
            for j in range(COUNT[k]):
                copy_block(full_ref, (SLOT[k] + j) * LEV, x_ref, (k * 8 + j) * LEV, sign)
        full_ref[BULK_WET : BULK_WET + 8, :] = mirror(x_ref[OWN_WET:OWN, :])
        split_halves(full_ref, a_ref, b_ref, HALF)


def block_at(k, place):
    return (k * ROWS + place) * LEV


def wet_row(ref, place, source, row):
    ref[WET_AT + place : WET_AT + place + 1, :] = source[row : row + 1, :]


def pack_strips(strips, frame_ref, east_ref, west_ref):
    lanes = lanes_of()
    zero = jnp.zeros((8, 128), jnp.float32)

    def add_strip(out, tile, n, shift):
        here = (lanes >= STRIP * n) & (lanes < STRIP * (n + 1))
        return jnp.where(here, pltpu.roll(tile, (STRIP * n + shift) % 128, axis=1), out)

    def pack(g, c):
        first = pl.multiple_of(g * 8, 8)
        for p in range(strips.packs):
            to_east = to_west = zero
            for n, (k, place) in enumerate(strips.items[p * WIDE : (p + 1) * WIDE]):
                tile = frame_ref[pl.ds(first + block_at(k, place), 8), :]
                to_east = add_strip(to_east, tile, n, STRIP)
                to_west = add_strip(to_west, tile, n, 0)
            east_ref[pl.ds(first + p * LEV, 8), :] = to_east
            west_ref[pl.ds(first + p * LEV, 8), :] = to_west
        return c

    lax.fori_loop(0, GROUPS, pack, 0)
    for t in range(0, 32, 8):
        tile = frame_ref[WET_AT + t : WET_AT + t + 8, :]
        east_ref[strips.wet + t : strips.wet + t + 8, :] = add_strip(zero, tile, 0, STRIP)
        west_ref[strips.wet + t : strips.wet + t + 8, :] = add_strip(zero, tile, 0, 0)


def early_frame_body(
    flag_ref, x_ref, y_ref, a_in, b_in, b_ref, fold_a_ref, fold_b_ref, frame_ref, east_ref, west_ref, full_ref
):
    fold = flag_ref[1] == 1

    @pl.when(jnp.logical_not(fold))
    def _():
        for k in (TEMP, SALT):
            copy_blocks(b_ref, HALF + k * LEV, y_ref, (k * 8 + 7) * LEV, 1)
        b_ref[HALF + 2 * LEV : HALF + FAR, :] = spread(y_ref, OWN_WET + 7)
        b_ref[0:HALF, :] = b_in[...]

    @pl.when(fold)
    def _():
        for n, (source, k, row, change) in enumerate(
            (
                (y_ref, TEMP, 7, mirror),
                (y_ref, SALT, 7, mirror),
                (y_ref, NORTH, 7, mirror),
                (y_ref, TEMP, 6, mirror),
                (y_ref, SALT, 6, mirror),
                (x_ref, EAST, 7, lambda t: -mirror(t)),
                (x_ref, COUP, 6, mirror),
            )
        ):
            copy_block(full_ref, n * LEV, source, (k * 8 + row) * LEV, change)
        wet = jnp.where(rows_of() == 0, spread(y_ref, OWN_WET + 7), spread(y_ref, OWN_WET + 6))
        full_ref[MORE_WET : MORE_WET + 8, :] = mirror(wet)
        split_halves(full_ref, fold_a_ref.at[HALF : HALF + MORE], fold_b_ref.at[HALF : HALF + MORE], MORE)
        fold_a_ref[0:HALF, :] = a_in[...]
        fold_b_ref[0:HALF, :] = b_in[...]

    for k in range(5):
        copy_blocks(frame_ref, block_at(k, PLACE_NEAR[0]), x_ref, k * 8 * LEV, 8)
        for r in range(8, 16):
            change = (lambda t: -t) if k == NORTH else (lambda t: t)
            copy_block(frame_ref, block_at(k, PLACE_NEAR[r]), y_ref, (k * 8 + 15 - r) * LEV, change)
    for r in range(8):
        wet_row(frame_ref, PLACE_NEAR[r], x_ref, OWN_WET + r)
        wet_row(frame_ref, PLACE_NEAR[r + 8], y_ref, OWN_WET + 7 - r)
    pack_strips(EARLY, frame_ref, east_ref, west_ref)


def frame_body(
    flag_ref, early_ref, a_ref, b_ref, fold_a_ref, fold_b_ref, main_early, side_early, frame_ref, far_ref, east_ref, west_ref, full_ref, more_ref
):
    fold = flag_ref[1] == 1

    def bulk(k, row, slot, count):
        for j in range(count):
            copy_blocks(frame_ref, block_at(k, PLACE_FAR[row - j]), full_ref, (SLOT[k] + slot + j) * LEV, 1)

    def send_far(slot):
        for k in (TEMP, SALT):
            copy_blocks(far_ref, k * LEV, full_ref, (SLOT[k] + slot) * LEV, 1)
        far_ref[2 * LEV : FAR, :] = spread(full_ref, BULK_WET + slot)

    frame_ref[...] = early_ref[...]

    @pl.when(jnp.logical_not(fold))
    def _():
        full_ref[0:HALF, :] = a_ref[...]
        full_ref[HALF : 2 * HALF, :] = b_ref[0:HALF, :]
        for k in range(5):
            copy_blocks(frame_ref, block_at(k, PLACE_FAR[0]), early_ref, block_at(k, PLACE_NEAR[0]), 1)
            bulk(k, -1, 0, COUNT[k])
        wet_row(frame_ref, PLACE_FAR[0], early_ref, WET_AT + PLACE_NEAR[0])
        for r in range(8):
            wet_row(frame_ref, PLACE_FAR[-1 - r], full_ref, BULK_WET + r)
        for k in (TEMP, SALT):
            copy_blocks(frame_ref, block_at(k, PLACE_FAR[-9]), b_ref, HALF + k * LEV, 1)
        wet_row(frame_ref, PLACE_FAR[-9], b_ref, HALF + 2 * LEV)
        send_far(0)

    @pl.when(fold)
    def _():
        join_halves(full_ref, fold_a_ref.at[0:HALF], fold_b_ref.at[0:HALF], HALF)
        join_halves(more_ref, fold_a_ref.at[HALF : HALF + MORE], fold_b_ref.at[HALF : HALF + MORE], MORE)
        for k in range(5):
            bulk(k, 0, 0, COUNT[k])
        for r in range(8):
            wet_row(frame_ref, PLACE_FAR[-r], full_ref, BULK_WET + r)
        for n, (k, row) in enumerate(
            ((TEMP, -8), (SALT, -8), (NORTH, -8), (TEMP, -9), (SALT, -9), (EAST, -7), (COUP, -6))
        ):
            copy_blocks(frame_ref, block_at(k, PLACE_FAR[row]), more_ref, n * LEV, 1)
        wet_row(frame_ref, PLACE_FAR[-8], more_ref, MORE_WET)
        wet_row(frame_ref, PLACE_FAR[-9], more_ref, MORE_WET + 1)
        send_far(1)

    pack_strips(LATE, frame_ref, east_ref, west_ref)


def east_of(a):
    return pltpu.roll(a, 127, axis=1)


def west_of(a):
    return pltpu.roll(a, 1, axis=1)


def minmod(a, b):
    return jnp.maximum(jnp.minimum(a, b), 0.0) + jnp.minimum(jnp.maximum(a, b), 0.0)


def place_of(row, far):
    if far:
        return PLACE_FAR[row] if row <= 0 else PLACE_NEAR[row]
    return PLACE_NEAR[row] if row >= 0 else PLACE_FAR[row]


WINDOW = 5


def in_turn(jobs):
    waiting, active = list(jobs), []
    while waiting or active:
        if waiting and len(active) < WINDOW:
            active.append(waiting.pop(0))
        for job in list(active):
            if next(job, "end") == "end":
                active.remove(job)


ADV = LEV + 16


def march(
    part, frame_ref, wet_ref, rate_ref, after, emit, f_ref, rhs_ref, adv_ref, adv_e_ref, p_ref, coef_ref, wet_e_ref, far_ref=None
):
    levels = rows_of().astype(jnp.float32)
    zero = jnp.zeros((8, 128), jnp.float32)
    spans = PARTS[part]
    last = len(spans) - 1
    wet_e_ref[...] = jnp.minimum(wet_ref[...], pltpu.roll(wet_ref[...], 127, axis=1))
    for k in range(2):
        for place in range(ROWS):
            at = (k * ROWS + place) * ADV
            for ref in (adv_ref, adv_e_ref):
                ref[at : at + 8, :] = zero
                ref[at + 8 + LEV : at + ADV, :] = zero

    def eight(ref, k, place, level):
        return ref[pl.ds((k * ROWS + place) * LEV + level, 8, stride=LEV), :]

    def put_eight(ref, k, place, level, value):
        ref[pl.ds((k * ROWS + place) * LEV + level, 8, stride=LEV), :] = value

    def pivots(l, carry):
        done = []
        for tile, (above, up_above) in zip(PIVOT_TILES[part], carry):
            c = eight(frame_ref, COUP, tile, l)
            inv = 1.0 / (1.0 + c + above * (1.0 - up_above))
            up = c * inv
            put_eight(coef_ref, 0, tile, l, inv)
            put_eight(coef_ref, 1, tile, l, above * inv)
            put_eight(coef_ref, 2, tile, l, up)
            done.append((c, up))
        return tuple(done)

    lax.fori_loop(0, LEV, pivots, ((zero, zero),) * len(PIVOT_TILES[part]), unroll=4)

    def explicit(step, g):
        near_a, far_a, near_f, far_f = spans[step][:4]
        first = g * 8 if isinstance(g, int) else pl.multiple_of(g * 8, 8)
        depth = levels + (float(8 * g) if isinstance(g, int) else (g * 8).astype(jnp.float32))
        cache = {}

        def once(key, make):
            if key not in cache:
                cache[key] = make()
            return cache[key]

        def field(k, place):
            if step == 0 and far_ref is not None and place == PLACE_NEAR[16] and k in (TEMP, SALT):
                return once((k, place), lambda: far_ref[pl.ds(first + k * LEV, 8), :])
            ref = frame_ref if step == 0 else f_ref
            return once((k, place), lambda: ref[pl.ds(first + block_at(k, place), 8), :])

        def pressure(place):
            return once(("p", place), lambda: p_ref[pl.ds(first + place * LEV, 8), :])

        def deep(place):
            return once(("m", place), lambda: spread(wet_ref, place) > depth)

        def face_e(place):
            return once(("e", place), lambda: spread(wet_e_ref, place) > depth)

        def to_east(k, place):
            return once(("r", k, place), lambda: east_of(field(k, place)))

        def piece(far, span_a, span_f):

            def here(row):
                return place_of(row, far)

            def face_n(row):
                return once(("n", far, row), lambda: deep(here(row)) & deep(here(row + 1)))

            def diff_n(k, row):
                def make():
                    return jnp.where(face_n(row), field(k, here(row + 1)) - field(k, here(row)), 0.0)

                return once(("d", far, k, row), make)

            def half_n(k, row):
                return once(("h", far, k, row), lambda: 0.5 * minmod(diff_n(k, row - 1), diff_n(k, row)))

            def speed_n(row):
                def make():
                    u = jnp.where(face_n(row), field(NORTH, here(row)) + field(NORTH, here(row + 1)), 0.0)
                    return u, u > 0.0

                return once(("s", far, row), make)

            def flux_n(k, row):
                def make():
                    speed, upward = speed_n(row)
                    below = field(k, here(row)) + half_n(k, row)
                    above = field(k, here(row + 1)) - half_n(k, row + 1)
                    return speed * jnp.where(upward, below, above)

                return once(("f", far, k, row), make)

            def work(row):
                place = here(row)
                mask_e = face_e(place)
                tracers = (TEMP, SALT)
                new_fields = row in span_f
                for k in (TEMP, SALT, EAST):
                    to_east(k, place)
                if new_fields:
                    to_east(NORTH, place)
                    p_e = east_of(pressure(place))
                yield
                diffs = [jnp.where(mask_e, to_east(k, place) - field(k, place), 0.0) for k in range(4 if new_fields else 2)]
                terms = list(diffs)
                if new_fields:
                    terms[EAST] = VISCOSITY * diffs[EAST] - (0.5 * PRESSURE) * pressure(place)
                diffs_w = [west_of(d) for d in terms]
                yield
                halves = [0.5 * minmod(diffs_w[k], diffs[k]) for k in tracers]
                beyond = [east_of(field(k, place) - halves[k]) for k in tracers]
                yield
                speed_e = jnp.where(mask_e, field(EAST, place) + to_east(EAST, place), 0.0)
                fluxes = [
                    speed_e * jnp.where(speed_e > 0.0, field(k, place) + halves[k], beyond[k]) for k in tracers
                ]
                fluxes_w = [west_of(f) for f in fluxes]
                yield
                for k in tracers if row in span_a else ():
                    div = (fluxes[k] - fluxes_w[k]) + (flux_n(k, row) - flux_n(k, row - 1))
                    out = jnp.where(deep(place), field(k, place) - (0.5 * ADVECT) * div, 0.0)
                    adv_ref[pl.ds(first + (k * ROWS + place) * ADV + 8, 8), :] = out
                    if new_fields:
                        adv_e_ref[pl.ds(first + (k * ROWS + place) * ADV + 8, 8), :] = east_of(out)
                if new_fields:
                    u, v = field(EAST, place), field(NORTH, place)
                    rate = spread(rate_ref, place)
                    push_n = pressure(here(row + 1)) - pressure(here(row - 1))
                    lap_n = [diff_n(k, row) - diff_n(k, row - 1) for k in (EAST, NORTH)]
                    u1 = u + rate * v - (0.5 * PRESSURE) * p_e + VISCOSITY * (diffs[EAST] + lap_n[0]) - diffs_w[EAST]
                    lap = (diffs[NORTH] - diffs_w[NORTH]) + lap_n[1]
                    v1 = v - rate * u - (0.5 * PRESSURE) * push_n + VISCOSITY * lap
                    for k, out in ((EAST, u1), (NORTH, v1)):
                        rhs_ref[pl.ds(first + (k * ROWS + place) * LEV, 8), :] = jnp.where(deep(place), out, 0.0)

            return [work(row) for row in sorted({*span_a, *span_f})]

        return piece(False, near_a, near_f) + piece(True, far_a, far_f)

    def lateral(step, g):
        near_f, far_f = spans[step][2:4]
        first = g * 8 if isinstance(g, int) else pl.multiple_of(g * 8, 8)
        depth = levels + (float(8 * g) if isinstance(g, int) else (g * 8).astype(jnp.float32))
        cache = {}

        def once(key, make):
            if key not in cache:
                cache[key] = make()
            return cache[key]

        def tracer(k, place, shift=0):
            at = first + (k * ROWS + place) * ADV + 8 + shift
            return once((k, place, shift), lambda: adv_ref[pl.ds(at, 8), :])

        def grad(k, place):
            return once(("g", k, place), lambda: tracer(k, place, 1) - tracer(k, place, -1))

        def deep(place):
            return once(("m", place), lambda: spread(wet_ref, place) > depth)

        def fluxes(mask, dt, ds, gt, gs):
            gr = EXPAND_SALT * gs - EXPAND_HEAT * gt
            dr = EXPAND_SALT * ds - EXPAND_HEAT * dt
            slope = dr * gr / (gr * gr + 16.0)
            return jnp.where(mask, dt - slope * gt, 0.0), jnp.where(mask, ds - slope * gs, 0.0)

        def piece(far, span_f):
            def here(row):
                return place_of(row, far)

            def flux_n(row):
                def make():
                    a, b = here(row), here(row + 1)
                    return fluxes(
                        deep(a) & deep(b),
                        tracer(TEMP, b) - tracer(TEMP, a),
                        tracer(SALT, b) - tracer(SALT, a),
                        grad(TEMP, a) + grad(TEMP, b),
                        grad(SALT, a) + grad(SALT, b),
                    )

                return once(("f", far, row), make)

            def work(row):
                place = here(row)
                cells = [(tracer(k, place), grad(k, place)) for k in (TEMP, SALT)]
                beyond = []
                for k in (TEMP, SALT):
                    at = first + (k * ROWS + place) * ADV + 8
                    q, below, above = (adv_e_ref[pl.ds(at + shift, 8), :] for shift in (0, 1, -1))
                    beyond.append((q, below - above))
                yield
                flux_n(row)
                yield
                (t, gt), (s, gs) = cells
                (t_e, gt_e), (s_e, gs_e) = beyond
                east = fluxes(spread(wet_e_ref, place) > depth, t_e - t, s_e - s, gt + gt_e, gs + gs_e)
                west = [west_of(f) for f in east]
                yield
                for k in (TEMP, SALT):
                    div = (east[k] - west[k]) + (flux_n(row)[k] - flux_n(row - 1)[k])
                    out = jnp.where(deep(place), cells[k][0] + DIFFUSE * div, 0.0)
                    rhs_ref[pl.ds(first + (k * ROWS + place) * LEV, 8), :] = out

            return [work(row) for row in sorted(span_f)]

        return piece(False, near_f) + piece(True, far_f)

    for step in range(len(spans)):
        source = frame_ref if step == 0 else f_ref
        weights, tiles = spans[step][4:]

        def weigh(l, carry):
            done = []
            for tile, p in zip(weights, carry):
                p = p + (EXPAND_SALT * eight(source, SALT, tile, l) - EXPAND_HEAT * eight(source, TEMP, tile, l))
                put_eight(p_ref, 0, tile, l, p)
                done.append(p)
            return tuple(done)

        lax.fori_loop(0, LEV, weigh, (zero,) * len(weights), unroll=UNROLL["column"])

        def by_groups(make, together):
            def one(g, c):
                in_turn(make(step, g))
                return c

            if not together:
                lax.fori_loop(0, GROUPS, one, 0)
                return
            for n in range(0, GROUPS, together):
                in_turn([job for g in range(n, min(n + together, GROUPS)) for job in make(step, g)])

        by_groups(explicit, TOGETHER["explicit"])
        after(step, "adv")
        by_groups(lateral, TOGETHER["lateral"])

        def down(l, carry):
            loads = [(eight(coef_ref, 0, t, l), eight(coef_ref, 1, t, l), [eight(rhs_ref, k, t, l) for k in range(4)]) for t in tiles]
            done = []
            for (inv, low, rhs), above in zip(loads, carry):
                done.append(tuple(rhs[k] * inv + low * above[k] for k in range(4)))
            for tile, solved in zip(tiles, done):
                for k in range(4):
                    put_eight(rhs_ref, k, tile, l, solved[k])
            return tuple(done)

        def up(i, carry):
            l = LEV - 1 - i
            done = []
            for tile, below in zip(tiles, carry):
                factor = eight(coef_ref, 2, tile, l)
                solved = []
                for k in range(4):
                    x = eight(rhs_ref, k, tile, l) + factor * below[k]
                    if emit is None or step < last:
                        put_eight(f_ref, k, tile, l, x)
                    else:
                        emit(k, l, x)
                    solved.append(x)
                done.append(tuple(solved))
            return tuple(done)

        start = ((zero,) * 4,) * len(tiles)
        lax.fori_loop(0, LEV, down, start, unroll=UNROLL["column"])
        lax.fori_loop(0, LEV, up, start, unroll=UNROLL["column"])
        after(step, "new")


WORK = [
    (4 * ROWS * LEV, 128),
    (4 * ROWS * LEV, 128),
    (2 * ROWS * ADV, 128),
    (2 * ROWS * ADV, 128),
    (ROWS * LEV, 128),
    (3 * ROWS * LEV, 128),
    (32, 128),
]
HANDED_SHAPES = [
    shape for rows, adv_rows in HANDED for shape in ((2 * len(adv_rows) * ADV, 128), (4 * len(rows) * LEV, 128))
]


def early(frame_ref, wet_ref, rate_ref, outs, work):
    f_ref, _, adv_ref = work[:3]

    def after(step, what):
        rows, adv_rows = HANDED[step]
        adv_out, new_out = outs[2 * step : 2 * step + 2]
        if what == "adv":
            for k in range(2):
                for n, r in enumerate(adv_rows):
                    at, to = (k * ROWS + PLACE_NEAR[r]) * ADV, (k * len(adv_rows) + n) * ADV
                    adv_out[to : to + ADV, :] = adv_ref[at : at + ADV, :]
        else:
            for k in range(4):
                copy_blocks(new_out, k * len(rows) * LEV, f_ref, block_at(k, PLACE_NEAR[rows[0]]), len(rows))

    march("early", frame_ref, wet_ref, rate_ref, after, None, *work)


def late(frame_ref, wet_ref, rate_ref, emit, ins, work, far_ref=None):
    f_ref, _, adv_ref, adv_e_ref = work[:4]

    def after(step, what):
        if step >= len(HANDED):
            return
        rows, adv_rows = HANDED[step]
        adv_in, new_in = ins[2 * step : 2 * step + 2]
        if what == "adv":
            for k in range(2):
                for n, r in enumerate(adv_rows):
                    at, source = (k * ROWS + PLACE_NEAR[r]) * ADV, (k * len(adv_rows) + n) * ADV
                    adv_ref[at : at + ADV, :] = adv_in[source : source + ADV, :]
                    if r in PARTS["late"][step][2]:
                        for g in range(GROUPS):
                            to, part = at + 8 + 8 * g, source + 8 + 8 * g
                            adv_e_ref[to : to + 8, :] = east_of(adv_in[part : part + 8, :])
        else:
            for k in range(4):
                copy_blocks(f_ref, block_at(k, PLACE_NEAR[rows[0]]), new_in, k * len(rows) * LEV, len(rows))

    march("late", frame_ref, wet_ref, rate_ref, after, emit, *work, far_ref=far_ref)


def early_main_body(flag_ref, frame_ref, rate_ref, *rest):
    outs, (wet_ref, *work) = rest[:4], rest[4:]
    wet_ref[...] = frame_ref[WET_AT : WET_AT + 32, :]
    early(frame_ref, wet_ref, rate_ref, outs, work)


def edges(tile):
    return jnp.where(lanes_of() < 64, pltpu.roll(tile, 32, axis=1), pltpu.roll(tile, 96, axis=1))


def with_strips(tile, west, east, n):
    lanes = lanes_of()
    out = edges(tile)
    west = pltpu.roll(west, (32 - STRIP - STRIP * n) % 128, axis=1)
    east = pltpu.roll(east, (96 - STRIP * n) % 128, axis=1)
    out = jnp.where((lanes >= 32 - STRIP) & (lanes < 32), west, out)
    return jnp.where((lanes >= 96) & (lanes < 96 + STRIP), east, out)


def unpack_strips(strips, frame_ref, east_ref, west_ref, side_ref):
    def unpack(g, c):
        first = pl.multiple_of(g * 8, 8)
        for n, (k, place) in enumerate(strips.items):
            at = pl.ds(first + block_at(k, place), 8)
            p = pl.ds(first + n // WIDE * LEV, 8)
            side_ref[at, :] = with_strips(frame_ref[at, :], east_ref[p, :], west_ref[p, :], n % WIDE)
        return c

    lax.fori_loop(0, GROUPS, unpack, 0)


def unpack_wet(strips, tile_ref, east_ref, west_ref, out_ref, base, places):
    rows = rows_of()
    for t in range(0, 32, 8):
        at = strips.wet + t
        here = [p - t for p in places if t <= p < t + 8]
        if here:
            tile = with_strips(tile_ref[WET_AT + t : WET_AT + t + 8, :], east_ref[at : at + 8, :], west_ref[at : at + 8, :], 0)
            mask = rows == here[0]
            for p in here[1:]:
                mask = mask | (rows == p)
            out_ref[base + t : base + t + 8, :] = jnp.where(mask, tile, out_ref[base + t : base + t + 8, :])


def early_side_body(flag_ref, frame_ref, rate_ref, east_ref, west_ref, side_ref, *rest):
    outs, work = rest[:4], rest[4:]
    wet_ref, *work = work
    side_ref[...] = jnp.zeros((FRAME, 128), jnp.float32)
    unpack_strips(EARLY, frame_ref, east_ref, west_ref, side_ref)
    unpack_wet(EARLY, frame_ref, east_ref, west_ref, side_ref, WET_AT, [PLACE_NEAR[r] for r in range(16)])
    wet_ref[...] = side_ref[WET_AT : WET_AT + 32, :]
    early(side_ref, wet_ref, rate_ref, outs, work)


def late_main_body(flag_ref, frame_ref, far_ref, rate_ref, *rest):
    ins, (out_ref, wet_ref, *work) = rest[:4], rest[4:]
    wet_ref[...] = frame_ref[WET_AT : WET_AT + 32, :]
    wet_ref[PLACE_NEAR[16] : PLACE_NEAR[16] + 1, :] = far_ref[2 * LEV : 2 * LEV + 1, :]

    def emit(k, l, x):
        out_ref[k, l] = x

    late(frame_ref, wet_ref, rate_ref, emit, ins, work, far_ref)


def late_side_body(flag_ref, frame_in, far_ref, rate_ref, side_in, east_ref, west_ref, main_ref, *rest):
    ins, (out_ref, frame_ref, wet_ref, *work) = rest[:4], rest[4:]
    frame_ref[...] = side_in[...]
    unpack_strips(LATE, frame_in, east_ref, west_ref, frame_ref)
    unpack_wet(LATE, frame_in, east_ref, west_ref, frame_ref, WET_AT, [PLACE_FAR[-r] for r in range(9)])
    for k in (TEMP, SALT):
        copy_block(frame_ref, block_at(k, PLACE_NEAR[16]), far_ref, k * LEV, edges)
        copy_block(frame_ref, block_at(k, PLACE_FAR[-9]), frame_in, block_at(k, PLACE_FAR[-9]), edges)
    wet_ref[...] = frame_ref[WET_AT : WET_AT + 32, :]
    for place, row in (
        (PLACE_NEAR[16], spread(far_ref, 2 * LEV)),
        (PLACE_FAR[-9], spread(frame_in, WET_AT + PLACE_FAR[-9])),
    ):
        wet_ref[place : place + 1, :] = edges(row)[0:1, :]
    lanes = lanes_of()
    odd = flag_ref[0] == 1
    order = jnp.where(odd, 7 - rows_of(), rows_of())
    sign = jnp.where(odd, -1.0, 1.0)

    def emit(k, l, x):
        out = jnp.where(lanes < STRIP, pltpu.roll(x, 96, axis=1), main_ref[k, l])
        out = jnp.where(lanes >= 128 - STRIP, pltpu.roll(x, 32, axis=1), out)
        out = jnp.take_along_axis(out, order, axis=0)
        out_ref[k, l] = out * sign if k == NORTH else out

    late(frame_ref, wet_ref, rate_ref, emit, ins, work)


def local(state, mixing, wet_levels):
    lons, lats = lax.axis_size("lon"), lax.axis_size("lat")
    lat = lax.axis_index("lat")
    odd = lax.rem(lat, 2)
    flags = jnp.stack([odd, (lat == lats - 1).astype(jnp.int32)]).astype(jnp.int32)
    rows = jnp.array([PLACE_ROW.get(p, 0) for p in range(32)], jnp.int32)
    grid_rows = lat * 8 + jnp.where(odd == 1, 7 - rows, rows)
    grid_rows = jnp.where(grid_rows > lats * 8 - 1, 2 * (lats * 8 - 1) - grid_rows, grid_rows).astype(jnp.float32)
    rate = CORIOLIS * jnp.sin(math.pi * (grid_rows + 0.5) / (lats * 8) - 0.9)
    rate = jnp.broadcast_to(jnp.where(odd == 1, -rate, rate)[:, None], (32, 128))

    def at(o, a):
        return o * lats + a

    pairs = [(at(o, a), at(o, a ^ 1)) for o in range(lons) for a in range(lats)]
    cross = [(at(o, a), at(o, a + 1 if a % 2 else a - 1)) for o in range(lons) for a in range(1, lats - 1)]
    fold_a = [(at(o, lats - 1), at((lons - o) % lons, lats - 1)) for o in range(lons)]
    fold_b = [(at(o, lats - 1), at(lons - 1 - o, lats - 1)) for o in range(lons)]
    both = ("lon", "lat")

    half = (HALF, 128)
    x, a, b = call(
        own_body,
        [(OWN, 128), half, half],
        [SM] + [VM] * 3,
        10**6,
        [(2 * HALF, 128)],
    )(
        flags, state.reshape(4 * LEV * 8, 128), mixing.reshape(LEV * 8, 128), wet_levels
    )
    far_a = lax.ppermute(a, both, cross)
    y = lax.ppermute(x, both, pairs)
    to_east_pairs = [(i, (i + 1) % lons) for i in range(lons)]
    to_west_pairs = [((i + 1) % lons, i) for i in range(lons)]
    b, beyond_a, beyond_b, early_frame, to_east, to_west = call(
        early_frame_body,
        [(HALF + FAR, 128), (HALF + MORE, 128), (HALF + MORE, 128), (FRAME, 128), EARLY.shape, EARLY.shape],
        [SM] + [VM] * 4,
        10**6,
        [(2 * MORE, 128)],
    )(flags, x, y, a, b)
    from_west = lax.ppermute(to_east, "lon", to_east_pairs)
    from_east = lax.ppermute(to_west, "lon", to_west_pairs)
    far_b = lax.ppermute(b, both, cross)
    beyond_a = lax.ppermute(beyond_a, both, fold_a)
    beyond_b = lax.ppermute(beyond_b, both, fold_b)
    wet = (32, 128)
    main_early = call(early_main_body, HANDED_SHAPES, [SM, VM, VM], 10**9, [wet] + WORK)(flags, early_frame, rate)
    side_frame, *side_early = call(
        early_side_body, [(FRAME, 128)] + HANDED_SHAPES, [SM] + [VM] * 4, 10**11, [wet] + WORK
    )(flags, early_frame, rate, from_west, from_east)
    frame, far, to_east, to_west = call(
        frame_body,
        [(FRAME, 128), (FAR, 128), LATE.shape, LATE.shape],
        [SM] + [VM] * 5 + [pl.BlockSpec(memory_space=pl.ANY)] * 2,
        10**6,
        [(2 * HALF, 128), (2 * MORE, 128)],
    )(flags, early_frame, far_a, far_b, beyond_a, beyond_b, main_early[0], side_early[0])
    far = lax.ppermute(far, both, pairs)
    from_west = lax.ppermute(to_east, "lon", to_east_pairs)
    from_east = lax.ppermute(to_west, "lon", to_west_pairs)
    work = [(FRAME, 128), wet] + WORK
    (middle,) = call(late_main_body, [state.shape], [SM] + [VM] * 7, 10**9, [wet] + WORK)(flags, frame, far, rate, *main_early)
    (out,) = call(late_side_body, [state.shape], [SM] + [VM] * 11, 10**9, work)(
        flags, frame, far, rate, side_frame, from_west, from_east, middle, *side_early
    )
    return out


def solution(mesh):
    return jax.shard_map(
        local,
        mesh=mesh,
        in_specs=(P(None, None, "lat", "lon"), P(None, "lat", "lon"), P("lat", "lon")),
        out_specs=P(None, None, "lat", "lon"),
        check_vma=False,
    )
```

```python
import math

import jax
import jax.numpy as jnp
from jax import lax
from jax.experimental import pallas as pl
from jax.experimental.pallas import tpu as pltpu
from jax.sharding import PartitionSpec as P

STEPS = 3
LEV = 40
GROUPS = LEV // 8
ADVECT = 0.15
DIFFUSE = 0.12
VISCOSITY = 0.1
PRESSURE = 0.03
CORIOLIS = 0.3
EXPAND_HEAT = 0.6
EXPAND_SALT = 0.8

TEMP, SALT, EAST, NORTH, COUP = range(5)

ROWS = 27
PLACE_NEAR = {16: 0, 15: 1, 14: 2, 13: 6} | {r: 14 + r for r in range(13)}
PLACE_FAR = {-9: 3, -8: 4, -7: 5} | {-r: 13 - r for r in range(7)}
PLACE_ROW = {p: r for r, p in (PLACE_NEAR | PLACE_FAR).items()} | {14: 0, 13: 0}
WET_AT = 5 * ROWS * LEV
FRAME = WET_AT + 32

OWN_WET = 40 * LEV
OWN = OWN_WET + 8
SLOT = {TEMP: 0, SALT: 8, NORTH: 16, EAST: 24, COUP: 31}
COUNT = {TEMP: 8, SALT: 8, NORTH: 8, EAST: 7, COUP: 6}
BULK_WET = 37 * LEV
HALF = (BULK_WET + 8) // 2
MORE = 144
MORE_WET = 7 * LEV
FAR = 2 * LEV + 8
STRIP = 9
WIDE = 14


class Strips:
    def __init__(self, items):
        self.items = items
        self.packs = -(-len(items) // WIDE)
        self.wet = self.packs * LEV
        self.shape = (self.wet + 32, 128)


EARLY = Strips([(k, PLACE_NEAR[r]) for k in range(4) for r in range(16)] + [(COUP, PLACE_NEAR[r]) for r in range(14)])
LATE = Strips(
    [(k, PLACE_FAR[-r]) for k in (TEMP, SALT, NORTH) for r in range(9)]
    + [(EAST, PLACE_FAR[-r]) for r in range(8)]
    + [(COUP, PLACE_FAR[-r]) for r in range(7)]
)

PARTS = {
    "early": (
        (range(2, 14), (), range(3, 13), (), (6, 16, 19), (17, 19)),
        (range(5, 11), (), range(6, 10), (), (19,), (19,)),
    ),
    "late": (
        ((0, 1, 14), range(0, -8, -1), (0, 1, 2, 13), range(0, -7, -1), (2, 10, 19), (6, 14)),
        ((0, 1, 2, 3, 4, 11), range(0, -5, -1), (0, 1, 2, 3, 4, 5, 10), range(0, -4, -1), (9, 17, 19), (10, 18)),
        (range(0, 9), (-1,), range(0, 8), (), (12, 15), (14,)),
    ),
}
PIVOT_TILES = {"early": (17, 19), "late": (6, 14, 19)}
HANDED = ((range(3, 13), (2, 3, 12, 13)), (range(6, 10), (5, 6, 9, 10)))

VM = pl.BlockSpec(memory_space=pltpu.VMEM)
SM = pl.BlockSpec(memory_space=pltpu.SMEM)
LIMIT = 32 * 1024 * 1024
UNROLL = {"column": 8}
TOGETHER = {"explicit": 0, "lateral": 0}


def call(body, outs, ins, flops, scratch=(), limit=LIMIT):
    return pl.pallas_call(
        body,
        out_shape=tuple(jax.ShapeDtypeStruct(s, jnp.float32) for s in outs),
        in_specs=ins,
        out_specs=tuple(VM for _ in outs),
        scratch_shapes=[pltpu.VMEM(s, jnp.float32) for s in scratch],
        compiler_params=pltpu.CompilerParams(vmem_limit_bytes=limit),
        cost_estimate=pl.CostEstimate(flops=flops, bytes_accessed=4 * 1024 * 1024, transcendentals=0),
    )


def rows_of(shape=(8, 128)):
    return lax.broadcasted_iota(jnp.int32, shape, 0)


def lanes_of(shape=(8, 128)):
    return lax.broadcasted_iota(jnp.int32, shape, 1)


def mirror(tile):
    return jnp.take_along_axis(tile, 127 - lanes_of(), axis=1)


def spread(ref, row):
    return jnp.broadcast_to(ref[row : row + 1, :], (8, 128))


def copy_block(out, to, source, at, change=lambda t: t):
    for g in range(GROUPS):
        out[to + 8 * g : to + 8 * g + 8, :] = change(source[at + 8 * g : at + 8 * g + 8, :])


def copy_blocks(out, to, source, at, count):
    if count:
        out[to : to + count * LEV, :] = source[at : at + count * LEV, :]


def split_halves(full_ref, a_ref, b_ref, rows):
    lanes = lanes_of()

    def one(k, c):
        at = pl.ds(pl.multiple_of(k * 8, 8), 8)
        near = pltpu.roll(full_ref[at, :], 64, axis=1)
        far = full_ref[pl.ds(pl.multiple_of(k * 8 + rows, 8), 8), :]
        a_ref[at, :] = jnp.where(lanes < 64, near, far)
        b_ref[at, :] = jnp.where(lanes < 64, far, near)
        return c

    lax.fori_loop(0, rows // 8, one, 0, unroll=8)


def join_halves(full_ref, a_ref, b_ref, rows):
    lanes = lanes_of()

    def one(k, c):
        at = pl.ds(pl.multiple_of(k * 8, 8), 8)
        a, b = a_ref[at, :], b_ref[at, :]
        full_ref[at, :] = jnp.where(lanes < 64, a, b)
        joined = pltpu.roll(jnp.where(lanes < 64, b, a), 64, axis=1)
        full_ref[pl.ds(pl.multiple_of(k * 8 + rows, 8), 8), :] = joined
        return c

    lax.fori_loop(0, rows // 8, one, 0, unroll=8)


def own_body(flag_ref, state_ref, mixing_ref, wet_ref, x_ref, a_ref, b_ref, full_ref):
    levels = rows_of().astype(jnp.float32)
    odd = flag_ref[0] == 1
    fold = flag_ref[1] == 1
    order = jnp.where(odd, 7 - rows_of(), rows_of())
    x_ref[OWN_WET:OWN, :] = jnp.take_along_axis(wet_ref[...].astype(jnp.float32), order, axis=0)

    def load(turned):
        for r in range(8):
            wet = spread(x_ref, OWN_WET + r)
            source = 7 - r if turned else r
            for g in range(GROUPS):
                deep = wet > levels + float(8 * g)
                for k in range(4):
                    tile = state_ref[pl.ds(k * 8 * LEV + g * 64 + source, 8, stride=8), :]
                    at = (k * 8 + r) * LEV + 8 * g
                    x_ref[at : at + 8, :] = jnp.where(deep, -tile if turned and k == NORTH else tile, 0.0)
                at = (COUP * 8 + r) * LEV + 8 * g
                tile = mixing_ref[pl.ds(g * 64 + source, 8, stride=8), :]
                x_ref[at : at + 8, :] = jnp.where(wet > levels + float(8 * g + 1), tile, 0.0)

    pl.when(odd)(lambda: load(True))
    pl.when(jnp.logical_not(odd))(lambda: load(False))

    @pl.when(jnp.logical_not(fold))
    def _():
        for k in SLOT:
            if k == NORTH:
                for j in range(COUNT[k]):
                    copy_block(full_ref, (SLOT[k] + j) * LEV, x_ref, (k * 8 + j) * LEV, lambda t: -t)
            else:
                copy_blocks(full_ref, SLOT[k] * LEV, x_ref, k * 8 * LEV, COUNT[k])
        full_ref[BULK_WET : BULK_WET + 8, :] = x_ref[OWN_WET:OWN, :]
        a_ref[...] = full_ref[0:HALF, :]
        b_ref[...] = full_ref[HALF : 2 * HALF, :]

    @pl.when(fold)
    def _():
        for k in SLOT:
            sign = (lambda t: -mirror(t)) if k in (EAST, NORTH) else mirror
            for j in range(COUNT[k]):
                copy_block(full_ref, (SLOT[k] + j) * LEV, x_ref, (k * 8 + j) * LEV, sign)
        full_ref[BULK_WET : BULK_WET + 8, :] = mirror(x_ref[OWN_WET:OWN, :])
        split_halves(full_ref, a_ref, b_ref, HALF)


def block_at(k, place):
    return (k * ROWS + place) * LEV


def wet_row(ref, place, source, row):
    ref[WET_AT + place : WET_AT + place + 1, :] = source[row : row + 1, :]


def pack_strips(strips, frame_ref, east_ref, west_ref):
    lanes = lanes_of()
    zero = jnp.zeros((8, 128), jnp.float32)

    def add_strip(out, tile, n, shift):
        here = (lanes >= STRIP * n) & (lanes < STRIP * (n + 1))
        return jnp.where(here, pltpu.roll(tile, (STRIP * n + shift) % 128, axis=1), out)

    def pack(g, c):
        first = pl.multiple_of(g * 8, 8)
        for p in range(strips.packs):
            to_east = to_west = zero
            for n, (k, place) in enumerate(strips.items[p * WIDE : (p + 1) * WIDE]):
                tile = frame_ref[pl.ds(first + block_at(k, place), 8), :]
                to_east = add_strip(to_east, tile, n, STRIP)
                to_west = add_strip(to_west, tile, n, 0)
            east_ref[pl.ds(first + p * LEV, 8), :] = to_east
            west_ref[pl.ds(first + p * LEV, 8), :] = to_west
        return c

    lax.fori_loop(0, GROUPS, pack, 0)
    for t in range(0, 32, 8):
        tile = frame_ref[WET_AT + t : WET_AT + t + 8, :]
        east_ref[strips.wet + t : strips.wet + t + 8, :] = add_strip(zero, tile, 0, STRIP)
        west_ref[strips.wet + t : strips.wet + t + 8, :] = add_strip(zero, tile, 0, 0)


def early_frame_body(
    flag_ref, x_ref, y_ref, a_in, b_in, b_ref, fold_a_ref, fold_b_ref, frame_ref, east_ref, west_ref, full_ref
):
    fold = flag_ref[1] == 1

    @pl.when(jnp.logical_not(fold))
    def _():
        for k in (TEMP, SALT):
            copy_blocks(b_ref, HALF + k * LEV, y_ref, (k * 8 + 7) * LEV, 1)
        b_ref[HALF + 2 * LEV : HALF + FAR, :] = spread(y_ref, OWN_WET + 7)
        b_ref[0:HALF, :] = b_in[...]

    @pl.when(fold)
    def _():
        for n, (source, k, row, change) in enumerate(
            (
                (y_ref, TEMP, 7, mirror),
                (y_ref, SALT, 7, mirror),
                (y_ref, NORTH, 7, mirror),
                (y_ref, TEMP, 6, mirror),
                (y_ref, SALT, 6, mirror),
                (x_ref, EAST, 7, lambda t: -mirror(t)),
                (x_ref, COUP, 6, mirror),
            )
        ):
            copy_block(full_ref, n * LEV, source, (k * 8 + row) * LEV, change)
        wet = jnp.where(rows_of() == 0, spread(y_ref, OWN_WET + 7), spread(y_ref, OWN_WET + 6))
        full_ref[MORE_WET : MORE_WET + 8, :] = mirror(wet)
        split_halves(full_ref, fold_a_ref.at[HALF : HALF + MORE], fold_b_ref.at[HALF : HALF + MORE], MORE)
        fold_a_ref[0:HALF, :] = a_in[...]
        fold_b_ref[0:HALF, :] = b_in[...]

    for k in range(5):
        copy_blocks(frame_ref, block_at(k, PLACE_NEAR[0]), x_ref, k * 8 * LEV, 8)
        for r in range(8, 16):
            change = (lambda t: -t) if k == NORTH else (lambda t: t)
            copy_block(frame_ref, block_at(k, PLACE_NEAR[r]), y_ref, (k * 8 + 15 - r) * LEV, change)
    for r in range(8):
        wet_row(frame_ref, PLACE_NEAR[r], x_ref, OWN_WET + r)
        wet_row(frame_ref, PLACE_NEAR[r + 8], y_ref, OWN_WET + 7 - r)
    pack_strips(EARLY, frame_ref, east_ref, west_ref)


def frame_body(
    flag_ref, early_ref, a_ref, b_ref, fold_a_ref, fold_b_ref, main_early, side_early, frame_ref, far_ref, east_ref, west_ref, full_ref, more_ref
):
    fold = flag_ref[1] == 1

    def bulk(k, row, slot, count):
        for j in range(count):
            copy_blocks(frame_ref, block_at(k, PLACE_FAR[row - j]), full_ref, (SLOT[k] + slot + j) * LEV, 1)

    def send_far(slot):
        for k in (TEMP, SALT):
            copy_blocks(far_ref, k * LEV, full_ref, (SLOT[k] + slot) * LEV, 1)
        far_ref[2 * LEV : FAR, :] = spread(full_ref, BULK_WET + slot)

    frame_ref[...] = early_ref[...]

    @pl.when(jnp.logical_not(fold))
    def _():
        full_ref[0:HALF, :] = a_ref[...]
        full_ref[HALF : 2 * HALF, :] = b_ref[0:HALF, :]
        for k in range(5):
            copy_blocks(frame_ref, block_at(k, PLACE_FAR[0]), early_ref, block_at(k, PLACE_NEAR[0]), 1)
            bulk(k, -1, 0, COUNT[k])
        wet_row(frame_ref, PLACE_FAR[0], early_ref, WET_AT + PLACE_NEAR[0])
        for r in range(8):
            wet_row(frame_ref, PLACE_FAR[-1 - r], full_ref, BULK_WET + r)
        for k in (TEMP, SALT):
            copy_blocks(frame_ref, block_at(k, PLACE_FAR[-9]), b_ref, HALF + k * LEV, 1)
        wet_row(frame_ref, PLACE_FAR[-9], b_ref, HALF + 2 * LEV)
        send_far(0)

    @pl.when(fold)
    def _():
        join_halves(full_ref, fold_a_ref.at[0:HALF], fold_b_ref.at[0:HALF], HALF)
        join_halves(more_ref, fold_a_ref.at[HALF : HALF + MORE], fold_b_ref.at[HALF : HALF + MORE], MORE)
        for k in range(5):
            bulk(k, 0, 0, COUNT[k])
        for r in range(8):
            wet_row(frame_ref, PLACE_FAR[-r], full_ref, BULK_WET + r)
        for n, (k, row) in enumerate(
            ((TEMP, -8), (SALT, -8), (NORTH, -8), (TEMP, -9), (SALT, -9), (EAST, -7), (COUP, -6))
        ):
            copy_blocks(frame_ref, block_at(k, PLACE_FAR[row]), more_ref, n * LEV, 1)
        wet_row(frame_ref, PLACE_FAR[-8], more_ref, MORE_WET)
        wet_row(frame_ref, PLACE_FAR[-9], more_ref, MORE_WET + 1)
        send_far(1)

    pack_strips(LATE, frame_ref, east_ref, west_ref)


def east_of(a):
    return pltpu.roll(a, 127, axis=1)


def west_of(a):
    return pltpu.roll(a, 1, axis=1)


def minmod(a, b):
    return jnp.maximum(jnp.minimum(a, b), 0.0) + jnp.minimum(jnp.maximum(a, b), 0.0)


def place_of(row, far):
    if far:
        return PLACE_FAR[row] if row <= 0 else PLACE_NEAR[row]
    return PLACE_NEAR[row] if row >= 0 else PLACE_FAR[row]


WINDOW = 5


def in_turn(jobs):
    waiting, active = list(jobs), []
    while waiting or active:
        if waiting and len(active) < WINDOW:
            active.append(waiting.pop(0))
        for job in list(active):
            if next(job, "end") == "end":
                active.remove(job)


ADV = LEV + 16


def march(
    part, frame_ref, wet_ref, rate_ref, after, emit, f_ref, rhs_ref, adv_ref, adv_e_ref, p_ref, coef_ref, wet_e_ref, far_ref=None
):
    levels = rows_of().astype(jnp.float32)
    zero = jnp.zeros((8, 128), jnp.float32)
    spans = PARTS[part]
    last = len(spans) - 1
    wet_e_ref[...] = jnp.minimum(wet_ref[...], pltpu.roll(wet_ref[...], 127, axis=1))
    for k in range(2):
        for place in range(ROWS):
            at = (k * ROWS + place) * ADV
            for ref in (adv_ref, adv_e_ref):
                ref[at : at + 8, :] = zero
                ref[at + 8 + LEV : at + ADV, :] = zero

    def eight(ref, k, place, level):
        return ref[pl.ds((k * ROWS + place) * LEV + level, 8, stride=LEV), :]

    def put_eight(ref, k, place, level, value):
        ref[pl.ds((k * ROWS + place) * LEV + level, 8, stride=LEV), :] = value

    def pivots(l, carry):
        done = []
        for tile, (above, up_above) in zip(PIVOT_TILES[part], carry):
            c = eight(frame_ref, COUP, tile, l)
            inv = 1.0 / (1.0 + c + above * (1.0 - up_above))
            up = c * inv
            put_eight(coef_ref, 0, tile, l, inv)
            put_eight(coef_ref, 1, tile, l, above * inv)
            put_eight(coef_ref, 2, tile, l, up)
            done.append((c, up))
        return tuple(done)

    lax.fori_loop(0, LEV, pivots, ((zero, zero),) * len(PIVOT_TILES[part]), unroll=4)

    def explicit(step, g):
        near_a, far_a, near_f, far_f = spans[step][:4]
        first = g * 8 if isinstance(g, int) else pl.multiple_of(g * 8, 8)
        depth = levels + (float(8 * g) if isinstance(g, int) else (g * 8).astype(jnp.float32))
        cache = {}

        def once(key, make):
            if key not in cache:
                cache[key] = make()
            return cache[key]

        def field(k, place):
            if step == 0 and far_ref is not None and place == PLACE_NEAR[16] and k in (TEMP, SALT):
                return once((k, place), lambda: far_ref[pl.ds(first + k * LEV, 8), :])
            ref = frame_ref if step == 0 else f_ref
            return once((k, place), lambda: ref[pl.ds(first + block_at(k, place), 8), :])

        def pressure(place):
            return once(("p", place), lambda: p_ref[pl.ds(first + place * LEV, 8), :])

        def deep(place):
            return once(("m", place), lambda: spread(wet_ref, place) > depth)

        def face_e(place):
            return once(("e", place), lambda: spread(wet_e_ref, place) > depth)

        def to_east(k, place):
            return once(("r", k, place), lambda: east_of(field(k, place)))

        def piece(far, span_a, span_f):

            def here(row):
                return place_of(row, far)

            def face_n(row):
                return once(("n", far, row), lambda: deep(here(row)) & deep(here(row + 1)))

            def diff_n(k, row):
                def make():
                    return jnp.where(face_n(row), field(k, here(row + 1)) - field(k, here(row)), 0.0)

                return once(("d", far, k, row), make)

            def half_n(k, row):
                return once(("h", far, k, row), lambda: 0.5 * minmod(diff_n(k, row - 1), diff_n(k, row)))

            def speed_n(row):
                def make():
                    u = jnp.where(face_n(row), field(NORTH, here(row)) + field(NORTH, here(row + 1)), 0.0)
                    return u, u > 0.0

                return once(("s", far, row), make)

            def flux_n(k, row):
                def make():
                    speed, upward = speed_n(row)
                    below = field(k, here(row)) + half_n(k, row)
                    above = field(k, here(row + 1)) - half_n(k, row + 1)
                    return speed * jnp.where(upward, below, above)

                return once(("f", far, k, row), make)

            def work(row):
                place = here(row)
                mask_e = face_e(place)
                tracers = (TEMP, SALT)
                new_fields = row in span_f
                for k in (TEMP, SALT, EAST):
                    to_east(k, place)
                if new_fields:
                    to_east(NORTH, place)
                    p_e = east_of(pressure(place))
                yield
                diffs = [jnp.where(mask_e, to_east(k, place) - field(k, place), 0.0) for k in range(4 if new_fields else 2)]
                terms = list(diffs)
                if new_fields:
                    terms[EAST] = VISCOSITY * diffs[EAST] - (0.5 * PRESSURE) * pressure(place)
                diffs_w = [west_of(d) for d in terms]
                yield
                halves = [0.5 * minmod(diffs_w[k], diffs[k]) for k in tracers]
                beyond = [east_of(field(k, place) - halves[k]) for k in tracers]
                yield
                speed_e = jnp.where(mask_e, field(EAST, place) + to_east(EAST, place), 0.0)
                fluxes = [
                    speed_e * jnp.where(speed_e > 0.0, field(k, place) + halves[k], beyond[k]) for k in tracers
                ]
                fluxes_w = [west_of(f) for f in fluxes]
                yield
                for k in tracers if row in span_a else ():
                    div = (fluxes[k] - fluxes_w[k]) + (flux_n(k, row) - flux_n(k, row - 1))
                    out = jnp.where(deep(place), field(k, place) - (0.5 * ADVECT) * div, 0.0)
                    adv_ref[pl.ds(first + (k * ROWS + place) * ADV + 8, 8), :] = out
                    if new_fields:
                        adv_e_ref[pl.ds(first + (k * ROWS + place) * ADV + 8, 8), :] = east_of(out)
                if new_fields:
                    u, v = field(EAST, place), field(NORTH, place)
                    rate = spread(rate_ref, place)
                    push_n = pressure(here(row + 1)) - pressure(here(row - 1))
                    lap_n = [diff_n(k, row) - diff_n(k, row - 1) for k in (EAST, NORTH)]
                    u1 = u + rate * v - (0.5 * PRESSURE) * p_e + VISCOSITY * (diffs[EAST] + lap_n[0]) - diffs_w[EAST]
                    lap = (diffs[NORTH] - diffs_w[NORTH]) + lap_n[1]
                    v1 = v - rate * u - (0.5 * PRESSURE) * push_n + VISCOSITY * lap
                    for k, out in ((EAST, u1), (NORTH, v1)):
                        rhs_ref[pl.ds(first + (k * ROWS + place) * LEV, 8), :] = jnp.where(deep(place), out, 0.0)

            return [work(row) for row in sorted({*span_a, *span_f})]

        return piece(False, near_a, near_f) + piece(True, far_a, far_f)

    def lateral(step, g):
        near_f, far_f = spans[step][2:4]
        first = g * 8 if isinstance(g, int) else pl.multiple_of(g * 8, 8)
        depth = levels + (float(8 * g) if isinstance(g, int) else (g * 8).astype(jnp.float32))
        cache = {}

        def once(key, make):
            if key not in cache:
                cache[key] = make()
            return cache[key]

        def tracer(k, place, shift=0):
            at = first + (k * ROWS + place) * ADV + 8 + shift
            return once((k, place, shift), lambda: adv_ref[pl.ds(at, 8), :])

        def grad(k, place):
            return once(("g", k, place), lambda: tracer(k, place, 1) - tracer(k, place, -1))

        def deep(place):
            return once(("m", place), lambda: spread(wet_ref, place) > depth)

        def fluxes(mask, dt, ds, gt, gs):
            gr = EXPAND_SALT * gs - EXPAND_HEAT * gt
            dr = EXPAND_SALT * ds - EXPAND_HEAT * dt
            slope = dr * gr / (gr * gr + 16.0)
            return jnp.where(mask, dt - slope * gt, 0.0), jnp.where(mask, ds - slope * gs, 0.0)

        def piece(far, span_f):
            def here(row):
                return place_of(row, far)

            def flux_n(row):
                def make():
                    a, b = here(row), here(row + 1)
                    return fluxes(
                        deep(a) & deep(b),
                        tracer(TEMP, b) - tracer(TEMP, a),
                        tracer(SALT, b) - tracer(SALT, a),
                        grad(TEMP, a) + grad(TEMP, b),
                        grad(SALT, a) + grad(SALT, b),
                    )

                return once(("f", far, row), make)

            def work(row):
                place = here(row)
                cells = [(tracer(k, place), grad(k, place)) for k in (TEMP, SALT)]
                beyond = []
                for k in (TEMP, SALT):
                    at = first + (k * ROWS + place) * ADV + 8
                    q, below, above = (adv_e_ref[pl.ds(at + shift, 8), :] for shift in (0, 1, -1))
                    beyond.append((q, below - above))
                yield
                flux_n(row)
                yield
                (t, gt), (s, gs) = cells
                (t_e, gt_e), (s_e, gs_e) = beyond
                east = fluxes(spread(wet_e_ref, place) > depth, t_e - t, s_e - s, gt + gt_e, gs + gs_e)
                west = [west_of(f) for f in east]
                yield
                for k in (TEMP, SALT):
                    div = (east[k] - west[k]) + (flux_n(row)[k] - flux_n(row - 1)[k])
                    out = jnp.where(deep(place), cells[k][0] + DIFFUSE * div, 0.0)
                    rhs_ref[pl.ds(first + (k * ROWS + place) * LEV, 8), :] = out

            return [work(row) for row in sorted(span_f)]

        return piece(False, near_f) + piece(True, far_f)

    for step in range(len(spans)):
        source = frame_ref if step == 0 else f_ref
        weights, tiles = spans[step][4:]

        def weigh(l, carry):
            done = []
            for tile, p in zip(weights, carry):
                p = p + (EXPAND_SALT * eight(source, SALT, tile, l) - EXPAND_HEAT * eight(source, TEMP, tile, l))
                put_eight(p_ref, 0, tile, l, p)
                done.append(p)
            return tuple(done)

        lax.fori_loop(0, LEV, weigh, (zero,) * len(weights), unroll=UNROLL["column"])

        def by_groups(make, together):
            def one(g, c):
                in_turn(make(step, g))
                return c

            if not together:
                lax.fori_loop(0, GROUPS, one, 0)
                return
            for n in range(0, GROUPS, together):
                in_turn([job for g in range(n, min(n + together, GROUPS)) for job in make(step, g)])

        by_groups(explicit, TOGETHER["explicit"])
        after(step, "adv")
        by_groups(lateral, TOGETHER["lateral"])

        def down(l, carry):
            loads = [(eight(coef_ref, 0, t, l), eight(coef_ref, 1, t, l), [eight(rhs_ref, k, t, l) for k in range(4)]) for t in tiles]
            done = []
            for (inv, low, rhs), above in zip(loads, carry):
                done.append(tuple(rhs[k] * inv + low * above[k] for k in range(4)))
            for tile, solved in zip(tiles, done):
                for k in range(4):
                    put_eight(rhs_ref, k, tile, l, solved[k])
            return tuple(done)

        def up(i, carry):
            l = LEV - 1 - i
            done = []
            for tile, below in zip(tiles, carry):
                factor = eight(coef_ref, 2, tile, l)
                solved = []
                for k in range(4):
                    x = eight(rhs_ref, k, tile, l) + factor * below[k]
                    if emit is None or step < last:
                        put_eight(f_ref, k, tile, l, x)
                    else:
                        emit(k, l, x)
                    solved.append(x)
                done.append(tuple(solved))
            return tuple(done)

        start = ((zero,) * 4,) * len(tiles)
        lax.fori_loop(0, LEV, down, start, unroll=UNROLL["column"])
        lax.fori_loop(0, LEV, up, start, unroll=UNROLL["column"])
        after(step, "new")


WORK = [
    (4 * ROWS * LEV, 128),
    (4 * ROWS * LEV, 128),
    (2 * ROWS * ADV, 128),
    (2 * ROWS * ADV, 128),
    (ROWS * LEV, 128),
    (3 * ROWS * LEV, 128),
    (32, 128),
]
HANDED_SHAPES = [
    shape for rows, adv_rows in HANDED for shape in ((2 * len(adv_rows) * ADV, 128), (4 * len(rows) * LEV, 128))
]


def early(frame_ref, wet_ref, rate_ref, outs, work):
    f_ref, _, adv_ref = work[:3]

    def after(step, what):
        rows, adv_rows = HANDED[step]
        adv_out, new_out = outs[2 * step : 2 * step + 2]
        if what == "adv":
            for k in range(2):
                for n, r in enumerate(adv_rows):
                    at, to = (k * ROWS + PLACE_NEAR[r]) * ADV, (k * len(adv_rows) + n) * ADV
                    adv_out[to : to + ADV, :] = adv_ref[at : at + ADV, :]
        else:
            for k in range(4):
                copy_blocks(new_out, k * len(rows) * LEV, f_ref, block_at(k, PLACE_NEAR[rows[0]]), len(rows))

    march("early", frame_ref, wet_ref, rate_ref, after, None, *work)


def late(frame_ref, wet_ref, rate_ref, emit, ins, work, far_ref=None):
    f_ref, _, adv_ref, adv_e_ref = work[:4]

    def after(step, what):
        if step >= len(HANDED):
            return
        rows, adv_rows = HANDED[step]
        adv_in, new_in = ins[2 * step : 2 * step + 2]
        if what == "adv":
            for k in range(2):
                for n, r in enumerate(adv_rows):
                    at, source = (k * ROWS + PLACE_NEAR[r]) * ADV, (k * len(adv_rows) + n) * ADV
                    adv_ref[at : at + ADV, :] = adv_in[source : source + ADV, :]
                    if r in PARTS["late"][step][2]:
                        for g in range(GROUPS):
                            to, part = at + 8 + 8 * g, source + 8 + 8 * g
                            adv_e_ref[to : to + 8, :] = east_of(adv_in[part : part + 8, :])
        else:
            for k in range(4):
                copy_blocks(f_ref, block_at(k, PLACE_NEAR[rows[0]]), new_in, k * len(rows) * LEV, len(rows))

    march("late", frame_ref, wet_ref, rate_ref, after, emit, *work, far_ref=far_ref)


def early_main_body(flag_ref, frame_ref, rate_ref, *rest):
    outs, (wet_ref, *work) = rest[:4], rest[4:]
    wet_ref[...] = frame_ref[WET_AT : WET_AT + 32, :]
    early(frame_ref, wet_ref, rate_ref, outs, work)


def edges(tile):
    return jnp.where(lanes_of() < 64, pltpu.roll(tile, 32, axis=1), pltpu.roll(tile, 96, axis=1))


def with_strips(tile, west, east, n):
    lanes = lanes_of()
    out = edges(tile)
    west = pltpu.roll(west, (32 - STRIP - STRIP * n) % 128, axis=1)
    east = pltpu.roll(east, (96 - STRIP * n) % 128, axis=1)
    out = jnp.where((lanes >= 32 - STRIP) & (lanes < 32), west, out)
    return jnp.where((lanes >= 96) & (lanes < 96 + STRIP), east, out)


def unpack_strips(strips, frame_ref, east_ref, west_ref, side_ref):
    def unpack(g, c):
        first = pl.multiple_of(g * 8, 8)
        for n, (k, place) in enumerate(strips.items):
            at = pl.ds(first + block_at(k, place), 8)
            p = pl.ds(first + n // WIDE * LEV, 8)
            side_ref[at, :] = with_strips(frame_ref[at, :], east_ref[p, :], west_ref[p, :], n % WIDE)
        return c

    lax.fori_loop(0, GROUPS, unpack, 0)


def unpack_wet(strips, tile_ref, east_ref, west_ref, out_ref, base, places):
    rows = rows_of()
    for t in range(0, 32, 8):
        at = strips.wet + t
        here = [p - t for p in places if t <= p < t + 8]
        if here:
            tile = with_strips(tile_ref[WET_AT + t : WET_AT + t + 8, :], east_ref[at : at + 8, :], west_ref[at : at + 8, :], 0)
            mask = rows == here[0]
            for p in here[1:]:
                mask = mask | (rows == p)
            out_ref[base + t : base + t + 8, :] = jnp.where(mask, tile, out_ref[base + t : base + t + 8, :])


def early_side_body(flag_ref, frame_ref, rate_ref, east_ref, west_ref, side_ref, *rest):
    outs, work = rest[:4], rest[4:]
    wet_ref, *work = work
    side_ref[...] = jnp.zeros((FRAME, 128), jnp.float32)
    unpack_strips(EARLY, frame_ref, east_ref, west_ref, side_ref)
    unpack_wet(EARLY, frame_ref, east_ref, west_ref, side_ref, WET_AT, [PLACE_NEAR[r] for r in range(16)])
    wet_ref[...] = side_ref[WET_AT : WET_AT + 32, :]
    early(side_ref, wet_ref, rate_ref, outs, work)


def late_main_body(flag_ref, frame_ref, far_ref, rate_ref, *rest):
    ins, (out_ref, wet_ref, *work) = rest[:4], rest[4:]
    wet_ref[...] = frame_ref[WET_AT : WET_AT + 32, :]
    wet_ref[PLACE_NEAR[16] : PLACE_NEAR[16] + 1, :] = far_ref[2 * LEV : 2 * LEV + 1, :]

    def emit(k, l, x):
        out_ref[k, l] = x

    late(frame_ref, wet_ref, rate_ref, emit, ins, work, far_ref)


def late_side_body(flag_ref, frame_in, far_ref, rate_ref, side_in, east_ref, west_ref, main_ref, *rest):
    ins, (out_ref, frame_ref, wet_ref, *work) = rest[:4], rest[4:]
    frame_ref[...] = side_in[...]
    unpack_strips(LATE, frame_in, east_ref, west_ref, frame_ref)
    unpack_wet(LATE, frame_in, east_ref, west_ref, frame_ref, WET_AT, [PLACE_FAR[-r] for r in range(9)])
    for k in (TEMP, SALT):
        copy_block(frame_ref, block_at(k, PLACE_NEAR[16]), far_ref, k * LEV, edges)
        copy_block(frame_ref, block_at(k, PLACE_FAR[-9]), frame_in, block_at(k, PLACE_FAR[-9]), edges)
    wet_ref[...] = frame_ref[WET_AT : WET_AT + 32, :]
    for place, row in (
        (PLACE_NEAR[16], spread(far_ref, 2 * LEV)),
        (PLACE_FAR[-9], spread(frame_in, WET_AT + PLACE_FAR[-9])),
    ):
        wet_ref[place : place + 1, :] = edges(row)[0:1, :]
    lanes = lanes_of()
    odd = flag_ref[0] == 1
    order = jnp.where(odd, 7 - rows_of(), rows_of())
    sign = jnp.where(odd, -1.0, 1.0)

    def emit(k, l, x):
        out = jnp.where(lanes < STRIP, pltpu.roll(x, 96, axis=1), main_ref[k, l])
        out = jnp.where(lanes >= 128 - STRIP, pltpu.roll(x, 32, axis=1), out)
        out = jnp.take_along_axis(out, order, axis=0)
        out_ref[k, l] = out * sign if k == NORTH else out

    late(frame_ref, wet_ref, rate_ref, emit, ins, work)


def local(state, mixing, wet_levels):
    lons, lats = lax.axis_size("lon"), lax.axis_size("lat")
    lat = lax.axis_index("lat")
    odd = lax.rem(lat, 2)
    flags = jnp.stack([odd, (lat == lats - 1).astype(jnp.int32)]).astype(jnp.int32)
    rows = jnp.array([PLACE_ROW.get(p, 0) for p in range(32)], jnp.int32)
    grid_rows = lat * 8 + jnp.where(odd == 1, 7 - rows, rows)
    grid_rows = jnp.where(grid_rows > lats * 8 - 1, 2 * (lats * 8 - 1) - grid_rows, grid_rows).astype(jnp.float32)
    rate = CORIOLIS * jnp.sin(math.pi * (grid_rows + 0.5) / (lats * 8) - 0.9)
    rate = jnp.broadcast_to(jnp.where(odd == 1, -rate, rate)[:, None], (32, 128))

    def at(o, a):
        return o * lats + a

    pairs = [(at(o, a), at(o, a ^ 1)) for o in range(lons) for a in range(lats)]
    cross = [(at(o, a), at(o, a + 1 if a % 2 else a - 1)) for o in range(lons) for a in range(1, lats - 1)]
    fold_a = [(at(o, lats - 1), at((lons - o) % lons, lats - 1)) for o in range(lons)]
    fold_b = [(at(o, lats - 1), at(lons - 1 - o, lats - 1)) for o in range(lons)]
    both = ("lon", "lat")

    half = (HALF, 128)
    x, a, b = call(
        own_body,
        [(OWN, 128), half, half],
        [SM] + [VM] * 3,
        10**6,
        [(2 * HALF, 128)],
        limit=63 * 1024 * 1024,
    )(
        flags, state.reshape(4 * LEV * 8, 128), mixing.reshape(LEV * 8, 128), wet_levels
    )
    far_a = lax.ppermute(a, both, cross)
    y = lax.ppermute(x, both, pairs)
    to_east_pairs = [(i, (i + 1) % lons) for i in range(lons)]
    to_west_pairs = [((i + 1) % lons, i) for i in range(lons)]
    b, beyond_a, beyond_b, early_frame, to_east, to_west = call(
        early_frame_body,
        [(HALF + FAR, 128), (HALF + MORE, 128), (HALF + MORE, 128), (FRAME, 128), EARLY.shape, EARLY.shape],
        [SM] + [VM] * 4,
        10**6,
        [(2 * MORE, 128)],
    )(flags, x, y, a, b)
    from_west = lax.ppermute(to_east, "lon", to_east_pairs)
    from_east = lax.ppermute(to_west, "lon", to_west_pairs)
    far_b = lax.ppermute(b, both, cross)
    beyond_a = lax.ppermute(beyond_a, both, fold_a)
    beyond_b = lax.ppermute(beyond_b, both, fold_b)
    wet = (32, 128)
    main_early = call(early_main_body, HANDED_SHAPES, [SM, VM, VM], 10**9, [wet] + WORK)(flags, early_frame, rate)
    side_frame, *side_early = call(
        early_side_body, [(FRAME, 128)] + HANDED_SHAPES, [SM] + [VM] * 4, 10**11, [wet] + WORK
    )(flags, early_frame, rate, from_west, from_east)
    frame, far, to_east, to_west = call(
        frame_body,
        [(FRAME, 128), (FAR, 128), LATE.shape, LATE.shape],
        [SM] + [VM] * 5 + [pl.BlockSpec(memory_space=pl.ANY)] * 2,
        10**6,
        [(2 * HALF, 128), (2 * MORE, 128)],
    )(flags, early_frame, far_a, far_b, beyond_a, beyond_b, main_early[0], side_early[0])
    far = lax.ppermute(far, both, pairs)
    from_west = lax.ppermute(to_east, "lon", to_east_pairs)
    from_east = lax.ppermute(to_west, "lon", to_west_pairs)
    work = [(FRAME, 128), wet] + WORK
    (middle,) = call(late_main_body, [state.shape], [SM] + [VM] * 7, 10**9, [wet] + WORK)(flags, frame, far, rate, *main_early)
    (out,) = call(late_side_body, [state.shape], [SM] + [VM] * 11, 10**9, work)(
        flags, frame, far, rate, side_frame, from_west, from_east, middle, *side_early
    )
    return out


def solution(mesh):
    return jax.shard_map(
        local,
        mesh=mesh,
        in_specs=(P(None, None, "lat", "lon"), P(None, "lat", "lon"), P("lat", "lon")),
        out_specs=P(None, None, "lat", "lon"),
        check_vma=False,
    )
```

```python
import math

import jax
import jax.numpy as jnp
from jax import lax
from jax.experimental import pallas as pl
from jax.experimental.pallas import tpu as pltpu
from jax.sharding import PartitionSpec as P

STEPS = 3
LEV = 40
GROUPS = LEV // 8
ADVECT = 0.15
DIFFUSE = 0.12
VISCOSITY = 0.1
PRESSURE = 0.03
CORIOLIS = 0.3
EXPAND_HEAT = 0.6
EXPAND_SALT = 0.8

TEMP, SALT, EAST, NORTH, COUP = range(5)

ROWS = 27
PLACE_NEAR = {16: 0, 15: 1, 14: 2, 13: 6} | {r: 14 + r for r in range(13)}
PLACE_FAR = {-9: 3, -8: 4, -7: 5} | {-r: 13 - r for r in range(7)}
PLACE_ROW = {p: r for r, p in (PLACE_NEAR | PLACE_FAR).items()} | {14: 0, 13: 0}
WET_AT = 5 * ROWS * LEV
FRAME = WET_AT + 32

OWN_WET = 40 * LEV
OWN = OWN_WET + 8
SLOT = {TEMP: 0, SALT: 8, NORTH: 16, EAST: 24, COUP: 31}
COUNT = {TEMP: 8, SALT: 8, NORTH: 8, EAST: 7, COUP: 6}
BULK_WET = 37 * LEV
HALF = (BULK_WET + 8) // 2
MORE = 144
MORE_WET = 7 * LEV
FAR = 2 * LEV + 8
STRIP = 9
WIDE = 14


class Strips:
    def __init__(self, items):
        self.items = items
        self.packs = -(-len(items) // WIDE)
        self.wet = self.packs * LEV
        self.shape = (self.wet + 32, 128)


EARLY = Strips([(k, PLACE_NEAR[r]) for k in range(4) for r in range(16)] + [(COUP, PLACE_NEAR[r]) for r in range(14)])
LATE = Strips(
    [(k, PLACE_FAR[-r]) for k in (TEMP, SALT, NORTH) for r in range(9)]
    + [(EAST, PLACE_FAR[-r]) for r in range(8)]
    + [(COUP, PLACE_FAR[-r]) for r in range(7)]
)

PARTS = {
    "early": (
        (range(2, 14), (), range(3, 13), (), (6, 16, 19), (17, 19)),
        (range(5, 11), (), range(6, 10), (), (19,), (19,)),
    ),
    "late": (
        ((0, 1, 14), range(0, -8, -1), (0, 1, 2, 13), range(0, -7, -1), (2, 10, 19), (6, 14)),
        ((0, 1, 2, 3, 4, 11), range(0, -5, -1), (0, 1, 2, 3, 4, 5, 10), range(0, -4, -1), (9, 17, 19), (10, 18)),
        (range(0, 9), (-1,), range(0, 8), (), (12, 15), (14,)),
    ),
}
PIVOT_TILES = {"early": (17, 19), "late": (6, 14, 19)}
HANDED = ((range(3, 13), (2, 3, 12, 13)), (range(6, 10), (5, 6, 9, 10)))

VM = pl.BlockSpec(memory_space=pltpu.VMEM)
SM = pl.BlockSpec(memory_space=pltpu.SMEM)
LIMIT = 32 * 1024 * 1024
UNROLL = {"column": 4}
TOGETHER = {"explicit": 0, "lateral": 0}


def call(body, outs, ins, flops, scratch=()):
    return pl.pallas_call(
        body,
        out_shape=tuple(jax.ShapeDtypeStruct(s, jnp.float32) for s in outs),
        in_specs=ins,
        out_specs=tuple(VM for _ in outs),
        scratch_shapes=[pltpu.VMEM(s, jnp.float32) for s in scratch],
        compiler_params=pltpu.CompilerParams(vmem_limit_bytes=LIMIT),
        cost_estimate=pl.CostEstimate(flops=flops, bytes_accessed=4 * 1024 * 1024, transcendentals=0),
    )


def rows_of(shape=(8, 128)):
    return lax.broadcasted_iota(jnp.int32, shape, 0)


def lanes_of(shape=(8, 128)):
    return lax.broadcasted_iota(jnp.int32, shape, 1)


def mirror(tile):
    return jnp.take_along_axis(tile, 127 - lanes_of(), axis=1)


def spread(ref, row):
    return jnp.broadcast_to(ref[row : row + 1, :], (8, 128))


def copy_block(out, to, source, at, change=lambda t: t):
    for g in range(GROUPS):
        out[to + 8 * g : to + 8 * g + 8, :] = change(source[at + 8 * g : at + 8 * g + 8, :])


def copy_blocks(out, to, source, at, count):
    if count:
        out[to : to + count * LEV, :] = source[at : at + count * LEV, :]


def split_halves(full_ref, a_ref, b_ref, rows):
    lanes = lanes_of()

    def one(k, c):
        at = pl.ds(pl.multiple_of(k * 8, 8), 8)
        near = pltpu.roll(full_ref[at, :], 64, axis=1)
        far = full_ref[pl.ds(pl.multiple_of(k * 8 + rows, 8), 8), :]
        a_ref[at, :] = jnp.where(lanes < 64, near, far)
        b_ref[at, :] = jnp.where(lanes < 64, far, near)
        return c

    lax.fori_loop(0, rows // 8, one, 0, unroll=8)


def join_halves(full_ref, a_ref, b_ref, rows):
    lanes = lanes_of()

    def one(k, c):
        at = pl.ds(pl.multiple_of(k * 8, 8), 8)
        a, b = a_ref[at, :], b_ref[at, :]
        full_ref[at, :] = jnp.where(lanes < 64, a, b)
        joined = pltpu.roll(jnp.where(lanes < 64, b, a), 64, axis=1)
        full_ref[pl.ds(pl.multiple_of(k * 8 + rows, 8), 8), :] = joined
        return c

    lax.fori_loop(0, rows // 8, one, 0, unroll=8)


def own_body(flag_ref, state_ref, mixing_ref, wet_ref, x_ref, a_ref, b_ref, full_ref):
    levels = rows_of().astype(jnp.float32)
    odd = flag_ref[0] == 1
    fold = flag_ref[1] == 1
    order = jnp.where(odd, 7 - rows_of(), rows_of())
    x_ref[OWN_WET:OWN, :] = jnp.take_along_axis(wet_ref[...].astype(jnp.float32), order, axis=0)

    def load(turned):
        for r in range(8):
            wet = spread(x_ref, OWN_WET + r)
            source = 7 - r if turned else r
            for g in range(GROUPS):
                deep = wet > levels + float(8 * g)
                for k in range(4):
                    tile = state_ref[pl.ds(k * 8 * LEV + g * 64 + source, 8, stride=8), :]
                    at = (k * 8 + r) * LEV + 8 * g
                    x_ref[at : at + 8, :] = jnp.where(deep, -tile if turned and k == NORTH else tile, 0.0)
                at = (COUP * 8 + r) * LEV + 8 * g
                tile = mixing_ref[pl.ds(g * 64 + source, 8, stride=8), :]
                x_ref[at : at + 8, :] = jnp.where(wet > levels + float(8 * g + 1), tile, 0.0)

    pl.when(odd)(lambda: load(True))
    pl.when(jnp.logical_not(odd))(lambda: load(False))

    @pl.when(jnp.logical_not(fold))
    def _():
        for k in SLOT:
            if k == NORTH:
                for j in range(COUNT[k]):
                    copy_block(full_ref, (SLOT[k] + j) * LEV, x_ref, (k * 8 + j) * LEV, lambda t: -t)
            else:
                copy_blocks(full_ref, SLOT[k] * LEV, x_ref, k * 8 * LEV, COUNT[k])
        full_ref[BULK_WET : BULK_WET + 8, :] = x_ref[OWN_WET:OWN, :]
        a_ref[...] = full_ref[0:HALF, :]
        b_ref[...] = full_ref[HALF : 2 * HALF, :]

    @pl.when(fold)
    def _():
        for k in SLOT:
            sign = (lambda t: -mirror(t)) if k in (EAST, NORTH) else mirror
            for j in range(COUNT[k]):
                copy_block(full_ref, (SLOT[k] + j) * LEV, x_ref, (k * 8 + j) * LEV, sign)
        full_ref[BULK_WET : BULK_WET + 8, :] = mirror(x_ref[OWN_WET:OWN, :])
        split_halves(full_ref, a_ref, b_ref, HALF)


def block_at(k, place):
    return (k * ROWS + place) * LEV


def wet_row(ref, place, source, row):
    ref[WET_AT + place : WET_AT + place + 1, :] = source[row : row + 1, :]


def pack_strips(strips, frame_ref, east_ref, west_ref):
    lanes = lanes_of()
    zero = jnp.zeros((8, 128), jnp.float32)

    def add_strip(out, tile, n, shift):
        here = (lanes >= STRIP * n) & (lanes < STRIP * (n + 1))
        return jnp.where(here, pltpu.roll(tile, (STRIP * n + shift) % 128, axis=1), out)

    def pack(g, c):
        first = pl.multiple_of(g * 8, 8)
        for p in range(strips.packs):
            to_east = to_west = zero
            for n, (k, place) in enumerate(strips.items[p * WIDE : (p + 1) * WIDE]):
                tile = frame_ref[pl.ds(first + block_at(k, place), 8), :]
                to_east = add_strip(to_east, tile, n, STRIP)
                to_west = add_strip(to_west, tile, n, 0)
            east_ref[pl.ds(first + p * LEV, 8), :] = to_east
            west_ref[pl.ds(first + p * LEV, 8), :] = to_west
        return c

    lax.fori_loop(0, GROUPS, pack, 0)
    for t in range(0, 32, 8):
        tile = frame_ref[WET_AT + t : WET_AT + t + 8, :]
        east_ref[strips.wet + t : strips.wet + t + 8, :] = add_strip(zero, tile, 0, STRIP)
        west_ref[strips.wet + t : strips.wet + t + 8, :] = add_strip(zero, tile, 0, 0)


def early_frame_body(
    flag_ref, x_ref, y_ref, a_in, b_in, b_ref, fold_a_ref, fold_b_ref, frame_ref, east_ref, west_ref, full_ref
):
    fold = flag_ref[1] == 1

    @pl.when(jnp.logical_not(fold))
    def _():
        for k in (TEMP, SALT):
            copy_blocks(b_ref, HALF + k * LEV, y_ref, (k * 8 + 7) * LEV, 1)
        b_ref[HALF + 2 * LEV : HALF + FAR, :] = spread(y_ref, OWN_WET + 7)
        b_ref[0:HALF, :] = b_in[...]

    @pl.when(fold)
    def _():
        for n, (source, k, row, change) in enumerate(
            (
                (y_ref, TEMP, 7, mirror),
                (y_ref, SALT, 7, mirror),
                (y_ref, NORTH, 7, mirror),
                (y_ref, TEMP, 6, mirror),
                (y_ref, SALT, 6, mirror),
                (x_ref, EAST, 7, lambda t: -mirror(t)),
                (x_ref, COUP, 6, mirror),
            )
        ):
            copy_block(full_ref, n * LEV, source, (k * 8 + row) * LEV, change)
        wet = jnp.where(rows_of() == 0, spread(y_ref, OWN_WET + 7), spread(y_ref, OWN_WET + 6))
        full_ref[MORE_WET : MORE_WET + 8, :] = mirror(wet)
        split_halves(full_ref, fold_a_ref.at[HALF : HALF + MORE], fold_b_ref.at[HALF : HALF + MORE], MORE)
        fold_a_ref[0:HALF, :] = a_in[...]
        fold_b_ref[0:HALF, :] = b_in[...]

    for k in range(5):
        copy_blocks(frame_ref, block_at(k, PLACE_NEAR[0]), x_ref, k * 8 * LEV, 8)
        for r in range(8, 16):
            change = (lambda t: -t) if k == NORTH else (lambda t: t)
            copy_block(frame_ref, block_at(k, PLACE_NEAR[r]), y_ref, (k * 8 + 15 - r) * LEV, change)
    for r in range(8):
        wet_row(frame_ref, PLACE_NEAR[r], x_ref, OWN_WET + r)
        wet_row(frame_ref, PLACE_NEAR[r + 8], y_ref, OWN_WET + 7 - r)
    pack_strips(EARLY, frame_ref, east_ref, west_ref)


def frame_body(
    flag_ref, early_ref, a_ref, b_ref, fold_a_ref, fold_b_ref, main_early, side_early, frame_ref, far_ref, east_ref, west_ref, full_ref, more_ref
):
    fold = flag_ref[1] == 1

    def bulk(k, row, slot, count):
        for j in range(count):
            copy_blocks(frame_ref, block_at(k, PLACE_FAR[row - j]), full_ref, (SLOT[k] + slot + j) * LEV, 1)

    def send_far(slot):
        for k in (TEMP, SALT):
            copy_blocks(far_ref, k * LEV, full_ref, (SLOT[k] + slot) * LEV, 1)
        far_ref[2 * LEV : FAR, :] = spread(full_ref, BULK_WET + slot)

    frame_ref[...] = early_ref[...]

    @pl.when(jnp.logical_not(fold))
    def _():
        full_ref[0:HALF, :] = a_ref[...]
        full_ref[HALF : 2 * HALF, :] = b_ref[0:HALF, :]
        for k in range(5):
            copy_blocks(frame_ref, block_at(k, PLACE_FAR[0]), early_ref, block_at(k, PLACE_NEAR[0]), 1)
            bulk(k, -1, 0, COUNT[k])
        wet_row(frame_ref, PLACE_FAR[0], early_ref, WET_AT + PLACE_NEAR[0])
        for r in range(8):
            wet_row(frame_ref, PLACE_FAR[-1 - r], full_ref, BULK_WET + r)
        for k in (TEMP, SALT):
            copy_blocks(frame_ref, block_at(k, PLACE_FAR[-9]), b_ref, HALF + k * LEV, 1)
        wet_row(frame_ref, PLACE_FAR[-9], b_ref, HALF + 2 * LEV)
        send_far(0)

    @pl.when(fold)
    def _():
        join_halves(full_ref, fold_a_ref.at[0:HALF], fold_b_ref.at[0:HALF], HALF)
        join_halves(more_ref, fold_a_ref.at[HALF : HALF + MORE], fold_b_ref.at[HALF : HALF + MORE], MORE)
        for k in range(5):
            bulk(k, 0, 0, COUNT[k])
        for r in range(8):
            wet_row(frame_ref, PLACE_FAR[-r], full_ref, BULK_WET + r)
        for n, (k, row) in enumerate(
            ((TEMP, -8), (SALT, -8), (NORTH, -8), (TEMP, -9), (SALT, -9), (EAST, -7), (COUP, -6))
        ):
            copy_blocks(frame_ref, block_at(k, PLACE_FAR[row]), more_ref, n * LEV, 1)
        wet_row(frame_ref, PLACE_FAR[-8], more_ref, MORE_WET)
        wet_row(frame_ref, PLACE_FAR[-9], more_ref, MORE_WET + 1)
        send_far(1)

    pack_strips(LATE, frame_ref, east_ref, west_ref)


def east_of(a):
    return pltpu.roll(a, 127, axis=1)


def west_of(a):
    return pltpu.roll(a, 1, axis=1)


def minmod(a, b):
    return jnp.maximum(jnp.minimum(a, b), 0.0) + jnp.minimum(jnp.maximum(a, b), 0.0)


def place_of(row, far):
    if far:
        return PLACE_FAR[row] if row <= 0 else PLACE_NEAR[row]
    return PLACE_NEAR[row] if row >= 0 else PLACE_FAR[row]


WINDOW = 5


def in_turn(jobs):
    waiting, active = list(jobs), []
    while waiting or active:
        if waiting and len(active) < WINDOW:
            active.append(waiting.pop(0))
        for job in list(active):
            if next(job, "end") == "end":
                active.remove(job)


ADV = LEV + 16


def march(
    part, frame_ref, wet_ref, rate_ref, after, emit, f_ref, rhs_ref, adv_ref, adv_e_ref, p_ref, coef_ref, wet_e_ref, far_ref=None
):
    levels = rows_of().astype(jnp.float32)
    zero = jnp.zeros((8, 128), jnp.float32)
    spans = PARTS[part]
    last = len(spans) - 1
    wet_e_ref[...] = jnp.minimum(wet_ref[...], pltpu.roll(wet_ref[...], 127, axis=1))
    for k in range(2):
        for place in range(ROWS):
            at = (k * ROWS + place) * ADV
            for ref in (adv_ref, adv_e_ref):
                ref[at : at + 8, :] = zero
                ref[at + 8 + LEV : at + ADV, :] = zero

    def eight(ref, k, place, level):
        return ref[pl.ds((k * ROWS + place) * LEV + level, 8, stride=LEV), :]

    def put_eight(ref, k, place, level, value):
        ref[pl.ds((k * ROWS + place) * LEV + level, 8, stride=LEV), :] = value

    def pivots(l, carry):
        done = []
        for tile, (above, up_above) in zip(PIVOT_TILES[part], carry):
            c = eight(frame_ref, COUP, tile, l)
            inv = 1.0 / (1.0 + c + above * (1.0 - up_above))
            up = c * inv
            put_eight(coef_ref, 0, tile, l, inv)
            put_eight(coef_ref, 1, tile, l, above * inv)
            put_eight(coef_ref, 2, tile, l, up)
            done.append((c, up))
        return tuple(done)

    lax.fori_loop(0, LEV, pivots, ((zero, zero),) * len(PIVOT_TILES[part]), unroll=4)

    def explicit(step, g):
        near_a, far_a, near_f, far_f = spans[step][:4]
        first = g * 8 if isinstance(g, int) else pl.multiple_of(g * 8, 8)
        depth = levels + (float(8 * g) if isinstance(g, int) else (g * 8).astype(jnp.float32))
        cache = {}

        def once(key, make):
            if key not in cache:
                cache[key] = make()
            return cache[key]

        def field(k, place):
            if step == 0 and far_ref is not None and place == PLACE_NEAR[16] and k in (TEMP, SALT):
                return once((k, place), lambda: far_ref[pl.ds(first + k * LEV, 8), :])
            ref = frame_ref if step == 0 else f_ref
            return once((k, place), lambda: ref[pl.ds(first + block_at(k, place), 8), :])

        def pressure(place):
            return once(("p", place), lambda: p_ref[pl.ds(first + place * LEV, 8), :])

        def deep(place):
            return once(("m", place), lambda: spread(wet_ref, place) > depth)

        def face_e(place):
            return once(("e", place), lambda: spread(wet_e_ref, place) > depth)

        def to_east(k, place):
            return once(("r", k, place), lambda: east_of(field(k, place)))

        def piece(far, span_a, span_f):

            def here(row):
                return place_of(row, far)

            def face_n(row):
                return once(("n", far, row), lambda: deep(here(row)) & deep(here(row + 1)))

            def diff_n(k, row):
                def make():
                    return jnp.where(face_n(row), field(k, here(row + 1)) - field(k, here(row)), 0.0)

                return once(("d", far, k, row), make)

            def half_n(k, row):
                return once(("h", far, k, row), lambda: 0.5 * minmod(diff_n(k, row - 1), diff_n(k, row)))

            def speed_n(row):
                def make():
                    u = jnp.where(face_n(row), field(NORTH, here(row)) + field(NORTH, here(row + 1)), 0.0)
                    return u, u > 0.0

                return once(("s", far, row), make)

            def flux_n(k, row):
                def make():
                    speed, upward = speed_n(row)
                    below = field(k, here(row)) + half_n(k, row)
                    above = field(k, here(row + 1)) - half_n(k, row + 1)
                    return speed * jnp.where(upward, below, above)

                return once(("f", far, k, row), make)

            def work(row):
                place = here(row)
                mask_e = face_e(place)
                tracers = (TEMP, SALT)
                new_fields = row in span_f
                for k in (TEMP, SALT, EAST):
                    to_east(k, place)
                if new_fields:
                    to_east(NORTH, place)
                    p_e = east_of(pressure(place))
                yield
                diffs = [jnp.where(mask_e, to_east(k, place) - field(k, place), 0.0) for k in range(4 if new_fields else 2)]
                terms = list(diffs)
                if new_fields:
                    terms[EAST] = VISCOSITY * diffs[EAST] - (0.5 * PRESSURE) * pressure(place)
                diffs_w = [west_of(d) for d in terms]
                yield
                halves = [0.5 * minmod(diffs_w[k], diffs[k]) for k in tracers]
                beyond = [east_of(field(k, place) - halves[k]) for k in tracers]
                yield
                speed_e = jnp.where(mask_e, field(EAST, place) + to_east(EAST, place), 0.0)
                fluxes = [
                    speed_e * jnp.where(speed_e > 0.0, field(k, place) + halves[k], beyond[k]) for k in tracers
                ]
                fluxes_w = [west_of(f) for f in fluxes]
                yield
                for k in tracers if row in span_a else ():
                    div = (fluxes[k] - fluxes_w[k]) + (flux_n(k, row) - flux_n(k, row - 1))
                    out = jnp.where(deep(place), field(k, place) - (0.5 * ADVECT) * div, 0.0)
                    adv_ref[pl.ds(first + (k * ROWS + place) * ADV + 8, 8), :] = out
                    if new_fields:
                        adv_e_ref[pl.ds(first + (k * ROWS + place) * ADV + 8, 8), :] = east_of(out)
                if new_fields:
                    u, v = field(EAST, place), field(NORTH, place)
                    rate = spread(rate_ref, place)
                    push_n = pressure(here(row + 1)) - pressure(here(row - 1))
                    lap_n = [diff_n(k, row) - diff_n(k, row - 1) for k in (EAST, NORTH)]
                    u1 = u + rate * v - (0.5 * PRESSURE) * p_e + VISCOSITY * (diffs[EAST] + lap_n[0]) - diffs_w[EAST]
                    lap = (diffs[NORTH] - diffs_w[NORTH]) + lap_n[1]
                    v1 = v - rate * u - (0.5 * PRESSURE) * push_n + VISCOSITY * lap
                    for k, out in ((EAST, u1), (NORTH, v1)):
                        rhs_ref[pl.ds(first + (k * ROWS + place) * LEV, 8), :] = jnp.where(deep(place), out, 0.0)

            return [work(row) for row in sorted({*span_a, *span_f})]

        return piece(False, near_a, near_f) + piece(True, far_a, far_f)

    def lateral(step, g):
        near_f, far_f = spans[step][2:4]
        first = g * 8 if isinstance(g, int) else pl.multiple_of(g * 8, 8)
        depth = levels + (float(8 * g) if isinstance(g, int) else (g * 8).astype(jnp.float32))
        cache = {}

        def once(key, make):
            if key not in cache:
                cache[key] = make()
            return cache[key]

        def tracer(k, place, shift=0):
            at = first + (k * ROWS + place) * ADV + 8 + shift
            return once((k, place, shift), lambda: adv_ref[pl.ds(at, 8), :])

        def grad(k, place):
            return once(("g", k, place), lambda: tracer(k, place, 1) - tracer(k, place, -1))

        def deep(place):
            return once(("m", place), lambda: spread(wet_ref, place) > depth)

        def fluxes(mask, dt, ds, gt, gs):
            gr = EXPAND_SALT * gs - EXPAND_HEAT * gt
            dr = EXPAND_SALT * ds - EXPAND_HEAT * dt
            slope = dr * gr / (gr * gr + 16.0)
            return jnp.where(mask, dt - slope * gt, 0.0), jnp.where(mask, ds - slope * gs, 0.0)

        def piece(far, span_f):
            def here(row):
                return place_of(row, far)

            def flux_n(row):
                def make():
                    a, b = here(row), here(row + 1)
                    return fluxes(
                        deep(a) & deep(b),
                        tracer(TEMP, b) - tracer(TEMP, a),
                        tracer(SALT, b) - tracer(SALT, a),
                        grad(TEMP, a) + grad(TEMP, b),
                        grad(SALT, a) + grad(SALT, b),
                    )

                return once(("f", far, row), make)

            def work(row):
                place = here(row)
                cells = [(tracer(k, place), grad(k, place)) for k in (TEMP, SALT)]
                beyond = []
                for k in (TEMP, SALT):
                    at = first + (k * ROWS + place) * ADV + 8
                    q, below, above = (adv_e_ref[pl.ds(at + shift, 8), :] for shift in (0, 1, -1))
                    beyond.append((q, below - above))
                yield
                flux_n(row)
                yield
                (t, gt), (s, gs) = cells
                (t_e, gt_e), (s_e, gs_e) = beyond
                east = fluxes(spread(wet_e_ref, place) > depth, t_e - t, s_e - s, gt + gt_e, gs + gs_e)
                west = [west_of(f) for f in east]
                yield
                for k in (TEMP, SALT):
                    div = (east[k] - west[k]) + (flux_n(row)[k] - flux_n(row - 1)[k])
                    out = jnp.where(deep(place), cells[k][0] + DIFFUSE * div, 0.0)
                    rhs_ref[pl.ds(first + (k * ROWS + place) * LEV, 8), :] = out

            return [work(row) for row in sorted(span_f)]

        return piece(False, near_f) + piece(True, far_f)

    for step in range(len(spans)):
        source = frame_ref if step == 0 else f_ref
        weights, tiles = spans[step][4:]

        def weigh(l, carry):
            done = []
            for tile, p in zip(weights, carry):
                p = p + (EXPAND_SALT * eight(source, SALT, tile, l) - EXPAND_HEAT * eight(source, TEMP, tile, l))
                put_eight(p_ref, 0, tile, l, p)
                done.append(p)
            return tuple(done)

        lax.fori_loop(0, LEV, weigh, (zero,) * len(weights), unroll=UNROLL["column"])

        def by_groups(make, together):
            def one(g, c):
                in_turn(make(step, g))
                return c

            if not together:
                lax.fori_loop(0, GROUPS, one, 0)
                return
            for n in range(0, GROUPS, together):
                in_turn([job for g in range(n, min(n + together, GROUPS)) for job in make(step, g)])

        by_groups(explicit, TOGETHER["explicit"])
        after(step, "adv")
        by_groups(lateral, TOGETHER["lateral"])

        def down(l, carry):
            loads = [(eight(coef_ref, 0, t, l), eight(coef_ref, 1, t, l), [eight(rhs_ref, k, t, l) for k in range(4)]) for t in tiles]
            done = []
            for (inv, low, rhs), above in zip(loads, carry):
                done.append(tuple(rhs[k] * inv + low * above[k] for k in range(4)))
            for tile, solved in zip(tiles, done):
                for k in range(4):
                    put_eight(rhs_ref, k, tile, l, solved[k])
            return tuple(done)

        def up(i, carry):
            l = LEV - 1 - i
            done = []
            for tile, below in zip(tiles, carry):
                factor = eight(coef_ref, 2, tile, l)
                solved = []
                for k in range(4):
                    x = eight(rhs_ref, k, tile, l) + factor * below[k]
                    if emit is None or step < last:
                        put_eight(f_ref, k, tile, l, x)
                    else:
                        emit(k, l, x)
                    solved.append(x)
                done.append(tuple(solved))
            return tuple(done)

        start = ((zero,) * 4,) * len(tiles)
        lax.fori_loop(0, LEV, down, start, unroll=UNROLL["column"])
        lax.fori_loop(0, LEV, up, start, unroll=UNROLL["column"])
        after(step, "new")


WORK = [
    (4 * ROWS * LEV, 128),
    (4 * ROWS * LEV, 128),
    (2 * ROWS * ADV, 128),
    (2 * ROWS * ADV, 128),
    (ROWS * LEV, 128),
    (3 * ROWS * LEV, 128),
    (32, 128),
]
HANDED_SHAPES = [
    shape for rows, adv_rows in HANDED for shape in ((2 * len(adv_rows) * ADV, 128), (4 * len(rows) * LEV, 128))
]


def early(frame_ref, wet_ref, rate_ref, outs, work):
    f_ref, _, adv_ref = work[:3]

    def after(step, what):
        rows, adv_rows = HANDED[step]
        adv_out, new_out = outs[2 * step : 2 * step + 2]
        if what == "adv":
            for k in range(2):
                for n, r in enumerate(adv_rows):
                    at, to = (k * ROWS + PLACE_NEAR[r]) * ADV, (k * len(adv_rows) + n) * ADV
                    adv_out[to : to + ADV, :] = adv_ref[at : at + ADV, :]
        else:
            for k in range(4):
                copy_blocks(new_out, k * len(rows) * LEV, f_ref, block_at(k, PLACE_NEAR[rows[0]]), len(rows))

    march("early", frame_ref, wet_ref, rate_ref, after, None, *work)


def late(frame_ref, wet_ref, rate_ref, emit, ins, work, far_ref=None):
    f_ref, _, adv_ref, adv_e_ref = work[:4]

    def after(step, what):
        if step >= len(HANDED):
            return
        rows, adv_rows = HANDED[step]
        adv_in, new_in = ins[2 * step : 2 * step + 2]
        if what == "adv":
            for k in range(2):
                for n, r in enumerate(adv_rows):
                    at, source = (k * ROWS + PLACE_NEAR[r]) * ADV, (k * len(adv_rows) + n) * ADV
                    adv_ref[at : at + ADV, :] = adv_in[source : source + ADV, :]
                    if r in PARTS["late"][step][2]:
                        for g in range(GROUPS):
                            to, part = at + 8 + 8 * g, source + 8 + 8 * g
                            adv_e_ref[to : to + 8, :] = east_of(adv_in[part : part + 8, :])
        else:
            for k in range(4):
                copy_blocks(f_ref, block_at(k, PLACE_NEAR[rows[0]]), new_in, k * len(rows) * LEV, len(rows))

    march("late", frame_ref, wet_ref, rate_ref, after, emit, *work, far_ref=far_ref)


def early_main_body(flag_ref, frame_ref, rate_ref, *rest):
    outs, (wet_ref, *work) = rest[:4], rest[4:]
    wet_ref[...] = frame_ref[WET_AT : WET_AT + 32, :]
    early(frame_ref, wet_ref, rate_ref, outs, work)


def edges(tile):
    return jnp.where(lanes_of() < 64, pltpu.roll(tile, 32, axis=1), pltpu.roll(tile, 96, axis=1))


def with_strips(tile, west, east, n):
    lanes = lanes_of()
    out = edges(tile)
    west = pltpu.roll(west, (32 - STRIP - STRIP * n) % 128, axis=1)
    east = pltpu.roll(east, (96 - STRIP * n) % 128, axis=1)
    out = jnp.where((lanes >= 32 - STRIP) & (lanes < 32), west, out)
    return jnp.where((lanes >= 96) & (lanes < 96 + STRIP), east, out)


def unpack_strips(strips, frame_ref, east_ref, west_ref, side_ref):
    def unpack(g, c):
        first = pl.multiple_of(g * 8, 8)
        for n, (k, place) in enumerate(strips.items):
            at = pl.ds(first + block_at(k, place), 8)
            p = pl.ds(first + n // WIDE * LEV, 8)
            side_ref[at, :] = with_strips(frame_ref[at, :], east_ref[p, :], west_ref[p, :], n % WIDE)
        return c

    lax.fori_loop(0, GROUPS, unpack, 0)


def unpack_wet(strips, tile_ref, east_ref, west_ref, out_ref, base, places):
    rows = rows_of()
    for t in range(0, 32, 8):
        at = strips.wet + t
        here = [p - t for p in places if t <= p < t + 8]
        if here:
            tile = with_strips(tile_ref[WET_AT + t : WET_AT + t + 8, :], east_ref[at : at + 8, :], west_ref[at : at + 8, :], 0)
            mask = rows == here[0]
            for p in here[1:]:
                mask = mask | (rows == p)
            out_ref[base + t : base + t + 8, :] = jnp.where(mask, tile, out_ref[base + t : base + t + 8, :])


def early_side_body(flag_ref, frame_ref, rate_ref, east_ref, west_ref, side_ref, *rest):
    outs, work = rest[:4], rest[4:]
    wet_ref, *work = work
    side_ref[...] = jnp.zeros((FRAME, 128), jnp.float32)
    unpack_strips(EARLY, frame_ref, east_ref, west_ref, side_ref)
    unpack_wet(EARLY, frame_ref, east_ref, west_ref, side_ref, WET_AT, [PLACE_NEAR[r] for r in range(16)])
    wet_ref[...] = side_ref[WET_AT : WET_AT + 32, :]
    early(side_ref, wet_ref, rate_ref, outs, work)


def late_main_body(flag_ref, frame_ref, far_ref, rate_ref, *rest):
    ins, (out_ref, wet_ref, *work) = rest[:4], rest[4:]
    wet_ref[...] = frame_ref[WET_AT : WET_AT + 32, :]
    wet_ref[PLACE_NEAR[16] : PLACE_NEAR[16] + 1, :] = far_ref[2 * LEV : 2 * LEV + 1, :]

    def emit(k, l, x):
        out_ref[k, l] = x

    late(frame_ref, wet_ref, rate_ref, emit, ins, work, far_ref)


def late_side_body(flag_ref, frame_in, far_ref, rate_ref, side_in, east_ref, west_ref, main_ref, *rest):
    ins, (out_ref, frame_ref, wet_ref, *work) = rest[:4], rest[4:]
    frame_ref[...] = side_in[...]
    unpack_strips(LATE, frame_in, east_ref, west_ref, frame_ref)
    unpack_wet(LATE, frame_in, east_ref, west_ref, frame_ref, WET_AT, [PLACE_FAR[-r] for r in range(9)])
    for k in (TEMP, SALT):
        copy_block(frame_ref, block_at(k, PLACE_NEAR[16]), far_ref, k * LEV, edges)
        copy_block(frame_ref, block_at(k, PLACE_FAR[-9]), frame_in, block_at(k, PLACE_FAR[-9]), edges)
    wet_ref[...] = frame_ref[WET_AT : WET_AT + 32, :]
    for place, row in (
        (PLACE_NEAR[16], spread(far_ref, 2 * LEV)),
        (PLACE_FAR[-9], spread(frame_in, WET_AT + PLACE_FAR[-9])),
    ):
        wet_ref[place : place + 1, :] = edges(row)[0:1, :]
    lanes = lanes_of()
    odd = flag_ref[0] == 1
    order = jnp.where(odd, 7 - rows_of(), rows_of())
    sign = jnp.where(odd, -1.0, 1.0)

    def emit(k, l, x):
        out = jnp.where(lanes < STRIP, pltpu.roll(x, 96, axis=1), main_ref[k, l])
        out = jnp.where(lanes >= 128 - STRIP, pltpu.roll(x, 32, axis=1), out)
        out = jnp.take_along_axis(out, order, axis=0)
        out_ref[k, l] = out * sign if k == NORTH else out

    late(frame_ref, wet_ref, rate_ref, emit, ins, work)


def local(state, mixing, wet_levels):
    lons, lats = lax.axis_size("lon"), lax.axis_size("lat")
    lat = lax.axis_index("lat")
    odd = lax.rem(lat, 2)
    flags = jnp.stack([odd, (lat == lats - 1).astype(jnp.int32)]).astype(jnp.int32)
    rows = jnp.array([PLACE_ROW.get(p, 0) for p in range(32)], jnp.int32)
    grid_rows = lat * 8 + jnp.where(odd == 1, 7 - rows, rows)
    grid_rows = jnp.where(grid_rows > lats * 8 - 1, 2 * (lats * 8 - 1) - grid_rows, grid_rows).astype(jnp.float32)
    rate = CORIOLIS * jnp.sin(math.pi * (grid_rows + 0.5) / (lats * 8) - 0.9)
    rate = jnp.broadcast_to(jnp.where(odd == 1, -rate, rate)[:, None], (32, 128))

    def at(o, a):
        return o * lats + a

    pairs = [(at(o, a), at(o, a ^ 1)) for o in range(lons) for a in range(lats)]
    cross = [(at(o, a), at(o, a + 1 if a % 2 else a - 1)) for o in range(lons) for a in range(1, lats - 1)]
    fold_a = [(at(o, lats - 1), at((lons - o) % lons, lats - 1)) for o in range(lons)]
    fold_b = [(at(o, lats - 1), at(lons - 1 - o, lats - 1)) for o in range(lons)]
    both = ("lon", "lat")

    half = (HALF, 128)
    x, a, b = call(
        own_body,
        [(OWN, 128), half, half],
        [SM] + [VM] * 3,
        10**6,
        [(2 * HALF, 128)],
    )(
        flags, state.reshape(4 * LEV * 8, 128), mixing.reshape(LEV * 8, 128), wet_levels
    )
    far_a = lax.ppermute(a, both, cross)
    y = lax.ppermute(x, both, pairs)
    to_east_pairs = [(i, (i + 1) % lons) for i in range(lons)]
    to_west_pairs = [((i + 1) % lons, i) for i in range(lons)]
    b, beyond_a, beyond_b, early_frame, to_east, to_west = call(
        early_frame_body,
        [(HALF + FAR, 128), (HALF + MORE, 128), (HALF + MORE, 128), (FRAME, 128), EARLY.shape, EARLY.shape],
        [SM] + [VM] * 4,
        10**6,
        [(2 * MORE, 128)],
    )(flags, x, y, a, b)
    from_west = lax.ppermute(to_east, "lon", to_east_pairs)
    from_east = lax.ppermute(to_west, "lon", to_west_pairs)
    far_b = lax.ppermute(b, both, cross)
    beyond_a = lax.ppermute(beyond_a, both, fold_a)
    beyond_b = lax.ppermute(beyond_b, both, fold_b)
    wet = (32, 128)
    main_early = call(early_main_body, HANDED_SHAPES, [SM, VM, VM], 10**9, [wet] + WORK)(flags, early_frame, rate)
    side_frame, *side_early = call(
        early_side_body, [(FRAME, 128)] + HANDED_SHAPES, [SM] + [VM] * 4, 10**11, [wet] + WORK
    )(flags, early_frame, rate, from_west, from_east)
    frame, far, to_east, to_west = call(
        frame_body,
        [(FRAME, 128), (FAR, 128), LATE.shape, LATE.shape],
        [SM] + [VM] * 5 + [pl.BlockSpec(memory_space=pl.ANY)] * 2,
        10**6,
        [(2 * HALF, 128), (2 * MORE, 128)],
    )(flags, early_frame, far_a, far_b, beyond_a, beyond_b, main_early[0], side_early[0])
    far = lax.ppermute(far, both, pairs)
    from_west = lax.ppermute(to_east, "lon", to_east_pairs)
    from_east = lax.ppermute(to_west, "lon", to_west_pairs)
    work = [(FRAME, 128), wet] + WORK
    (middle,) = call(late_main_body, [state.shape], [SM] + [VM] * 7, 10**9, [wet] + WORK)(flags, frame, far, rate, *main_early)
    (out,) = call(late_side_body, [state.shape], [SM] + [VM] * 11, 10**9, work)(
        flags, frame, far, rate, side_frame, from_west, from_east, middle, *side_early
    )
    return out


def solution(mesh):
    return jax.shard_map(
        local,
        mesh=mesh,
        in_specs=(P(None, None, "lat", "lon"), P(None, "lat", "lon"), P("lat", "lon")),
        out_specs=P(None, None, "lat", "lon"),
        check_vma=False,
    )
```
